32 devices in a mesh: groups: 2 (over x), surf: 16 (over z, y, core).
Axes of the slice: x: 2, y: 2, z: 4, core: 2. Of those that a mesh axis runs over, the one named last changes fastest.
Arguments:
- currents: bfloat16 [32, 65536], P(None, ('groups', 'surf')), parts along dimension 1, may hold values from -6 to 6
- near_tiles: bfloat16 [1536, 256, 256], P(('groups', 'surf')), parts along dimension 0, may hold values from -0.15625 to 0.15625
- near_target: int32 [1536], P(('groups', 'surf')), parts along dimension 0, may hold values from 0 to 7
- near_source: int32 [1536], P(('groups', 'surf')), parts along dimension 0, may hold values from 0 to 127, as said below
- primal_compress: bfloat16 [256, 32, 256], P(('groups', 'surf')), parts along dimension 0, may hold values from -0.375 to 0.375
- primal_expand: bfloat16 [256, 32, 256], P(('groups', 'surf')), parts along dimension 0, may hold values from -1 to 1
- primal_coupling: bfloat16 [4096, 1024], P(('groups', 'surf')), parts along dimension 0, may hold values from -0.25 to 0.25
- far_source: int32 [4096], P(('groups', 'surf')), parts along dimension 0, may hold values from 0 to 7
- far_owner: int32 [4096, 1], P(('groups', 'surf')), parts along dimension 0, may hold values from 0 to 15; in each aligned block of 128 rows (0 to 127, 128 to 255, ...) at most 16 rows name the same one
- far_block: int32 [4096], P(('groups', 'surf')), parts along dimension 0, may hold values from 0 to 7
- gram_inverse: bfloat16 [256, 256, 256], P(('groups', 'surf')), parts along dimension 0, may hold values from -0.5 to 1.5
- gram_lower: bfloat16 [256, 256, 256], P(('groups', 'surf')), parts along dimension 0, may hold values from -0.15625 to 0.15625
- gram_upper: bfloat16 [256, 256, 256], P(('groups', 'surf')), parts along dimension 0, may hold values from -0.15625 to 0.15625
- refine_weight: float32 [65536], P(('groups', 'surf')), parts along dimension 0, may hold values from 0.5 to 2
- dual_owner: int32 [65536, 1], P(('groups', 'surf')), parts along dimension 0, may hold values from 0 to 15; in each aligned block of 2048 rows (0 to 2047, 2048 to 4095, ...) at most 256 rows name the same one
- dual_index: int32 [65536], P(('groups', 'surf')), parts along dimension 0, may hold values from 0 to 2047
- dual_self: bfloat16 [256, 256, 256], P(('groups', 'surf')), parts along dimension 0, may hold values from -0.375 to 0.375
- dual_compress: bfloat16 [256, 32, 256], P(('groups', 'surf')), parts along dimension 0, may hold values from -0.375 to 0.375
- dual_expand: bfloat16 [256, 32, 256], P(('groups', 'surf')), parts along dimension 0, may hold values from -1 to 1
- dual_coupling: bfloat16 [4096, 1024], P(('groups', 'surf')), parts along dimension 0, may hold values from -0.25 to 0.25
Outputs:
- response: bfloat16 [32, 65536], P(None, ('groups', 'surf')), parts along dimension 1
The draws below stay inside these ranges and needn't reach their ends.
There are 2 independent parts, one for each index of `groups`. The reference program is written for one: setup_inputs(seed, part) draws one part's arguments, and reference() takes and returns one part's arrays. A program takes and returns all parts, laid end to end along the dimension named above; each array names one. Nothing has to cross between parts.
Inputs may be any that keep to these rules, and one draw needn't show every extreme that they name: `near_source`: tiles of device d (rows d * 48 to (d + 1) * 48 - 1) take sources among blocks d * 8 - 1 to (d + 1) * 8 + 1 - 1 that exist. `far_owner`: of the far tiles of one device, at most 16 name the same owner. `dual_owner`: of the unknowns of one device, at most 256 name the same dual owner.
All inputs are finite; a program needn't handle non-finite values.
Results may differ from the reference program's by a relative error of at most 0.015.
Values may be sent and summed in bfloat16 or wider, within the bound.
No kernel may reach another device: no remote copies, remote signals or barrier semaphores. Data moves between devices by JAX's collectives and lax.ppermute only.
A program may use at most 64 MiB of HBM per device.

```python
import math
import jax
import jax.numpy as jnp
import numpy as np
from jax import lax

TILE = 256
INC = 32
RANK = 32
HALO = 1
SWEEPS = 4
NEAR_PER = 6
FAR_PER = 16
BLK_DEV = 8
NP_DEV = 2048
NBLK = 128
NP = 32768
NEAR_DEV = 48
NEAR = 768
FAR_DEV = 128
FAR = 2048
FCAP = 16
CAP = 256
N_SURF = 16


def draw_near_source(key, part):
    key = jax.random.fold_in(key, 11)
    relative = jax.random.randint(key, (NEAR,), 0, BLK_DEV + 2 * HALO)
    relative = relative.at[0].set(0).at[NEAR - 1].set(BLK_DEV + 2 * HALO - 1)
    device = jnp.arange(NEAR, dtype=jnp.int32) // NEAR_DEV
    return jnp.clip(device * BLK_DEV - HALO + relative, 0, NBLK - 1).astype(jnp.int32)


def draw_gram_inverse(key, part):
    key = jax.random.fold_in(key, 23)
    noise_part = jax.random.normal(key, (NBLK, TILE, TILE), jnp.float32) * (0.3 / math.sqrt(TILE))
    noise_part = jnp.clip(noise_part, -0.5, 0.5)
    return (jnp.eye(TILE, dtype=jnp.float32)[None, :, :] + noise_part).astype(jnp.bfloat16)


def set_ends(values, stream_key, low, high):
    dims = values.shape
    index_at = [jax.random.randint(jax.random.fold_in(stream_key, axis), (), 0, dims[axis]) for axis in range(len(dims))]
    values = values.at[tuple(index_at)].set(low)
    longest = dims.index(max(dims))
    index_at[longest] = (index_at[longest] + 1) % dims[longest]
    return values.at[tuple(index_at)].set(high)


def levels(stream_key, shape, split, least, high):
    def one(dim, shards_of):
        steps = jax.random.uniform(jax.random.fold_in(jax.random.fold_in(stream_key, 6), dim), (shards_of,), jnp.float32, least / len(split), high / len(split))
        return jnp.repeat(jnp.exp(steps), shape[dim] // shards_of).reshape((-1,) + (1,) * (len(shape) - dim - 1))

    gain = one(*split[0])
    for cut in split[1:]:
        gain = gain * one(*cut)
    return gain


def assign_block(stream_key, own, number, rows, number_of, top, limit, skew):
    order = jax.random.permutation(stream_key, number_of)
    crowded, common = load_shares(number_of, rows * top, limit, skew, True), load_shares(number_of, rows * top, limit, skew, False)
    places = jnp.arange(number_of)

    def named(sizes, rotation):
        used = int((sizes > 0).sum())
        fixed = max(1, used // 4)
        moved = fixed + (places - fixed + rotation * (used - fixed)) % max(1, number_of - fixed)
        return jnp.zeros((number_of,), jnp.int32).at[order[jnp.where(places < fixed, places, moved)]].set(jnp.asarray(sizes, jnp.int32))

    sizes = jnp.where(number % 4 == 0, named(crowded, number // 4), named(common, number - number // 4 - 1))
    mixed = jax.random.permutation(jax.random.fold_in(own, 3), number_of)
    donor, sink = mixed[0:number_of // 2 * 2:2], mixed[1:number_of // 2 * 2:2]
    room = jnp.minimum(sizes[donor] - 1, limit - sizes[sink]) // 2
    room = jnp.where((donor == order[0]) | (sink == order[0]) | (sizes[sink] == 0), 0, jnp.maximum(room, 0))
    moved = jax.random.randint(jax.random.fold_in(own, 4), (number_of // 2,), 0, 1 << 20) % (room + 1)
    sizes = sizes.at[donor].add(-moved).at[sink].add(moved)
    items = jnp.searchsorted(jnp.cumsum(sizes), jnp.arange(rows * top), side="right").astype(jnp.int32)
    table = items.reshape(top, rows).T
    table = table[jax.random.permutation(jax.random.fold_in(own, 1), rows)]
    rotation = jax.random.randint(jax.random.fold_in(own, 2), (rows, 1), 0, top)
    return jnp.take_along_axis(table, (jnp.arange(top)[None, :] + rotation) % top, axis=1)


def load_shares(amount, total, limit, lean, full):
    portions = [(1 << 20) // math.isqrt(grade ** lean) + 1 for grade in range(1, amount + 1)]
    largest = limit if full else min(limit, max(-(-total // amount), total * portions[0] // sum(portions)))
    least = 1 if total - largest >= amount - 1 else 0
    counts, spare = [largest] + [least] * (amount - 1), total - largest - least * (amount - 1)
    while spare > 0:
        movable = [i for i in range(1, amount) if counts[i] < largest] or [i for i in range(1, amount) if counts[i] < limit]
        mass, budget = sum([portions[i] for i in movable]), spare
        for i in movable:
            addition = min(limit - counts[i], max(1, budget * portions[i] // mass), spare)
            counts[i] = counts[i] + addition
            spare = spare - addition
    return np.array(counts)


def noise(own_key, extent, width, limit, split=(), kind=jnp.bfloat16):
    entries = jax.random.normal(own_key, extent, jnp.float32) * width
    if len(split) > 0:
        entries = levels(own_key, extent, split, -0.22, 0.18) * entries
    return jnp.clip(entries, min=-limit, max=limit).astype(kind)


def setup_inputs(seed: int = 0, part: int = 0) -> dict:
    streams_of = jax.random.split(jax.random.key(seed), 21)
    part_keys = jax.random.split(jax.random.fold_in(streams_of[20], part), 21)
    currents = noise(part_keys[0], (INC, NP), 1.0, 6.0, ((1, 16),))
    near_tiles = noise(part_keys[1], (NEAR, TILE, TILE), (TILE * NEAR_PER) ** -0.5, 0.15625, ((0, 16),))
    near_target = set_ends(jax.random.randint(part_keys[2], (NEAR,), 0, BLK_DEV), jax.random.fold_in(part_keys[2], 1), 0, BLK_DEV - 1).astype(jnp.int32)
    near_source = draw_near_source(jax.random.fold_in(jax.random.fold_in(streams_of[20], part), 71), part)
    primal_compress = noise(part_keys[4], (NBLK, RANK, TILE), TILE ** -0.5, 0.375, ((0, 16),))
    primal_expand = noise(part_keys[5], (NBLK, RANK, TILE), RANK ** -0.5, 1.0, ((0, 16),))
    primal_coupling = noise(part_keys[6], (FAR, RANK * RANK), (RANK * FAR_PER) ** -0.5, 0.25, ((0, 16),))
    far_source = set_ends(jax.random.randint(part_keys[7], (FAR,), 0, BLK_DEV), jax.random.fold_in(part_keys[7], 1), 0, BLK_DEV - 1).astype(jnp.int32)
    far_owner_keys = jax.random.split(jax.random.fold_in(part_keys[8], 1), FAR // FAR_DEV)
    far_owner_turns = jax.random.permutation(jax.random.fold_in(part_keys[8], 3), FAR // FAR_DEV)
    far_owner = jax.vmap(lambda own, number: assign_block(jax.random.fold_in(part_keys[8], 2), own, number, FAR_DEV, N_SURF, 1, FCAP, 2))(far_owner_keys, far_owner_turns).reshape((FAR, 1))
    far_block = set_ends(jax.random.randint(part_keys[9], (FAR,), 0, BLK_DEV), jax.random.fold_in(part_keys[9], 1), 0, BLK_DEV - 1).astype(jnp.int32)
    gram_inverse = draw_gram_inverse(jax.random.fold_in(jax.random.fold_in(streams_of[20], part), 71), part)
    gram_lower = noise(part_keys[11], (NBLK, TILE, TILE), (TILE * 25 // 4) ** -0.5, 0.15625, ((0, 16),))
    gram_upper = noise(part_keys[12], (NBLK, TILE, TILE), (TILE * 25 // 4) ** -0.5, 0.15625, ((0, 16),))
    refine_weight = jnp.clip(jnp.exp(math.log(2.0) - 1.3862944 * jax.random.uniform(part_keys[13], (NP,), jnp.float32) ** levels(part_keys[13], (NP,), ((0, 16),), -0.2, 0.2)), 0.5, 2.0)
    dual_owner_keys = jax.random.split(jax.random.fold_in(part_keys[14], 1), NP // NP_DEV)
    dual_owner_turns = jax.random.permutation(jax.random.fold_in(part_keys[14], 3), NP // NP_DEV)
    dual_owner = jax.vmap(lambda own, number: assign_block(jax.random.fold_in(part_keys[14], 2), own, number, NP_DEV, N_SURF, 1, CAP, 2))(dual_owner_keys, dual_owner_turns).reshape((NP, 1))
    dual_index = set_ends(jax.random.randint(part_keys[15], (NP,), 0, NP_DEV), jax.random.fold_in(part_keys[15], 1), 0, NP_DEV - 1).astype(jnp.int32)
    dual_self = noise(part_keys[16], (NBLK, TILE, TILE), TILE ** -0.5, 0.375, ((0, 16),))
    dual_compress = noise(part_keys[17], (NBLK, RANK, TILE), TILE ** -0.5, 0.375, ((0, 16),))
    dual_expand = noise(part_keys[18], (NBLK, RANK, TILE), RANK ** -0.5, 1.0, ((0, 16),))
    dual_coupling = noise(part_keys[19], (FAR, RANK * RANK), (RANK * FAR_PER) ** -0.5, 0.25, ((0, 16),))
    return {"currents": currents, "near_tiles": near_tiles, "near_target": near_target, "near_source": near_source, "primal_compress": primal_compress, "primal_expand": primal_expand, "primal_coupling": primal_coupling, "far_source": far_source, "far_owner": far_owner, "far_block": far_block, "gram_inverse": gram_inverse, "gram_lower": gram_lower, "gram_upper": gram_upper, "refine_weight": refine_weight, "dual_owner": dual_owner, "dual_index": dual_index, "dual_self": dual_self, "dual_compress": dual_compress, "dual_expand": dual_expand, "dual_coupling": dual_coupling}


def narrow(value):
    return lax.optimization_barrier(value.astype(jnp.bfloat16)).astype(jnp.float32)


def apply_near(blocks, near_tiles, near_target, near_source):
    tile_sets = near_tiles.reshape(N_SURF, NEAR_DEV, TILE, TILE)
    targets = near_target.reshape(N_SURF, NEAR_DEV)
    sources = near_source.reshape(N_SURF, NEAR_DEV)

    def one_device(packed):
        tile_set, target_row, source_row = packed
        picked = jnp.take(blocks, source_row, axis=1)
        product = jnp.einsum('ikt,kts->iks', picked, tile_set.astype(jnp.float32))
        select = (target_row[:, None] == jnp.arange(BLK_DEV, dtype=jnp.int32)[None, :]).astype(jnp.float32)
        return jnp.einsum('iks,kb->ibs', product, select, precision=lax.Precision.HIGHEST)

    result = lax.map(one_device, (tile_sets, targets, sources))
    return jnp.transpose(result, (1, 0, 2, 3)).reshape(INC, NBLK, TILE)


def apply_far(blocks, compress, expand, coupling, far_source, far_owner, far_block):
    coefficients = narrow(jnp.einsum('ibt,brt->ibr', blocks, compress.astype(jnp.float32)))
    sources = (jnp.arange(FAR, dtype=jnp.int32) // FAR_DEV) * BLK_DEV + far_source
    targets = far_owner[:, 0] * BLK_DEV + far_block
    picked = jnp.take(coefficients, sources, axis=1)
    far_terms = jnp.einsum('ifr,frs->ifs', picked, coupling.reshape(FAR, RANK, RANK).astype(jnp.float32))
    summed = jnp.zeros((INC, NBLK, RANK), jnp.float32).at[:, targets, :].add(far_terms)
    summed = narrow(summed)
    return jnp.einsum('ibr,brt->ibt', summed, expand.astype(jnp.float32))


def reference(currents, near_tiles, near_target, near_source, primal_compress, primal_expand,
              primal_coupling, far_source, far_owner, far_block, gram_inverse, gram_lower,
              gram_upper, refine_weight, dual_owner, dual_index, dual_self, dual_compress,
              dual_expand, dual_coupling):
    blocks = currents.astype(jnp.float32).reshape(INC, NBLK, TILE)
    near_part = apply_near(blocks, near_tiles, near_target, near_source)
    far_part = apply_far(blocks, primal_compress, primal_expand, primal_coupling,
                         far_source, far_owner, far_block)
    primal_wide = narrow(near_part + far_part)
    inverse = gram_inverse.astype(jnp.float32)
    lower = gram_lower.astype(jnp.float32)
    upper = gram_upper.astype(jnp.float32)
    iterate = narrow(jnp.einsum('ibt,bts->ibs', primal_wide, inverse))
    for sweep_number in range(SWEEPS - 1):
        padded = jnp.pad(iterate, ((0, 0), (1, 1), (0, 0)))
        residue = primal_wide - jnp.einsum('ibt,bts->ibs', padded[:, :-2], lower)
        residue = residue - jnp.einsum('ibt,bts->ibs', padded[:, 2:], upper)
        iterate = narrow(jnp.einsum('ibt,bts->ibs', narrow(residue), inverse))
    shares = narrow(iterate.reshape(INC, NP) * refine_weight[None, :])
    destinations = dual_owner[:, 0] * NP_DEV + dual_index
    dual_field = narrow(jnp.zeros((INC, NP), jnp.float32).at[:, destinations].add(shares))
    dual_blocks = dual_field.reshape(INC, NBLK, TILE)
    near_dual = jnp.einsum('ibt,bts->ibs', dual_blocks, dual_self.astype(jnp.float32))
    far_dual = apply_far(dual_blocks, dual_compress, dual_expand, dual_coupling,
                         far_source, far_owner, far_block)
    return (near_dual + far_dual).reshape(INC, NP).astype(jnp.bfloat16)
```

```python
import functools

import jax
import jax.numpy as jnp
from jax import lax
from jax.experimental import pallas as pl
from jax.experimental.pallas import tpu as pltpu
from jax.sharding import PartitionSpec as P

TILE = 256
INC = 32
RANK = 32
BLK = 8
NP_DEV = 2048
IDX_ROWS = 16
F32 = jnp.float32
BF16 = jnp.bfloat16
NT = (((1,), (1,)), ((), ()))
VMEM_LIMIT = 48 * 1024 * 1024


def dot(a, b):
    return jnp.dot(a, b, preferred_element_type=F32)


def dot_nt(a, b):
    return lax.dot_general(a, b, NT, preferred_element_type=F32)


def iota(shape, dim):
    return lax.broadcasted_iota(jnp.int32, shape, dim)


def block(array, i):
    return array[:, i * TILE : (i + 1) * TILE]


def call(body, outs, args, scratch=(), smem=(), flops=0, name=None):
    specs = [
        pl.BlockSpec(memory_space=pltpu.SMEM if k in smem else pltpu.VMEM) for k in range(len(args))
    ]
    outs = tuple(jax.ShapeDtypeStruct(s, d) for s, d in outs)
    size = sum(a.size * a.dtype.itemsize for a in args) + sum(
        o.size * o.dtype.itemsize for o in outs
    )
    return pl.pallas_call(
        body,
        out_shape=outs,
        in_specs=specs,
        out_specs=tuple(pl.BlockSpec(memory_space=pltpu.VMEM) for _ in outs),
        scratch_shapes=list(scratch),
        compiler_params=pltpu.CompilerParams(vmem_limit_bytes=VMEM_LIMIT),
        cost_estimate=pl.CostEstimate(flops=flops, bytes_accessed=size, transcendentals=0),
        name=name,
    )(*args)


def transpose_coupling(coupling_ref, turned):
    turned[...] = coupling_ref[...].astype(F32).T


def far_terms(value, compress_ref, turned, source_ref, owner_ref, block_ref, coef, spread, pick, terms, out_ref):
    for s in range(BLK):
        coef[:, s * RANK : (s + 1) * RANK] = dot_nt(block(value, s), compress_ref[s])
    width = BLK * RANK
    keep = (iota((RANK, width), 1) % RANK) == iota((RANK, width), 0)
    for i in range(INC):
        spread[i * RANK : (i + 1) * RANK, :] = jnp.where(keep, coef[i : i + 1, :], 0.0).astype(BF16)
    tiles = source_ref.shape[1]
    chosen = (iota((width, tiles), 0) // RANK) == source_ref[...]
    pick[...] = dot(spread[...], chosen.astype(F32).astype(BF16))

    def step(pair, carry):
        rows = pl.multiple_of(pair * (2 * RANK), 2 * RANK)
        got = pick[pl.ds(rows, 2 * RANK), :]
        first = jnp.zeros((RANK, tiles), F32)
        second = jnp.zeros((RANK, tiles), F32)
        for r in range(RANK):
            factor = turned[r * RANK : (r + 1) * RANK, :]
            first += got[r : r + 1, :] * factor
            second += got[RANK + r : RANK + r + 1, :] * factor
        terms[pl.ds(rows, 2 * RANK), :] = jnp.concatenate([first, second], axis=0).astype(BF16)
        return carry

    lax.fori_loop(0, INC // 2, step, 0)
    targets = out_ref.shape[0]
    place = owner_ref[...] * BLK + block_ref[...]
    select = (iota((targets, tiles), 0) == place).astype(F32).astype(BF16)
    out_ref[...] = dot_nt(select, terms[...]).astype(BF16)


def far_scratch(tiles):
    return [
        pltpu.VMEM((INC, BLK * RANK), F32),
        pltpu.VMEM((INC * RANK, BLK * RANK), BF16),
        pltpu.VMEM((INC * RANK, tiles), F32),
        pltpu.VMEM((INC * RANK, tiles), BF16),
    ]


def far_up_body(value_ref, compress_ref, coupling_ref, source_ref, owner_ref, block_ref, out_ref, turned, *scratch):
    transpose_coupling(coupling_ref, turned)
    far_terms(value_ref[...], compress_ref, turned, source_ref, owner_ref, block_ref, *scratch, out_ref)


def far_down(arrived_ref, spread, expand_ref):
    rows = arrived_ref.shape[0]
    total = jnp.sum(arrived_ref[...].astype(F32).reshape(rows // BLK, BLK, INC * RANK), axis=0)
    width = INC * RANK
    keep = (iota((INC, width), 1) // RANK) == iota((INC, width), 0)
    for b in range(BLK):
        spread[b * INC : (b + 1) * INC, :] = jnp.where(keep, total[b : b + 1, :], 0.0).astype(BF16)
    fold = ((iota((width, RANK), 0) % RANK) == iota((width, RANK), 1)).astype(F32).astype(BF16)
    sums = dot(spread[...], fold).astype(BF16)
    return [dot(sums[b * INC : (b + 1) * INC, :], expand_ref[b]) for b in range(BLK)]


def near_body(target_ref, source_ref, cells_ref, tiles_ref, out_ref, total):
    total[...] = jnp.zeros_like(total)
    start = lax.axis_index("surf") * BLK - 1

    def step(k, carry):
        rel = source_ref[k] - start
        cell = cells_ref[:, pl.ds(pl.multiple_of(rel * TILE, TILE), TILE)]
        total[target_ref[k]] += dot(cell, tiles_ref[k])
        return carry

    lax.fori_loop(0, tiles_ref.shape[0], step, 0, unroll=4)
    for b in range(BLK):
        out_ref[:, b * TILE : (b + 1) * TILE] = total[b]


def products_body(inverse_ref, lower_ref, upper_ref, lower_out, upper_out):
    for b in range(BLK):
        lower_out[b] = dot(lower_ref[b], inverse_ref[b]).astype(BF16)
        upper_out[b] = dot(upper_ref[b], inverse_ref[b]).astype(BF16)


def solve_body(
    arrived_ref, near_ref, expand_ref, inverse_ref, lower_ref, upper_ref,
    start_out, next_out, left_out, right_out, spread,
):
    far = far_down(arrived_ref, spread, expand_ref)
    start, low = [], []
    for b in range(BLK):
        field = (block(near_ref, b) + far[b]).astype(BF16)
        value = dot(field, inverse_ref[b])
        start.append(value)
        low.append(value.astype(BF16))
        start_out[:, b * TILE : (b + 1) * TILE] = value
    after = []
    for b in range(BLK):
        value = start[b]
        if b > 0:
            value = value - dot(low[b - 1], lower_ref[b])
        if b < BLK - 1:
            value = value - dot(low[b + 1], upper_ref[b])
        after.append(value)
        next_out[:, b * TILE : (b + 1) * TILE] = value
    last = BLK - 1
    left_out[0] = low[0]
    left_out[1] = after[0].astype(BF16)
    left_out[2] = (start[0] - dot(after[1].astype(BF16), upper_ref[0])).astype(BF16)
    right_out[0] = low[last]
    right_out[1] = after[last].astype(BF16)
    right_out[2] = (start[last] - dot(after[last - 1].astype(BF16), lower_ref[last])).astype(BF16)


def finish_body(
    start_ref, next_ref, from_left, from_right, upper_left, lower_right, lower_ref, upper_ref,
    weight_ref, index_rows, place_ref, bounds_ref, send_ref, lhs, ordered,
):
    last = BLK - 1
    start = [block(start_ref, b) for b in range(BLK)]
    low = [start[0].astype(BF16), start[last].astype(BF16)]
    now = [block(next_ref, b) for b in range(BLK)]
    beside_left = from_left[1].astype(F32) - dot(low[0], upper_left[...])
    beside_right = from_right[1].astype(F32) - dot(low[1], lower_right[...])
    now[0] = now[0] - dot(from_left[0], lower_ref[0])
    now[last] = now[last] - dot(from_right[0], upper_ref[last])

    def sweep(values, left, right):
        values = [v.astype(BF16) for v in values]
        chain = [left.astype(BF16)] + values + [right.astype(BF16)]
        return values, [
            start[b] - dot(chain[b], lower_ref[b]) - dot(chain[b + 2], upper_ref[b])
            for b in range(BLK)
        ]

    values, then = sweep(now, beside_left, beside_right)
    beside_left = from_left[2].astype(F32) - dot(values[0], upper_left[...])
    beside_right = from_right[2].astype(F32) - dot(values[last], lower_right[...])
    values, then = sweep(then, beside_left, beside_right)
    for b in range(BLK):
        solved = then[b].astype(BF16).astype(F32)
        lhs[0:INC, b * TILE : (b + 1) * TILE] = (solved * block(weight_ref, b)).astype(BF16)
    lhs[INC : INC + IDX_ROWS, :] = index_rows[...]
    lane = iota((TILE, TILE), 1)
    columns = [jnp.broadcast_to(place_ref[:, b : b + 1], (TILE, TILE)) for b in range(BLK)]
    for p in range(BLK):
        total = jnp.zeros((INC + IDX_ROWS, TILE), F32)
        for b in range(BLK):
            hot = (lane + p * TILE == columns[b]).astype(F32).astype(BF16)
            total += dot(lhs[:, b * TILE : (b + 1) * TILE], hot)
        ordered[:, p * TILE : (p + 1) * TILE] = total
    owners, rows, window = send_ref.shape
    ordered[:, NP_DEV:] = jnp.zeros((rows, ordered.shape[1] - NP_DEV), F32)
    row = iota((rows, window), 0)
    slot = iota((rows, window), 1)
    wide = window + 128
    for o in range(owners):
        begin = bounds_ref[o, 0]
        base = pl.multiple_of((begin // 128) * 128, 128)
        piece = ordered[:, pl.ds(base, wide)]
        piece = pltpu.roll(piece, wide - (begin - base), 1)[:, :window]
        empty = (row >= INC) & (slot >= bounds_ref[o, 1])
        send_ref[o] = jnp.where(empty, -16.0, piece).astype(BF16)


def order_body(owner_ref, index_ref, place_out, bounds_out, rows_out, ranks):
    owners = bounds_out.shape[0]
    before = (iota((TILE, TILE), 0) < iota((TILE, TILE), 1)).astype(F32).astype(BF16)
    number = iota((owners, TILE), 0)
    count = jnp.zeros((owners, 1), F32)
    begin = jnp.zeros((owners, 1), F32)
    hots, carries = [], []
    for c in range(BLK):
        names = owner_ref[:, c * TILE : (c + 1) * TILE]
        hot = (number == names).astype(F32)
        hots.append(hot)
        carries.append(count)
        count = count + jnp.sum(hot, axis=1, keepdims=True)
        begin = begin + jnp.sum((names < number).astype(F32), axis=1, keepdims=True)
    for c in range(BLK):
        rank = dot(hots[c].astype(BF16), before)
        ranks[c : c + 1, :] = jnp.sum(hots[c] * (rank + carries[c] + begin), axis=0, keepdims=True)
    place_out[...] = ranks[...].T.astype(jnp.int32)
    pair = iota((owners, 2), 1)
    bounds_out[...] = jnp.where(pair == 0, begin, count).astype(jnp.int32)
    row = iota((IDX_ROWS, NP_DEV), 0)
    index = index_ref[...]
    digits = jnp.where(row == 0, index // TILE, jnp.where(row == 1, index % TILE, 0))
    rows_out[...] = digits.astype(F32).astype(BF16)


def gather_body(
    arrived_ref, compress_ref, coupling_ref, source_ref, owner_ref, block_ref,
    field_out, out_ref, index, turned, *scratch,
):
    transpose_coupling(coupling_ref, turned)
    owners, rows, window = arrived_ref.shape
    for e in range(owners):
        digits = arrived_ref[e, INC:, :].astype(F32)
        index[e : e + 1, :] = digits[0:1] * TILE + digits[1:2]
    columns = index[...].T.astype(jnp.int32)
    lane = iota((window, TILE), 1)
    wide = [jnp.broadcast_to(columns[:, e : e + 1], (window, TILE)) for e in range(owners)]
    for b in range(BLK):
        total = jnp.zeros((INC, TILE), F32)
        for e in range(owners):
            hot = (lane + b * TILE == wide[e]).astype(F32).astype(BF16)
            total += dot(arrived_ref[e, 0:INC, :], hot)
        field_out[:, b * TILE : (b + 1) * TILE] = total.astype(BF16)
    far_terms(field_out[...], compress_ref, turned, source_ref, owner_ref, block_ref, *scratch, out_ref)


def self_body(field_ref, self_ref, out_ref):
    for b in range(BLK):
        out_ref[:, b * TILE : (b + 1) * TILE] = dot(block(field_ref, b), self_ref[b])


def answer_body(arrived_ref, near_ref, expand_ref, out_ref, spread):
    far = far_down(arrived_ref, spread, expand_ref)
    for b in range(BLK):
        out_ref[:, b * TILE : (b + 1) * TILE] = (block(near_ref, b) + far[b]).astype(BF16)


def exchange(array, surf_count):
    shape = array.shape
    array = array.reshape((surf_count, shape[0] // surf_count) + shape[1:])
    array = lax.all_to_all(array, "surf", split_axis=0, concat_axis=0, tiled=True)
    return array.reshape(shape)


def shards(
    currents, near_tiles, near_target, near_source, primal_compress, primal_expand, primal_coupling,
    far_source, far_owner, far_block, gram_inverse, gram_lower, gram_upper, refine_weight,
    dual_owner, dual_index, dual_self, dual_compress, dual_expand, dual_coupling,
):
    surf_count = lax.axis_size("surf")
    tiles = far_source.shape[0]
    targets = surf_count * BLK
    capacity = max(2, 2 * NP_DEV // surf_count)
    window = max(128, -(-capacity // 128) * 128)
    to_right = [(i, i + 1) for i in range(surf_count - 1)]
    to_left = [(i + 1, i) for i in range(surf_count - 1)]
    source = far_source.reshape(1, tiles)
    owner = far_owner.reshape(1, tiles)
    place = far_block.reshape(1, tiles)

    from_left = lax.ppermute(currents[:, NP_DEV - TILE :], "surf", to_right)
    from_right = lax.ppermute(currents[:, :TILE], "surf", to_left)
    turned = pltpu.VMEM((RANK * RANK, tiles), F32)

    (partial,) = call(
        far_up_body,
        [((targets, INC * RANK), BF16)],
        (currents, primal_compress, primal_coupling, source, owner, place),
        scratch=[turned] + far_scratch(tiles),
        name="far_up",
    )
    arrived = exchange(partial, surf_count)

    lower, upper = call(
        products_body,
        [((BLK, TILE, TILE), BF16)] * 2,
        (gram_inverse, gram_lower, gram_upper),
        name="products",
    )
    upper_left = lax.ppermute(upper[BLK - 1], "surf", to_right)
    lower_right = lax.ppermute(lower[0], "surf", to_left)
    cells = jnp.concatenate([from_left, currents, from_right], axis=1)
    (near_part,) = call(
        near_body,
        [((INC, NP_DEV), F32)],
        (near_target, near_source, cells, near_tiles),
        scratch=[pltpu.VMEM((BLK, INC, TILE), F32)],
        smem=(0, 1),
        name="near",
    )
    where_to, bounds, index_rows = call(
        order_body,
        [((TILE, BLK), jnp.int32), ((surf_count, 2), jnp.int32), ((IDX_ROWS, NP_DEV), BF16)],
        (dual_owner.reshape(1, NP_DEV), dual_index.reshape(1, NP_DEV)),
        scratch=[pltpu.VMEM((BLK, TILE), F32)],
        name="order",
    )

    start, after, left_note, right_note = call(
        solve_body,
        [((INC, NP_DEV), F32)] * 2 + [((3, INC, TILE), BF16)] * 2,
        (arrived, near_part, primal_expand, gram_inverse, lower, upper),
        scratch=[pltpu.VMEM((BLK * INC, INC * RANK), BF16)],
        name="solve",
    )
    note_left = lax.ppermute(right_note, "surf", to_right)
    note_right = lax.ppermute(left_note, "surf", to_left)
    (send,) = call(
        finish_body,
        [((surf_count, INC + IDX_ROWS, window), BF16)],
        (
            start, after, note_left, note_right, upper_left, lower_right, lower, upper,
            refine_weight.reshape(1, NP_DEV), index_rows, where_to, bounds,
        ),
        scratch=[
            pltpu.VMEM((INC + IDX_ROWS, NP_DEV), BF16),
            pltpu.VMEM((INC + IDX_ROWS, NP_DEV + window + 128), F32),
        ],
        smem=(11,),
        name="finish",
    )
    shares = lax.all_to_all(send, "surf", split_axis=0, concat_axis=0, tiled=True)
    field, partial = call(
        gather_body,
        [((INC, NP_DEV), BF16), ((targets, INC * RANK), BF16)],
        (shares, dual_compress, dual_coupling, source, owner, place),
        scratch=[pltpu.VMEM((surf_count, window), F32), turned] + far_scratch(tiles),
        name="gather",
    )
    arrived = exchange(partial, surf_count)
    (near_dual,) = call(self_body, [((INC, NP_DEV), F32)], (field, dual_self), name="self_part")
    (response,) = call(
        answer_body,
        [((INC, NP_DEV), BF16)],
        (arrived, near_dual, dual_expand),
        scratch=[pltpu.VMEM((BLK * INC, INC * RANK), BF16)],
        name="answer",
    )
    return response


def solution(mesh):
    both = ("groups", "surf")
    row, flat = P(None, both), P(both)
    cube, flat2 = P(both, None, None), P(both, None)
    return jax.shard_map(
        shards,
        mesh=mesh,
        in_specs=(
            row, cube, flat, flat, cube, cube, flat2, flat, flat2, flat, cube, cube, cube, flat,
            flat2, flat, cube, cube, cube, flat2,
        ),
        out_specs=row,
        check_vma=False,
    )
```

```python
import jax
import jax.numpy as jnp
from jax import lax
from jax.experimental import pallas as pl
from jax.experimental.pallas import tpu as pltpu
from jax.sharding import PartitionSpec as P

TILE = 256
INC = 32
RANK = 32
BLK = 8
NP_DEV = 2048
LANES = 128
IDX_ROWS = 16
TAIL = 8
NEAR_CHUNK = 8
F32 = jnp.float32
BF16 = jnp.bfloat16
I32 = jnp.int32
NT = (((1,), (1,)), ((), ()))
VMEM_LIMIT = 24 * 1024 * 1024


def dot(a, b):
    return jnp.dot(a, b, preferred_element_type=F32)


def dot_nt(a, b):
    return lax.dot_general(a, b, NT, preferred_element_type=F32)


def iota(shape, dim):
    return lax.broadcasted_iota(I32, shape, dim)


def block(array, i):
    return array[:, i * TILE : (i + 1) * TILE]


def as_hot(mask):
    return mask.astype(F32).astype(BF16)


def call(body, outs, args, scratch=(), smem=(), held=(), far=(), small=(), name=None):
    spaces = [
        pltpu.SMEM if k in smem else pltpu.HBM if k in held or k in far else pltpu.VMEM
        for k in range(len(args))
    ]
    outs = tuple(jax.ShapeDtypeStruct(s, d) for s, d in outs)
    size = sum(a.size * a.dtype.itemsize for a in args) + sum(
        o.size * o.dtype.itemsize for o in outs
    )
    buffers = [
        (pltpu.SMEM if k in small else pltpu.VMEM)(args[k].shape, args[k].dtype) for k in held
    ]
    waits = [pltpu.SemaphoreType.DMA(()) for _ in held]

    def wrapped(*refs):
        ins = list(refs[: len(args)])
        rest = refs[len(args) : len(refs) - 2 * len(held)]
        extra = refs[len(refs) - 2 * len(held) :]
        for n, k in enumerate(held):
            ins[k] = pltpu.make_async_copy(ins[k], extra[n], extra[len(held) + n])
            ins[k].start()
            ins[k] = (ins[k], extra[n])
        body(*ins, *rest)

    return pl.pallas_call(
        wrapped,
        out_shape=outs,
        in_specs=[pl.BlockSpec(memory_space=m) for m in spaces],
        out_specs=tuple(pl.BlockSpec(memory_space=pltpu.VMEM) for _ in outs),
        scratch_shapes=list(scratch) + buffers + waits,
        compiler_params=pltpu.CompilerParams(vmem_limit_bytes=VMEM_LIMIT),
        cost_estimate=pl.CostEstimate(flops=0, bytes_accessed=size, transcendentals=0),
        name=name,
    )(*[pltpu.with_memory_space_constraint(a, m) if m is pltpu.HBM else a for a, m in zip(args, spaces)])


def ready(operand):
    operand[0].wait()
    return operand[1]


def far_terms(blocks, compress, coupling, source, owner, place, coef, turned, spread, pick, terms, out_ref):
    coupling = ready(coupling)
    turned[...] = coupling[...].astype(F32).T
    compress = ready(compress)
    for s in range(BLK):
        coef[:, s * RANK : (s + 1) * RANK] = dot_nt(blocks[s], compress[s])
    width = BLK * RANK
    keep = (iota((RANK, width), 1) % RANK) == iota((RANK, width), 0)
    for i in range(INC):
        spread[i * RANK : (i + 1) * RANK, :] = jnp.where(keep, coef[i : i + 1, :], 0.0).astype(BF16)
    source = ready(source)
    tiles = source.shape[1]
    pick[...] = dot(spread[...], as_hot((iota((width, tiles), 0) // RANK) == source[...]))

    def step(pair, carry):
        rows = pl.multiple_of(pair * (2 * RANK), 2 * RANK)
        got = pick[pl.ds(rows, 2 * RANK), :]
        first = jnp.zeros((RANK, tiles), F32)
        second = jnp.zeros((RANK, tiles), F32)
        for r in range(RANK):
            factor = turned[r * RANK : (r + 1) * RANK, :]
            first += got[r : r + 1, :] * factor
            second += got[RANK + r : RANK + r + 1, :] * factor
        terms[pl.ds(rows, 2 * RANK), :] = jnp.concatenate([first, second], axis=0).astype(BF16)
        return carry

    lax.fori_loop(0, INC // 2, step, 0)
    targets = out_ref.shape[0]
    owner, place = ready(owner), ready(place)
    select = as_hot(iota((targets, tiles), 0) == owner[...] * BLK + place[...])
    out_ref[...] = dot_nt(select, terms[...]).astype(BF16)


def far_scratch(tiles):
    return [
        pltpu.VMEM((INC, BLK * RANK), F32),
        pltpu.VMEM((RANK * RANK, tiles), F32),
        pltpu.VMEM((INC * RANK, BLK * RANK), BF16),
        pltpu.VMEM((INC * RANK, tiles), F32),
        pltpu.VMEM((INC * RANK, tiles), BF16),
    ]


def far_up_body(value, compress, coupling, source, owner, place, out_ref, first_out, last_out, *scratch):
    value = ready(value)
    first_out[...] = block(value, 0)
    last_out[...] = block(value, BLK - 1)
    blocks = [block(value, s) for s in range(BLK)]
    far_terms(blocks, compress, coupling, source, owner, place, *scratch, out_ref)


def far_down(arrived_ref, spread, expand):
    rows = arrived_ref.shape[0]
    total = jnp.sum(arrived_ref[...].astype(F32).reshape(rows // BLK, BLK, INC * RANK), axis=0)
    width = INC * RANK
    keep = (iota((INC, width), 1) // RANK) == iota((INC, width), 0)
    for b in range(BLK):
        spread[b * INC : (b + 1) * INC, :] = jnp.where(keep, total[b : b + 1, :], 0.0).astype(BF16)
    fold = as_hot((iota((width, RANK), 0) % RANK) == iota((width, RANK), 1))
    sums = dot(spread[...], fold).astype(BF16)
    expand = ready(expand)
    return [dot(sums[b * INC : (b + 1) * INC, :], expand[b]) for b in range(BLK)]


def order(owner, index, ranks, owners, window, high_out, low_out, bounds_out, rows_out):
    before = as_hot(iota((TILE, TILE), 0) < iota((TILE, TILE), 1))
    number = iota((owners, TILE), 0)
    count = jnp.zeros((owners, 1), F32)
    begin = jnp.zeros((owners, 1), F32)
    hots, carries = [], []
    for c in range(BLK):
        names = block(owner, c)
        hot = (number == names).astype(F32)
        hots.append(hot)
        carries.append(count)
        count = count + jnp.sum(hot, axis=1, keepdims=True)
        begin = begin + jnp.sum((names < number).astype(F32), axis=1, keepdims=True)
    for c in range(BLK):
        rank = dot(hots[c].astype(BF16), before)
        ranks[c : c + 1, :] = jnp.sum(hots[c] * (rank + carries[c] + begin), axis=0, keepdims=True)
    spots = ranks[...].astype(I32)
    high_out[...] = spots // TILE
    low = (spots % TILE).astype(F32).T.astype(I32)
    lane = iota((TILE, TILE), 1)
    for c in range(BLK):
        low_out[c * TILE : (c + 1) * TILE, :] = as_hot(lane == low[:, c : c + 1])
    pair = iota((owners, 2), 1)
    bounds_out[...] = jnp.where(pair == 0, begin, count).astype(I32)
    row = iota((IDX_ROWS, NP_DEV), 0)
    index = index[...]
    digits = jnp.where(row % 2 == 0, index // TILE, index % TILE)
    rows_out[...] = jnp.where(row < 2 * (window // LANES), digits, 0).astype(F32).astype(BF16)


def prepare_body(
    target, origin, own, from_left, from_right, inverse, lower, upper, owner, index, tiles_ref,
    near_out, lower_out, upper_out, lower_edge, upper_edge, high_out, low_out, bounds_out, rows_out,
    cells, total, ranks, tiles, arrivals,
):
    count = tiles_ref.shape[0]
    copies = []
    for c in range(count // NEAR_CHUNK):
        part = pl.ds(c * NEAR_CHUNK, NEAR_CHUNK)
        copy = pltpu.make_async_copy(tiles_ref.at[part], tiles.at[part], arrivals.at[c])
        copy.start()
        copies.append(copy)
    owner, index = ready(owner), ready(index)
    window = max(LANES, -(-(2 * NP_DEV // bounds_out.shape[0]) // LANES) * LANES)
    order(owner, index, ranks, bounds_out.shape[0], window, high_out, low_out, bounds_out, rows_out)
    inverse, lower, upper = ready(inverse), ready(lower), ready(upper)
    for b in range(BLK):
        lower_out[b] = dot(lower[b], inverse[b]).astype(BF16)
        upper_out[b] = dot(upper[b], inverse[b]).astype(BF16)
    lower_edge[...] = lower_out[0]
    upper_edge[...] = upper_out[BLK - 1]
    own = ready(own)
    cells[0] = from_left[...]
    cells[BLK + 1] = from_right[...]
    for b in range(BLK):
        cells[b + 1] = block(own, b)
    total[...] = jnp.zeros_like(total)
    target, origin = ready(target), ready(origin)
    start = lax.axis_index("surf") * BLK - 1
    for c, copy in enumerate(copies):
        copy.wait()
        for k in range(c * NEAR_CHUNK, (c + 1) * NEAR_CHUNK):
            total[target[k]] += dot(cells[origin[k] - start], tiles[k])
    for b in range(BLK):
        near_out[:, b * TILE : (b + 1) * TILE] = total[b]


def solve_body(
    arrived_ref, near_ref, expand, inverse, lower_ref, upper_ref,
    start_out, next_out, left_out, right_out, spread,
):
    far = far_down(arrived_ref, spread, expand)
    inverse = ready(inverse)
    start, low = [], []
    for b in range(BLK):
        field = (block(near_ref, b) + far[b]).astype(BF16)
        value = dot(field, inverse[b])
        start.append(value)
        low.append(value.astype(BF16))
        start_out[:, b * TILE : (b + 1) * TILE] = value
    after = []
    for b in range(BLK):
        value = start[b]
        if b > 0:
            value = value - dot(low[b - 1], lower_ref[b])
        if b < BLK - 1:
            value = value - dot(low[b + 1], upper_ref[b])
        after.append(value)
        next_out[:, b * TILE : (b + 1) * TILE] = value
    last = BLK - 1
    left_out[0] = low[0]
    left_out[1] = after[0].astype(BF16)
    left_out[2] = (start[0] - dot(after[1].astype(BF16), upper_ref[0])).astype(BF16)
    right_out[0] = low[last]
    right_out[1] = after[last].astype(BF16)
    right_out[2] = (start[last] - dot(after[last - 1].astype(BF16), lower_ref[last])).astype(BF16)


def finish_body(
    start_ref, next_ref, from_left, from_right, upper_left, lower_right, lower_ref, upper_ref,
    weight, index_rows, high_ref, low_ref, bounds_ref, send_ref, spread, ordered,
):
    last = BLK - 1
    position = lax.axis_index("surf")
    has_left = (position > 0).astype(F32)
    has_right = (position < lax.axis_size("surf") - 1).astype(F32)
    start = [block(start_ref, b) for b in range(BLK)]
    low = [start[0].astype(BF16), start[last].astype(BF16)]
    now = [block(next_ref, b) for b in range(BLK)]
    beside_left = (from_left[1].astype(F32) - dot(low[0], upper_left[...])) * has_left
    beside_right = (from_right[1].astype(F32) - dot(low[1], lower_right[...])) * has_right
    now[0] = now[0] - dot(from_left[0], lower_ref[0]) * has_left
    now[last] = now[last] - dot(from_right[0], upper_ref[last]) * has_right

    def sweep(values, left, right):
        values = [v.astype(BF16) for v in values]
        chain = [left.astype(BF16)] + values + [right.astype(BF16)]
        return values, [
            start[b] - dot(chain[b], lower_ref[b]) - dot(chain[b + 2], upper_ref[b])
            for b in range(BLK)
        ]

    values, then = sweep(now, beside_left, beside_right)
    beside_left = (from_left[2].astype(F32) - dot(values[0], upper_left[...])) * has_left
    beside_right = (from_right[2].astype(F32) - dot(values[last], lower_right[...])) * has_right
    values, then = sweep(then, beside_left, beside_right)
    weight = ready(weight)
    rows = INC + IDX_ROWS
    for b in range(BLK):
        solved = then[b].astype(BF16).astype(F32)
        shares = solved * block(weight, b)
        every = jnp.concatenate([shares, block(index_rows, b).astype(F32)], axis=0)
        high = high_ref[b : b + 1, :]
        for h in range(BLK):
            spread[h * rows : (h + 1) * rows, b * TILE : (b + 1) * TILE] = jnp.where(
                high == h, every, 0.0
            ).astype(BF16)
    sorted_rows = dot(spread[...], low_ref[...])
    for h in range(BLK):
        ordered[:, h * TILE : (h + 1) * TILE] = sorted_rows[h * rows : (h + 1) * rows]
    owners = send_ref.shape[0]
    pieces = (send_ref.shape[1] - TAIL) // INC
    wide = (pieces + 1) * LANES
    ordered[:, NP_DEV:] = jnp.zeros((rows, ordered.shape[1] - NP_DEV), F32)
    row = iota((TAIL, LANES), 0)
    slot = iota((TAIL, LANES), 1) + (row // 2) * LANES
    for o in range(owners):
        begin = bounds_ref[o, 0]
        base = pl.multiple_of((begin // LANES) * LANES, LANES)
        piece = pltpu.roll(ordered[:, pl.ds(base, wide)], wide - (begin - base), 1)
        parts = [piece[:INC, j * LANES : (j + 1) * LANES] for j in range(pieces)]
        tail = piece[INC : INC + TAIL, :LANES]
        for j in range(1, pieces):
            tail = jnp.where(row // 2 == j, piece[INC : INC + TAIL, j * LANES : (j + 1) * LANES], tail)
        tail = jnp.where(slot >= bounds_ref[o, 1], -16.0, tail)
        send_ref[o] = jnp.concatenate(parts + [tail], axis=0).astype(BF16)


def gather_body(
    arrived_ref, compress, coupling, source, owner, place,
    field_out, out_ref, index, spread, hot, *scratch,
):
    owners, rows, _ = arrived_ref.shape
    pieces = (rows - TAIL) // INC
    for e in range(owners):
        digits = arrived_ref[e].astype(F32)
        tail = digits[INC * pieces :]
        for j in range(pieces):
            k = e * pieces + j
            part = digits[j * INC : (j + 1) * INC]
            high = tail[2 * j : 2 * j + 1]
            index[k : k + 1, :] = tail[2 * j + 1 : 2 * j + 2]
            for h in range(BLK):
                spread[h * INC : (h + 1) * INC, k * LANES : (k + 1) * LANES] = jnp.where(
                    high == h, part, 0.0
                ).astype(BF16)
    columns = index[...].T.astype(I32)
    lane = iota((LANES, TILE), 1)
    for k in range(owners * pieces):
        hot[k * LANES : (k + 1) * LANES, :] = as_hot(lane == columns[:, k : k + 1])
    field = dot(spread[...], hot[...]).astype(BF16)
    blocks = [field[b * INC : (b + 1) * INC] for b in range(BLK)]
    for b in range(BLK):
        field_out[b] = blocks[b]
    far_terms(blocks, compress, coupling, source, owner, place, *scratch, out_ref)


def self_body(field_ref, tiles, out_ref):
    tiles = ready(tiles)
    for b in range(BLK):
        out_ref[:, b * TILE : (b + 1) * TILE] = dot(field_ref[b], tiles[b])


def answer_body(arrived_ref, near_ref, expand, out_ref, spread):
    far = far_down(arrived_ref, spread, expand)
    for b in range(BLK):
        out_ref[:, b * TILE : (b + 1) * TILE] = (block(near_ref, b) + far[b]).astype(BF16)


def exchange(array, surf_count):
    shape = array.shape
    array = array.reshape((surf_count, shape[0] // surf_count) + shape[1:])
    array = lax.all_to_all(array, "surf", split_axis=0, concat_axis=0, tiled=True)
    return array.reshape(shape)


def shards(
    currents, near_tiles, near_target, near_source, primal_compress, primal_expand, primal_coupling,
    far_source, far_owner, far_block, gram_inverse, gram_lower, gram_upper, refine_weight,
    dual_owner, dual_index, dual_self, dual_compress, dual_expand, dual_coupling,
):
    surf_count = lax.axis_size("surf")
    tiles = far_source.shape[0]
    near_count = near_tiles.shape[0]
    targets = surf_count * BLK
    capacity = max(2, 2 * NP_DEV // surf_count)
    pieces = -(-capacity // LANES)
    to_right = [(i, (i + 1) % surf_count) for i in range(surf_count)]
    to_left = [((i + 1) % surf_count, i) for i in range(surf_count)]
    lists = (far_source.reshape(1, tiles), far_owner.reshape(1, tiles), far_block.reshape(1, tiles))
    square = ((TILE, TILE), BF16)
    cube = ((BLK, TILE, TILE), BF16)

    partial, first, last = call(
        far_up_body,
        [((targets, INC * RANK), BF16), ((INC, TILE), BF16), ((INC, TILE), BF16)],
        (currents, primal_compress, primal_coupling) + lists,
        scratch=far_scratch(tiles),
        held=(2, 0, 1, 3, 4, 5),
        name="far_up",
    )
    from_left = lax.ppermute(last, "surf", to_right)
    from_right = lax.ppermute(first, "surf", to_left)
    arrived = exchange(partial, surf_count)

    near_part, lower, upper, lower_edge, upper_edge, high, low, bounds, index_rows = call(
        prepare_body,
        [
            ((INC, NP_DEV), F32), cube, cube, square, square, ((BLK, TILE), I32),
            ((NP_DEV, TILE), BF16), ((surf_count, 2), I32), ((IDX_ROWS, NP_DEV), BF16),
        ],
        (
            near_target, near_source, currents, from_left, from_right, gram_inverse, gram_lower,
            gram_upper, dual_owner.reshape(1, NP_DEV), dual_index.reshape(1, NP_DEV), near_tiles,
        ),
        scratch=[
            pltpu.VMEM((BLK + 2, INC, TILE), BF16),
            pltpu.VMEM((BLK, INC, TILE), F32),
            pltpu.VMEM((BLK, TILE), F32),
            pltpu.VMEM(near_tiles.shape, BF16),
            pltpu.SemaphoreType.DMA((near_count // NEAR_CHUNK,)),
        ],
        held=(8, 9, 5, 6, 7, 2, 0, 1),
        far=(10,),
        small=(0, 1),
        name="prepare",
    )
    upper_left = lax.ppermute(upper_edge, "surf", to_right)
    lower_right = lax.ppermute(lower_edge, "surf", to_left)

    start, after, left_note, right_note = call(
        solve_body,
        [((INC, NP_DEV), F32)] * 2 + [((3, INC, TILE), BF16)] * 2,
        (arrived, near_part, primal_expand, gram_inverse, lower, upper),
        scratch=[pltpu.VMEM((BLK * INC, INC * RANK), BF16)],
        held=(2, 3),
        name="solve",
    )
    note_left = lax.ppermute(right_note, "surf", to_right)
    note_right = lax.ppermute(left_note, "surf", to_left)
    rows = INC + IDX_ROWS
    (send,) = call(
        finish_body,
        [((surf_count, INC * pieces + TAIL, LANES), BF16)],
        (
            start, after, note_left, note_right, upper_left, lower_right, lower, upper,
            refine_weight.reshape(1, NP_DEV), index_rows, high, low, bounds,
        ),
        scratch=[
            pltpu.VMEM((BLK * rows, NP_DEV), BF16),
            pltpu.VMEM((rows, NP_DEV + (pieces + 1) * LANES), F32),
        ],
        smem=(12,),
        held=(8,),
        name="finish",
    )
    shares = lax.all_to_all(send, "surf", split_axis=0, concat_axis=0, tiled=True)
    slots = surf_count * pieces * LANES
    field, partial = call(
        gather_body,
        [((BLK, INC, TILE), BF16), ((targets, INC * RANK), BF16)],
        (shares, dual_compress, dual_coupling) + lists,
        scratch=[
            pltpu.VMEM((surf_count * pieces, LANES), F32),
            pltpu.VMEM((BLK * INC, slots), BF16),
            pltpu.VMEM((slots, TILE), BF16),
        ]
        + far_scratch(tiles),
        held=(2, 1, 3, 4, 5),
        name="gather",
    )
    arrived = exchange(partial, surf_count)
    (near_dual,) = call(
        self_body, [((INC, NP_DEV), F32)], (field, dual_self), held=(1,), name="self_part"
    )
    (response,) = call(
        answer_body,
        [((INC, NP_DEV), BF16)],
        (arrived, near_dual, dual_expand),
        scratch=[pltpu.VMEM((BLK * INC, INC * RANK), BF16)],
        held=(2,),
        name="answer",
    )
    return response


def solution(mesh):
    both = ("groups", "surf")
    row, flat = P(None, both), P(both)
    cube, flat2 = P(both, None, None), P(both, None)
    return jax.shard_map(
        shards,
        mesh=mesh,
        in_specs=(
            row, cube, flat, flat, cube, cube, flat2, flat, flat2, flat, cube, cube, cube, flat,
            flat2, flat, cube, cube, cube, flat2,
        ),
        out_specs=row,
        check_vma=False,
    )
```

```python
import jax
import jax.numpy as jnp
from jax import lax
from jax.experimental import pallas as pl
from jax.experimental.pallas import tpu as pltpu
from jax.sharding import PartitionSpec as P

TILE = 256
INC = 32
RANK = 32
BLK = 8
NP_DEV = 2048
LANES = 128
IDX_ROWS = 16
TAIL = 8
NEAR_CHUNK = 8
F32 = jnp.float32
BF16 = jnp.bfloat16
I32 = jnp.int32
NT = (((1,), (1,)), ((), ()))
VMEM_LIMIT = 24 * 1024 * 1024


def dot(a, b):
    return jnp.dot(a, b, preferred_element_type=F32)


def dot_nt(a, b):
    return lax.dot_general(a, b, NT, preferred_element_type=F32)


def iota(shape, dim):
    return lax.broadcasted_iota(I32, shape, dim)


def block(array, i):
    return array[:, i * TILE : (i + 1) * TILE]


def as_hot(mask):
    return mask.astype(F32).astype(BF16)


def call(body, outs, args, scratch=(), smem=(), held=(), far=(), small=(), pinned=(), kept=(), flops=0, name=None):
    spaces = [
        pltpu.SMEM if k in smem else pltpu.HBM if k in held or k in far else pltpu.VMEM
        for k in range(len(args))
    ]
    size = sum(a.size * a.dtype.itemsize for a in args)
    outs = tuple(
        pltpu.VMEM(s, d) if k in kept else jax.ShapeDtypeStruct(s, d)
        for k, (s, d) in enumerate(outs)
    )
    buffers = [
        (pltpu.SMEM if k in small else pltpu.VMEM)(args[k].shape, args[k].dtype) for k in held
    ]
    waits = [pltpu.SemaphoreType.DMA(()) for _ in held]

    def wrapped(*refs):
        ins = list(refs[: len(args)])
        rest = refs[len(args) : len(refs) - 2 * len(held)]
        extra = refs[len(refs) - 2 * len(held) :]
        for n, k in enumerate(held):
            ins[k] = pltpu.make_async_copy(ins[k], extra[n], extra[len(held) + n])
            ins[k].start()
            ins[k] = (ins[k], extra[n])
        body(*ins, *rest)

    return pl.pallas_call(
        wrapped,
        out_shape=outs,
        in_specs=[pl.BlockSpec(memory_space=m) for m in spaces],
        out_specs=tuple(pl.BlockSpec(memory_space=pltpu.VMEM) for _ in outs),
        scratch_shapes=list(scratch) + buffers + waits,
        compiler_params=pltpu.CompilerParams(vmem_limit_bytes=VMEM_LIMIT),
        cost_estimate=pl.CostEstimate(flops=flops, bytes_accessed=size, transcendentals=0),
        name=name,
    )(*[pltpu.with_memory_space_constraint(a, m) if m is pltpu.HBM or k in pinned else a for k, (a, m) in enumerate(zip(args, spaces))])


def ready(operand):
    operand[0].wait()
    return operand[1]


def fill_hot(hot, columns):
    height, count = columns.shape
    columns = columns.astype(BF16)
    lane = iota((height, TILE), 1).astype(F32).astype(BF16)
    one, zero = jnp.ones((height, TILE), BF16), jnp.zeros((height, TILE), BF16)
    for k in range(count):
        hot[k * height : (k + 1) * height, :] = jnp.where(lane == columns[:, k : k + 1], one, zero)


def far_terms(blocks, compress, coupling, source, owner, place, coef, turned, spread, pick, terms, out_ref):
    coupling = ready(coupling)
    turned[...] = coupling[...].astype(F32).T
    compress = ready(compress)
    for s in range(BLK):
        coef[:, s * RANK : (s + 1) * RANK] = dot_nt(blocks[s], compress[s])
    width = BLK * RANK
    keep = (iota((RANK, width), 1) % RANK) == iota((RANK, width), 0)
    for i in range(INC):
        spread[i * RANK : (i + 1) * RANK, :] = jnp.where(keep, coef[i : i + 1, :], 0.0).astype(BF16)
    source = ready(source)
    tiles = source.shape[1]
    pick[...] = dot(spread[...], as_hot((iota((width, tiles), 0) // RANK) == source[...]))

    def step(pair, carry):
        rows = pl.multiple_of(pair * (2 * RANK), 2 * RANK)
        got = pick[pl.ds(rows, 2 * RANK), :]
        first = jnp.zeros((RANK, tiles), F32)
        second = jnp.zeros((RANK, tiles), F32)
        for r in range(RANK):
            factor = turned[r * RANK : (r + 1) * RANK, :]
            first += got[r : r + 1, :] * factor
            second += got[RANK + r : RANK + r + 1, :] * factor
        terms[pl.ds(rows, 2 * RANK), :] = jnp.concatenate([first, second], axis=0).astype(BF16)
        return carry

    lax.fori_loop(0, INC // 2, step, 0)
    targets = out_ref.shape[0]
    owner, place = ready(owner), ready(place)
    select = as_hot(iota((targets, tiles), 0) == owner[...] * BLK + place[...])
    out_ref[...] = dot_nt(select, terms[...]).astype(BF16)


def far_scratch(tiles):
    return [
        pltpu.VMEM((INC, BLK * RANK), F32),
        pltpu.VMEM((RANK * RANK, tiles), F32),
        pltpu.VMEM((INC * RANK, BLK * RANK), BF16),
        pltpu.VMEM((INC * RANK, tiles), F32),
        pltpu.VMEM((INC * RANK, tiles), BF16),
    ]


def far_up_body(value, compress, coupling, source, owner, place, out_ref, *scratch):
    value = ready(value)
    blocks = [block(value, s) for s in range(BLK)]
    far_terms(blocks, compress, coupling, source, owner, place, *scratch, out_ref)


def far_down(arrived_ref, spread, expand):
    rows = arrived_ref.shape[0]
    total = jnp.sum(arrived_ref[...].astype(F32).reshape(rows // BLK, BLK, INC * RANK), axis=0)
    width = INC * RANK
    keep = (iota((INC, width), 1) // RANK) == iota((INC, width), 0)
    for b in range(BLK):
        spread[b * INC : (b + 1) * INC, :] = jnp.where(keep, total[b : b + 1, :], 0.0).astype(BF16)
    fold = as_hot((iota((width, RANK), 0) % RANK) == iota((width, RANK), 1))
    sums = dot(spread[...], fold).astype(BF16)
    expand = ready(expand)
    return [dot(sums[b * INC : (b + 1) * INC, :], expand[b]) for b in range(BLK)]


def order(owner, index, ranks, owners, window, high_out, low_out, bounds_out, rows_out):
    before = as_hot(iota((TILE, TILE), 0) < iota((TILE, TILE), 1))
    number = iota((owners, TILE), 0)
    count = jnp.zeros((owners, 1), F32)
    begin = jnp.zeros((owners, 1), F32)
    hots, carries = [], []
    for c in range(BLK):
        names = block(owner, c)
        hot = (number == names).astype(F32)
        hots.append(hot)
        carries.append(count)
        count = count + jnp.sum(hot, axis=1, keepdims=True)
        begin = begin + jnp.sum((names < number).astype(F32), axis=1, keepdims=True)
    for c in range(BLK):
        rank = dot(hots[c].astype(BF16), before)
        ranks[c : c + 1, :] = jnp.sum(hots[c] * (rank + carries[c] + begin), axis=0, keepdims=True)
    spots = ranks[...].astype(I32)
    high_out[...] = spots // TILE
    low_out[...] = (spots % TILE).astype(F32).T
    pair = iota((owners, 2), 1)
    bounds_out[...] = jnp.where(pair == 0, begin, count).astype(I32)
    row = iota((IDX_ROWS, NP_DEV), 0)
    index = index[...]
    digits = jnp.where(row % 2 == 0, index // TILE, index % TILE)
    rows_out[...] = jnp.where(row < 2 * (window // LANES), digits, 0).astype(F32).astype(BF16)


def prepare_body(
    target, origin, own, from_left, from_right, inverse, lower, upper, owner, index, tiles_ref,
    near_out, lower_out, upper_out, lower_edge, upper_edge, high_out, low_out, bounds_out, rows_out,
    cells, total, products, ranks, tiles, arrivals,
):
    count = tiles_ref.shape[0]
    copies = []
    for c in range(count // NEAR_CHUNK):
        part = pl.ds(c * NEAR_CHUNK, NEAR_CHUNK)
        copy = pltpu.make_async_copy(tiles_ref.at[part], tiles.at[part], arrivals.at[c])
        copy.start()
        copies.append(copy)
    owner, index = ready(owner), ready(index)
    window = max(LANES, -(-(2 * NP_DEV // bounds_out.shape[0]) // LANES) * LANES)
    order(owner, index, ranks, bounds_out.shape[0], window, high_out, low_out, bounds_out, rows_out)
    inverse, lower, upper = ready(inverse), ready(lower), ready(upper)
    for b in range(BLK):
        lower_out[b] = dot(lower[b], inverse[b]).astype(BF16)
        upper_out[b] = dot(upper[b], inverse[b]).astype(BF16)
    lower_edge[...] = lower_out[0]
    upper_edge[...] = upper_out[BLK - 1]
    own = ready(own)
    cells[0] = block(from_left, BLK - 1)
    cells[BLK + 1] = block(from_right, 0)
    for b in range(BLK):
        cells[b + 1] = block(own, b)
    total[...] = jnp.zeros_like(total)
    target, origin = ready(target), ready(origin)
    start = lax.axis_index("surf") * BLK - 1
    for c, copy in enumerate(copies):
        copy.wait()
        for k in range(c * NEAR_CHUNK, (c + 1) * NEAR_CHUNK):
            products[k] = dot(cells[origin[k] - start], tiles[k])
    for k in range(count):
        total[target[k]] += products[k]
    for b in range(BLK):
        near_out[:, b * TILE : (b + 1) * TILE] = total[b]


def solve_body(
    arrived_ref, near_ref, expand, inverse, lower_ref, upper_ref,
    start_out, next_out, left_out, right_out, spread,
):
    far = far_down(arrived_ref, spread, expand)
    inverse = ready(inverse)
    start, low = [], []
    for b in range(BLK):
        field = (block(near_ref, b) + far[b]).astype(BF16)
        value = dot(field, inverse[b])
        start.append(value)
        low.append(value.astype(BF16))
        start_out[:, b * TILE : (b + 1) * TILE] = value
    after = []
    for b in range(BLK):
        value = start[b]
        if b > 0:
            value = value - dot(low[b - 1], lower_ref[b])
        if b < BLK - 1:
            value = value - dot(low[b + 1], upper_ref[b])
        after.append(value)
        next_out[:, b * TILE : (b + 1) * TILE] = value
    last = BLK - 1
    left_out[0] = low[0]
    left_out[1] = after[0].astype(BF16)
    left_out[2] = (start[0] - dot(after[1].astype(BF16), upper_ref[0])).astype(BF16)
    right_out[0] = low[last]
    right_out[1] = after[last].astype(BF16)
    right_out[2] = (start[last] - dot(after[last - 1].astype(BF16), lower_ref[last])).astype(BF16)


def finish_body(
    start_ref, next_ref, from_left, from_right, upper_left, lower_right, lower_ref, upper_ref,
    weight, index_rows, high_ref, low_ref, bounds_ref, send_ref, spread, hot, ordered,
):
    fill_hot(hot, low_ref[...])
    last = BLK - 1
    position = lax.axis_index("surf")
    has_left = (position > 0).astype(F32)
    has_right = (position < lax.axis_size("surf") - 1).astype(F32)
    start = [block(start_ref, b) for b in range(BLK)]
    low = [start[0].astype(BF16), start[last].astype(BF16)]
    now = [block(next_ref, b) for b in range(BLK)]
    beside_left = (from_left[1].astype(F32) - dot(low[0], upper_left[...])) * has_left
    beside_right = (from_right[1].astype(F32) - dot(low[1], lower_right[...])) * has_right
    now[0] = now[0] - dot(from_left[0], lower_ref[0]) * has_left
    now[last] = now[last] - dot(from_right[0], upper_ref[last]) * has_right

    def sweep(values, left, right):
        values = [v.astype(BF16) for v in values]
        chain = [left.astype(BF16)] + values + [right.astype(BF16)]
        return values, [
            start[b] - dot(chain[b], lower_ref[b]) - dot(chain[b + 2], upper_ref[b])
            for b in range(BLK)
        ]

    values, then = sweep(now, beside_left, beside_right)
    beside_left = (from_left[2].astype(F32) - dot(values[0], upper_left[...])) * has_left
    beside_right = (from_right[2].astype(F32) - dot(values[last], lower_right[...])) * has_right
    values, then = sweep(then, beside_left, beside_right)
    weight = ready(weight)
    rows = INC + IDX_ROWS
    for b in range(BLK):
        solved = then[b].astype(BF16).astype(F32)
        shares = solved * block(weight, b)
        every = jnp.concatenate([shares.astype(BF16), block(index_rows, b)], axis=0)
        high = high_ref[b : b + 1, :].astype(F32).astype(BF16)
        for h in range(BLK):
            spread[h * rows : (h + 1) * rows, b * TILE : (b + 1) * TILE] = jnp.where(
                high == h, every, jnp.zeros_like(every)
            )
    sorted_rows = dot(spread[...], hot[...])
    for h in range(BLK):
        ordered[:, h * TILE : (h + 1) * TILE] = sorted_rows[h * rows : (h + 1) * rows]
    owners = send_ref.shape[0]
    pieces = (send_ref.shape[1] - TAIL) // INC
    wide = (pieces + 1) * LANES
    ordered[:, NP_DEV:] = jnp.zeros((rows, ordered.shape[1] - NP_DEV), F32)
    row = iota((TAIL, LANES), 0)
    slot = iota((TAIL, LANES), 1) + (row // 2) * LANES
    for o in range(owners):
        begin = bounds_ref[o, 0]
        base = pl.multiple_of((begin // LANES) * LANES, LANES)
        piece = pltpu.roll(ordered[:, pl.ds(base, wide)], wide - (begin - base), 1)
        parts = [piece[:INC, j * LANES : (j + 1) * LANES] for j in range(pieces)]
        tail = piece[INC : INC + TAIL, :LANES]
        for j in range(1, pieces):
            tail = jnp.where(row // 2 == j, piece[INC : INC + TAIL, j * LANES : (j + 1) * LANES], tail)
        tail = jnp.where(slot >= bounds_ref[o, 1], -16.0, tail)
        send_ref[o] = jnp.concatenate(parts + [tail], axis=0).astype(BF16)


def gather_body(
    arrived_ref, compress, coupling, source, owner, place,
    field_out, out_ref, index, spread, hot, *scratch,
):
    owners, rows, _ = arrived_ref.shape
    pieces = (rows - TAIL) // INC
    for e in range(owners):
        tail = arrived_ref[e].astype(F32)[INC * pieces :]
        marks = tail.astype(BF16)
        for j in range(pieces):
            k = e * pieces + j
            part = arrived_ref[e, j * INC : (j + 1) * INC, :]
            high = marks[2 * j : 2 * j + 1]
            index[k : k + 1, :] = tail[2 * j + 1 : 2 * j + 2]
            for h in range(BLK):
                spread[h * INC : (h + 1) * INC, k * LANES : (k + 1) * LANES] = jnp.where(
                    high == h, part, jnp.zeros_like(part)
                )
    fill_hot(hot, index[...].T)
    field = dot(spread[...], hot[...]).astype(BF16)
    blocks = [field[b * INC : (b + 1) * INC] for b in range(BLK)]
    for b in range(BLK):
        field_out[b] = blocks[b]
    far_terms(blocks, compress, coupling, source, owner, place, *scratch, out_ref)


def self_body(field_ref, tiles, out_ref):
    tiles = ready(tiles)
    for b in range(BLK):
        out_ref[:, b * TILE : (b + 1) * TILE] = dot(field_ref[b], tiles[b])


def answer_body(arrived_ref, near_ref, expand, out_ref, spread):
    far = far_down(arrived_ref, spread, expand)
    for b in range(BLK):
        out_ref[:, b * TILE : (b + 1) * TILE] = (block(near_ref, b) + far[b]).astype(BF16)


def exchange(array, surf_count):
    shape = array.shape
    array = array.reshape((surf_count, shape[0] // surf_count) + shape[1:])
    array = lax.all_to_all(array, "surf", split_axis=0, concat_axis=0, tiled=True)
    return array.reshape(shape)


def shards(
    currents, near_tiles, near_target, near_source, primal_compress, primal_expand, primal_coupling,
    far_source, far_owner, far_block, gram_inverse, gram_lower, gram_upper, refine_weight,
    dual_owner, dual_index, dual_self, dual_compress, dual_expand, dual_coupling,
):
    surf_count = lax.axis_size("surf")
    tiles = far_source.shape[0]
    near_count = near_tiles.shape[0]
    targets = surf_count * BLK
    capacity = max(2, 2 * NP_DEV // surf_count)
    pieces = -(-capacity // LANES)
    to_right = [(i, (i + 1) % surf_count) for i in range(surf_count)]
    to_left = [((i + 1) % surf_count, i) for i in range(surf_count)]
    lists = (far_source.reshape(1, tiles), far_owner.reshape(1, tiles), far_block.reshape(1, tiles))
    square = ((TILE, TILE), BF16)
    cube = ((BLK, TILE, TILE), BF16)

    from_left = lax.ppermute(currents, "surf", to_right)
    from_right = lax.ppermute(currents, "surf", to_left)
    (partial,) = call(
        far_up_body,
        [((targets, INC * RANK), BF16)],
        (currents, primal_compress, primal_coupling) + lists,
        scratch=far_scratch(tiles),
        held=(2, 0, 1, 3, 4, 5),
        flops=10**11,
        name="far_up",
    )
    arrived = exchange(partial, surf_count)

    near_part, lower, upper, lower_edge, upper_edge, high, low, bounds, index_rows = call(
        prepare_body,
        [
            ((INC, NP_DEV), F32), cube, cube, square, square, ((BLK, TILE), I32),
            ((TILE, BLK), F32), ((surf_count, 2), I32), ((IDX_ROWS, NP_DEV), BF16),
        ],
        (
            near_target, near_source, currents, from_left, from_right, gram_inverse, gram_lower,
            gram_upper, dual_owner.reshape(1, NP_DEV), dual_index.reshape(1, NP_DEV), near_tiles,
        ),
        scratch=[
            pltpu.VMEM((BLK + 2, INC, TILE), BF16),
            pltpu.VMEM((BLK, INC, TILE), F32),
            pltpu.VMEM((near_count, INC, TILE), F32),
            pltpu.VMEM((BLK, TILE), F32),
            pltpu.VMEM(near_tiles.shape, BF16),
            pltpu.SemaphoreType.DMA((near_count // NEAR_CHUNK,)),
        ],
        held=(8, 9, 5, 6, 7, 2, 0, 1),
        far=(10,),
        small=(0, 1),
        kept=(0, 8),
        flops=10**11,
        name="prepare",
    )
    upper_left = lax.ppermute(upper_edge, "surf", to_right)
    lower_right = lax.ppermute(lower_edge, "surf", to_left)

    start, after, left_note, right_note = call(
        solve_body,
        [((INC, NP_DEV), F32)] * 2 + [((3, INC, TILE), BF16)] * 2,
        (arrived, near_part, primal_expand, gram_inverse, lower, upper),
        scratch=[pltpu.VMEM((BLK * INC, INC * RANK), BF16)],
        held=(2, 3),
        pinned=(1,),
        name="solve",
    )
    note_left = lax.ppermute(right_note, "surf", to_right)
    note_right = lax.ppermute(left_note, "surf", to_left)
    rows = INC + IDX_ROWS
    (send,) = call(
        finish_body,
        [((surf_count, INC * pieces + TAIL, LANES), BF16)],
        (
            start, after, note_left, note_right, upper_left, lower_right, lower, upper,
            refine_weight.reshape(1, NP_DEV), index_rows, high, low, bounds,
        ),
        scratch=[
            pltpu.VMEM((BLK * rows, NP_DEV), BF16),
            pltpu.VMEM((NP_DEV, TILE), BF16),
            pltpu.VMEM((rows, NP_DEV + (pieces + 1) * LANES), F32),
        ],
        smem=(12,),
        held=(8,),
        pinned=(9,),
        name="finish",
    )
    shares = lax.all_to_all(send, "surf", split_axis=0, concat_axis=0, tiled=True)
    slots = surf_count * pieces * LANES
    field, partial = call(
        gather_body,
        [((BLK, INC, TILE), BF16), ((targets, INC * RANK), BF16)],
        (shares, dual_compress, dual_coupling) + lists,
        scratch=[
            pltpu.VMEM((surf_count * pieces, LANES), F32),
            pltpu.VMEM((BLK * INC, slots), BF16),
            pltpu.VMEM((slots, TILE), BF16),
        ]
        + far_scratch(tiles),
        held=(2, 1, 3, 4, 5),
        name="gather",
    )
    arrived = exchange(partial, surf_count)
    (near_dual,) = call(
        self_body, [((INC, NP_DEV), F32)], (field, dual_self), held=(1,), name="self_part"
    )
    (response,) = call(
        answer_body,
        [((INC, NP_DEV), BF16)],
        (arrived, near_dual, dual_expand),
        scratch=[pltpu.VMEM((BLK * INC, INC * RANK), BF16)],
        held=(2,),
        name="answer",
    )
    return response


def solution(mesh):
    both = ("groups", "surf")
    row, flat = P(None, both), P(both)
    cube, flat2 = P(both, None, None), P(both, None)
    return jax.shard_map(
        shards,
        mesh=mesh,
        in_specs=(
            row, cube, flat, flat, cube, cube, flat2, flat, flat2, flat, cube, cube, cube, flat,
            flat2, flat, cube, cube, cube, flat2,
        ),
        out_specs=row,
        check_vma=False,
    )
```

```python
import jax
import jax.numpy as jnp
from jax import lax
from jax.experimental import pallas as pl
from jax.experimental.pallas import tpu as pltpu
from jax.sharding import PartitionSpec as P

TILE = 256
INC = 32
RANK = 32
BLK = 8
NP_DEV = 2048
LANES = 128
IDX_ROWS = 16
TAIL = 8
NEAR_CHUNK = 8
F32 = jnp.float32
BF16 = jnp.bfloat16
I32 = jnp.int32
NT = (((1,), (1,)), ((), ()))
VMEM_LIMIT = 24 * 1024 * 1024


def dot(a, b):
    return jnp.dot(a, b, preferred_element_type=F32)


def dot_nt(a, b):
    return lax.dot_general(a, b, NT, preferred_element_type=F32)


def iota(shape, dim):
    return lax.broadcasted_iota(I32, shape, dim)


def block(array, i):
    return array[:, i * TILE : (i + 1) * TILE]


def as_hot(mask):
    return mask.astype(F32).astype(BF16)


def call(body, outs, args, scratch=(), smem=(), held=(), far=(), small=(), pinned=(), kept=(), flops=0, name=None):
    spaces = [
        pltpu.SMEM if k in smem else pltpu.HBM if k in held or k in far else pltpu.VMEM
        for k in range(len(args))
    ]
    size = sum(a.size * a.dtype.itemsize for a in args)
    outs = tuple(
        pltpu.VMEM(s, d) if k in kept else jax.ShapeDtypeStruct(s, d)
        for k, (s, d) in enumerate(outs)
    )
    buffers = [
        (pltpu.SMEM if k in small else pltpu.VMEM)(args[k].shape, args[k].dtype) for k in held
    ]
    waits = [pltpu.SemaphoreType.DMA(()) for _ in held]

    def wrapped(*refs):
        ins = list(refs[: len(args)])
        rest = refs[len(args) : len(refs) - 2 * len(held)]
        extra = refs[len(refs) - 2 * len(held) :]
        for n, k in enumerate(held):
            ins[k] = pltpu.make_async_copy(ins[k], extra[n], extra[len(held) + n])
            ins[k].start()
            ins[k] = (ins[k], extra[n])
        body(*ins, *rest)

    return pl.pallas_call(
        wrapped,
        out_shape=outs,
        in_specs=[pl.BlockSpec(memory_space=m) for m in spaces],
        out_specs=tuple(pl.BlockSpec(memory_space=pltpu.VMEM) for _ in outs),
        scratch_shapes=list(scratch) + buffers + waits,
        compiler_params=pltpu.CompilerParams(vmem_limit_bytes=VMEM_LIMIT),
        cost_estimate=pl.CostEstimate(flops=flops, bytes_accessed=size, transcendentals=0),
        name=name,
    )(*[pltpu.with_memory_space_constraint(a, m) if m is pltpu.HBM or k in pinned else a for k, (a, m) in enumerate(zip(args, spaces))])


def ready(operand):
    operand[0].wait()
    return operand[1]


def fill_hot(hot, columns):
    height, count = columns.shape
    columns = columns.astype(BF16)
    lane = iota((height, TILE), 1).astype(F32).astype(BF16)
    one, zero = jnp.ones((height, TILE), BF16), jnp.zeros((height, TILE), BF16)
    for k in range(count):
        hot[k * height : (k + 1) * height, :] = jnp.where(lane == columns[:, k : k + 1], one, zero)


def far_terms(blocks, compress, coupling, source, owner, place, coef, turned, spread, pick, terms, out_ref):
    coupling = ready(coupling)
    turned[...] = coupling[...].astype(F32).T
    compress = ready(compress)
    for s in range(BLK):
        coef[:, s * RANK : (s + 1) * RANK] = dot_nt(blocks[s], compress[s])
    width = BLK * RANK
    keep = (iota((RANK, width), 1) % RANK) == iota((RANK, width), 0)
    for i in range(INC):
        spread[i * RANK : (i + 1) * RANK, :] = jnp.where(keep, coef[i : i + 1, :], 0.0).astype(BF16)
    source = ready(source)
    tiles = source.shape[1]
    pick[...] = dot(spread[...], as_hot((iota((width, tiles), 0) // RANK) == source[...]))

    def step(pair, carry):
        rows = pl.multiple_of(pair * (2 * RANK), 2 * RANK)
        got = pick[pl.ds(rows, 2 * RANK), :]
        first = jnp.zeros((RANK, tiles), F32)
        second = jnp.zeros((RANK, tiles), F32)
        for r in range(RANK):
            factor = turned[r * RANK : (r + 1) * RANK, :]
            first += got[r : r + 1, :] * factor
            second += got[RANK + r : RANK + r + 1, :] * factor
        terms[pl.ds(rows, 2 * RANK), :] = jnp.concatenate([first, second], axis=0).astype(BF16)
        return carry

    lax.fori_loop(0, INC // 2, step, 0)
    targets = out_ref.shape[0]
    owner, place = ready(owner), ready(place)
    select = as_hot(iota((targets, tiles), 0) == owner[...] * BLK + place[...])
    out_ref[...] = dot_nt(select, terms[...]).astype(BF16)


def far_scratch(tiles):
    return [
        pltpu.VMEM((INC, BLK * RANK), F32),
        pltpu.VMEM((RANK * RANK, tiles), F32),
        pltpu.VMEM((INC * RANK, BLK * RANK), BF16),
        pltpu.VMEM((INC * RANK, tiles), F32),
        pltpu.VMEM((INC * RANK, tiles), BF16),
    ]


def far_up_body(value, compress, coupling, source, owner, place, out_ref, *scratch):
    value = ready(value)
    blocks = [block(value, s) for s in range(BLK)]
    far_terms(blocks, compress, coupling, source, owner, place, *scratch, out_ref)


def far_down(arrived_ref, spread, expand):
    rows = arrived_ref.shape[0]
    total = jnp.sum(arrived_ref[...].astype(F32).reshape(rows // BLK, BLK, INC * RANK), axis=0)
    width = INC * RANK
    keep = (iota((INC, width), 1) // RANK) == iota((INC, width), 0)
    for b in range(BLK):
        spread[b * INC : (b + 1) * INC, :] = jnp.where(keep, total[b : b + 1, :], 0.0).astype(BF16)
    fold = as_hot((iota((width, RANK), 0) % RANK) == iota((width, RANK), 1))
    sums = dot(spread[...], fold).astype(BF16)
    expand = ready(expand)
    return [dot(sums[b * INC : (b + 1) * INC, :], expand[b]) for b in range(BLK)]


def order(owner, index, ranks, owners, window, high_out, low_out, bounds_out, rows_out):
    before = as_hot(iota((TILE, TILE), 0) < iota((TILE, TILE), 1))
    number = iota((owners, TILE), 0)
    count = jnp.zeros((owners, 1), F32)
    begin = jnp.zeros((owners, 1), F32)
    hots, carries = [], []
    for c in range(BLK):
        names = block(owner, c)
        hot = (number == names).astype(F32)
        hots.append(hot)
        carries.append(count)
        count = count + jnp.sum(hot, axis=1, keepdims=True)
        begin = begin + jnp.sum((names < number).astype(F32), axis=1, keepdims=True)
    for c in range(BLK):
        rank = dot(hots[c].astype(BF16), before)
        ranks[c : c + 1, :] = jnp.sum(hots[c] * (rank + carries[c] + begin), axis=0, keepdims=True)
    spots = ranks[...].astype(I32)
    high_out[...] = spots // TILE
    low_out[...] = (spots % TILE).astype(F32).T
    pair = iota((owners, 2), 1)
    bounds_out[...] = jnp.where(pair == 0, begin, count).astype(I32)
    row = iota((IDX_ROWS, NP_DEV), 0)
    index = index[...]
    digits = jnp.where(row % 2 == 0, index // TILE, index % TILE)
    rows_out[...] = jnp.where(row < 2 * (window // LANES), digits, 0).astype(F32).astype(BF16)


def prepare_body(
    target, origin, own, inner, outer, inverse, lower, upper, owner, index, tiles_ref,
    near_out, lower_out, upper_out, inner_edge, outer_edge, high_out, low_out, bounds_out, rows_out,
    cells, total, products, ranks, tiles, arrivals,
):
    count = tiles_ref.shape[0]
    copies = []
    for c in range(count // NEAR_CHUNK):
        part = pl.ds(c * NEAR_CHUNK, NEAR_CHUNK)
        copy = pltpu.make_async_copy(tiles_ref.at[part], tiles.at[part], arrivals.at[c])
        copy.start()
        copies.append(copy)
    owner, index = ready(owner), ready(index)
    window = max(LANES, -(-(2 * NP_DEV // bounds_out.shape[0]) // LANES) * LANES)
    order(owner, index, ranks, bounds_out.shape[0], window, high_out, low_out, bounds_out, rows_out)
    inverse, lower, upper = ready(inverse), ready(lower), ready(upper)
    for b in range(BLK):
        lower_out[b] = dot(lower[b], inverse[b]).astype(BF16)
        upper_out[b] = dot(upper[b], inverse[b]).astype(BF16)
    position = lax.axis_index("surf")
    even = position % 2 == 0

    @pl.when(even)
    def _():
        inner_edge[...] = upper_out[BLK - 1]
        outer_edge[...] = lower_out[0]
        cells[0] = block(outer, BLK - 1)
        cells[BLK + 1] = block(inner, 0)

    @pl.when(jnp.logical_not(even))
    def _():
        inner_edge[...] = lower_out[0]
        outer_edge[...] = upper_out[BLK - 1]
        cells[0] = block(inner, BLK - 1)
        cells[BLK + 1] = block(outer, 0)

    own = ready(own)
    for b in range(BLK):
        cells[b + 1] = block(own, b)
    total[...] = jnp.zeros_like(total)
    target, origin = ready(target), ready(origin)
    start = position * BLK - 1
    for c, copy in enumerate(copies):
        copy.wait()
        for k in range(c * NEAR_CHUNK, (c + 1) * NEAR_CHUNK):
            products[k] = dot(cells[origin[k] - start], tiles[k])
    for k in range(count):
        total[target[k]] += products[k]
    for b in range(BLK):
        near_out[:, b * TILE : (b + 1) * TILE] = total[b]


def solve_body(
    arrived_ref, near_ref, expand, inverse, lower_ref, upper_ref,
    start_out, next_out, inner_out, outer_out, notes, spread,
):
    far = far_down(arrived_ref, spread, expand)
    inverse = ready(inverse)
    start, low = [], []
    for b in range(BLK):
        field = (block(near_ref, b) + far[b]).astype(BF16)
        value = dot(field, inverse[b])
        start.append(value)
        low.append(value.astype(BF16))
        start_out[:, b * TILE : (b + 1) * TILE] = value
    after = []
    for b in range(BLK):
        value = start[b]
        if b > 0:
            value = value - dot(low[b - 1], lower_ref[b])
        if b < BLK - 1:
            value = value - dot(low[b + 1], upper_ref[b])
        after.append(value)
        next_out[:, b * TILE : (b + 1) * TILE] = value
    last = BLK - 1
    odd = lax.axis_index("surf") % 2
    notes[0, 0] = low[last]
    notes[0, 1] = after[last].astype(BF16)
    notes[0, 2] = (start[last] - dot(after[last - 1].astype(BF16), lower_ref[last])).astype(BF16)
    notes[1, 0] = low[0]
    notes[1, 1] = after[0].astype(BF16)
    notes[1, 2] = (start[0] - dot(after[1].astype(BF16), upper_ref[0])).astype(BF16)
    inner_out[...] = notes[odd]
    outer_out[...] = notes[1 - odd]


def finish_body(
    start_ref, next_ref, inner_note, outer_note, inner_edge, outer_edge, lower_ref, upper_ref,
    weight, index_rows, high_ref, low_ref, bounds_ref, send_ref,
    notes, edges, spread, hot, ordered,
):
    fill_hot(hot, low_ref[...])
    last = BLK - 1
    position = lax.axis_index("surf")
    odd = position % 2
    notes[0] = inner_note[...]
    notes[1] = outer_note[...]
    edges[0] = inner_edge[...]
    edges[1] = outer_edge[...]
    from_left, from_right = notes.at[1 - odd], notes.at[odd]
    upper_left, lower_right = edges.at[1 - odd], edges.at[odd]
    has_left = (position > 0).astype(F32)
    has_right = (position < lax.axis_size("surf") - 1).astype(F32)
    start = [block(start_ref, b) for b in range(BLK)]
    low = [start[0].astype(BF16), start[last].astype(BF16)]
    now = [block(next_ref, b) for b in range(BLK)]
    beside_left = (from_left[1].astype(F32) - dot(low[0], upper_left[...])) * has_left
    beside_right = (from_right[1].astype(F32) - dot(low[1], lower_right[...])) * has_right
    now[0] = now[0] - dot(from_left[0], lower_ref[0]) * has_left
    now[last] = now[last] - dot(from_right[0], upper_ref[last]) * has_right

    def sweep(values, left, right):
        values = [v.astype(BF16) for v in values]
        chain = [left.astype(BF16)] + values + [right.astype(BF16)]
        return values, [
            start[b] - dot(chain[b], lower_ref[b]) - dot(chain[b + 2], upper_ref[b])
            for b in range(BLK)
        ]

    values, then = sweep(now, beside_left, beside_right)
    beside_left = (from_left[2].astype(F32) - dot(values[0], upper_left[...])) * has_left
    beside_right = (from_right[2].astype(F32) - dot(values[last], lower_right[...])) * has_right
    values, then = sweep(then, beside_left, beside_right)
    weight = ready(weight)
    rows = INC + IDX_ROWS
    for b in range(BLK):
        solved = then[b].astype(BF16).astype(F32)
        shares = solved * block(weight, b)
        every = jnp.concatenate([shares.astype(BF16), block(index_rows, b)], axis=0)
        high = high_ref[b : b + 1, :].astype(F32).astype(BF16)
        for h in range(BLK):
            spread[h * rows : (h + 1) * rows, b * TILE : (b + 1) * TILE] = jnp.where(
                high == h, every, jnp.zeros_like(every)
            )
    sorted_rows = dot(spread[...], hot[...])
    for h in range(BLK):
        ordered[:, h * TILE : (h + 1) * TILE] = sorted_rows[h * rows : (h + 1) * rows]
    owners = send_ref.shape[0]
    pieces = (send_ref.shape[1] - TAIL) // INC
    wide = (pieces + 1) * LANES
    ordered[:, NP_DEV:] = jnp.zeros((rows, ordered.shape[1] - NP_DEV), F32)
    row = iota((TAIL, LANES), 0)
    slot = iota((TAIL, LANES), 1) + (row // 2) * LANES
    for o in range(owners):
        begin = bounds_ref[o, 0]
        base = pl.multiple_of((begin // LANES) * LANES, LANES)
        piece = pltpu.roll(ordered[:, pl.ds(base, wide)], wide - (begin - base), 1)
        parts = [piece[:INC, j * LANES : (j + 1) * LANES] for j in range(pieces)]
        tail = piece[INC : INC + TAIL, :LANES]
        for j in range(1, pieces):
            tail = jnp.where(row // 2 == j, piece[INC : INC + TAIL, j * LANES : (j + 1) * LANES], tail)
        tail = jnp.where(slot >= bounds_ref[o, 1], -16.0, tail)
        send_ref[o] = jnp.concatenate(parts + [tail], axis=0).astype(BF16)


def gather_body(
    arrived_ref, compress, coupling, source, owner, place,
    field_out, out_ref, index, spread, hot, *scratch,
):
    owners, rows, _ = arrived_ref.shape
    pieces = (rows - TAIL) // INC
    for e in range(owners):
        tail = arrived_ref[e].astype(F32)[INC * pieces :]
        marks = tail.astype(BF16)
        for j in range(pieces):
            k = e * pieces + j
            part = arrived_ref[e, j * INC : (j + 1) * INC, :]
            high = marks[2 * j : 2 * j + 1]
            index[k : k + 1, :] = tail[2 * j + 1 : 2 * j + 2]
            for h in range(BLK):
                spread[h * INC : (h + 1) * INC, k * LANES : (k + 1) * LANES] = jnp.where(
                    high == h, part, jnp.zeros_like(part)
                )
    fill_hot(hot, index[...].T)
    field = dot(spread[...], hot[...]).astype(BF16)
    blocks = [field[b * INC : (b + 1) * INC] for b in range(BLK)]
    for b in range(BLK):
        field_out[b] = blocks[b]
    far_terms(blocks, compress, coupling, source, owner, place, *scratch, out_ref)


def self_body(field_ref, tiles, out_ref):
    tiles = ready(tiles)
    for b in range(BLK):
        out_ref[:, b * TILE : (b + 1) * TILE] = dot(field_ref[b], tiles[b])


def answer_body(arrived_ref, near_ref, expand, out_ref, spread):
    far = far_down(arrived_ref, spread, expand)
    for b in range(BLK):
        out_ref[:, b * TILE : (b + 1) * TILE] = (block(near_ref, b) + far[b]).astype(BF16)


def swap(inner, outer, surf_count):
    pairs = [(i, i ^ 1) for i in range(surf_count)]
    others = [(0, 0), (surf_count - 1, surf_count - 1)]
    for i in range(1, surf_count - 1, 2):
        others += [(i, i + 1), (i + 1, i)]
    return lax.ppermute(inner, "surf", pairs), lax.ppermute(outer, "surf", others)


def exchange(array, surf_count):
    shape = array.shape
    array = array.reshape((surf_count, shape[0] // surf_count) + shape[1:])
    array = lax.all_to_all(array, "surf", split_axis=0, concat_axis=0, tiled=True)
    return array.reshape(shape)


def shards(
    currents, near_tiles, near_target, near_source, primal_compress, primal_expand, primal_coupling,
    far_source, far_owner, far_block, gram_inverse, gram_lower, gram_upper, refine_weight,
    dual_owner, dual_index, dual_self, dual_compress, dual_expand, dual_coupling,
):
    surf_count = lax.axis_size("surf")
    tiles = far_source.shape[0]
    near_count = near_tiles.shape[0]
    targets = surf_count * BLK
    capacity = max(2, 2 * NP_DEV // surf_count)
    pieces = -(-capacity // LANES)
    lists = (far_source.reshape(1, tiles), far_owner.reshape(1, tiles), far_block.reshape(1, tiles))
    square = ((TILE, TILE), BF16)
    cube = ((BLK, TILE, TILE), BF16)

    inner, outer = swap(currents, currents, surf_count)
    (partial,) = call(
        far_up_body,
        [((targets, INC * RANK), BF16)],
        (currents, primal_compress, primal_coupling) + lists,
        scratch=far_scratch(tiles),
        held=(2, 0, 1, 3, 4, 5),
        flops=10**11,
        name="far_up",
    )
    arrived = exchange(partial, surf_count)

    near_part, lower, upper, inner_edge, outer_edge, high, low, bounds, index_rows = call(
        prepare_body,
        [
            ((INC, NP_DEV), F32), cube, cube, square, square, ((BLK, TILE), I32),
            ((TILE, BLK), F32), ((surf_count, 2), I32), ((IDX_ROWS, NP_DEV), BF16),
        ],
        (
            near_target, near_source, currents, inner, outer, gram_inverse, gram_lower,
            gram_upper, dual_owner.reshape(1, NP_DEV), dual_index.reshape(1, NP_DEV), near_tiles,
        ),
        scratch=[
            pltpu.VMEM((BLK + 2, INC, TILE), BF16),
            pltpu.VMEM((BLK, INC, TILE), F32),
            pltpu.VMEM((near_count, INC, TILE), F32),
            pltpu.VMEM((BLK, TILE), F32),
            pltpu.VMEM(near_tiles.shape, BF16),
            pltpu.SemaphoreType.DMA((near_count // NEAR_CHUNK,)),
        ],
        held=(8, 9, 5, 6, 7, 2, 0, 1),
        far=(10,),
        small=(0, 1),
        kept=(0, 8),
        flops=10**11,
        name="prepare",
    )
    inner_edge, outer_edge = swap(inner_edge, outer_edge, surf_count)

    start, after, inner_note, outer_note = call(
        solve_body,
        [((INC, NP_DEV), F32)] * 2 + [((3, INC, TILE), BF16)] * 2,
        (arrived, near_part, primal_expand, gram_inverse, lower, upper),
        scratch=[
            pltpu.VMEM((2, 3, INC, TILE), BF16),
            pltpu.VMEM((BLK * INC, INC * RANK), BF16),
        ],
        held=(2, 3),
        pinned=(1,),
        name="solve",
    )
    inner_note, outer_note = swap(inner_note, outer_note, surf_count)
    rows = INC + IDX_ROWS
    (send,) = call(
        finish_body,
        [((surf_count, INC * pieces + TAIL, LANES), BF16)],
        (
            start, after, inner_note, outer_note, inner_edge, outer_edge, lower, upper,
            refine_weight.reshape(1, NP_DEV), index_rows, high, low, bounds,
        ),
        scratch=[
            pltpu.VMEM((2, 3, INC, TILE), BF16),
            pltpu.VMEM((2, TILE, TILE), BF16),
            pltpu.VMEM((BLK * rows, NP_DEV), BF16),
            pltpu.VMEM((NP_DEV, TILE), BF16),
            pltpu.VMEM((rows, NP_DEV + (pieces + 1) * LANES), F32),
        ],
        smem=(12,),
        held=(8,),
        pinned=(9,),
        name="finish",
    )
    shares = lax.all_to_all(send, "surf", split_axis=0, concat_axis=0, tiled=True)
    slots = surf_count * pieces * LANES
    field, partial = call(
        gather_body,
        [((BLK, INC, TILE), BF16), ((targets, INC * RANK), BF16)],
        (shares, dual_compress, dual_coupling) + lists,
        scratch=[
            pltpu.VMEM((surf_count * pieces, LANES), F32),
            pltpu.VMEM((BLK * INC, slots), BF16),
            pltpu.VMEM((slots, TILE), BF16),
        ]
        + far_scratch(tiles),
        held=(2, 1, 3, 4, 5),
        name="gather",
    )
    arrived = exchange(partial, surf_count)
    (near_dual,) = call(
        self_body, [((INC, NP_DEV), F32)], (field, dual_self), held=(1,), name="self_part"
    )
    (response,) = call(
        answer_body,
        [((INC, NP_DEV), BF16)],
        (arrived, near_dual, dual_expand),
        scratch=[pltpu.VMEM((BLK * INC, INC * RANK), BF16)],
        held=(2,),
        name="answer",
    )
    return response


def solution(mesh):
    both = ("groups", "surf")
    row, flat = P(None, both), P(both)
    cube, flat2 = P(both, None, None), P(both, None)
    return jax.shard_map(
        shards,
        mesh=mesh,
        in_specs=(
            row, cube, flat, flat, cube, cube, flat2, flat, flat2, flat, cube, cube, cube, flat,
            flat2, flat, cube, cube, cube, flat2,
        ),
        out_specs=row,
        check_vma=False,
    )
```

```python
import jax
import jax.numpy as jnp
from jax import lax
from jax.experimental import pallas as pl
from jax.experimental.pallas import tpu as pltpu
from jax.sharding import PartitionSpec as P

TILE = 256
INC = 32
RANK = 32
BLK = 8
NP_DEV = 2048
LANES = 128
IDX_ROWS = 16
TAIL = 8
NEAR_CHUNK = 8
F32 = jnp.float32
BF16 = jnp.bfloat16
I32 = jnp.int32
NT = (((1,), (1,)), ((), ()))
VMEM_LIMIT = 36 * 1024 * 1024


def dot(a, b):
    return jnp.dot(a, b, preferred_element_type=F32)


def dot_nt(a, b):
    return lax.dot_general(a, b, NT, preferred_element_type=F32)


def iota(shape, dim):
    return lax.broadcasted_iota(I32, shape, dim)


def block(array, i):
    return array[:, i * TILE : (i + 1) * TILE]


def as_hot(mask):
    return mask.astype(F32).astype(BF16)


def call(body, outs, args, scratch=(), smem=(), held=(), far=(), small=(), pinned=(), kept=(), flops=0, name=None):
    spaces = [
        pltpu.SMEM if k in smem else pltpu.HBM if k in held or k in far else pltpu.VMEM
        for k in range(len(args))
    ]
    size = sum(a.size * a.dtype.itemsize for a in args)
    outs = tuple(
        pltpu.VMEM(s, d) if k in kept else jax.ShapeDtypeStruct(s, d)
        for k, (s, d) in enumerate(outs)
    )
    buffers = [
        (pltpu.SMEM if k in small else pltpu.VMEM)(args[k].shape, args[k].dtype) for k in held
    ]
    waits = [pltpu.SemaphoreType.DMA(()) for _ in held]

    def wrapped(*refs):
        ins = list(refs[: len(args)])
        rest = refs[len(args) : len(refs) - 2 * len(held)]
        extra = refs[len(refs) - 2 * len(held) :]
        for n, k in enumerate(held):
            ins[k] = pltpu.make_async_copy(ins[k], extra[n], extra[len(held) + n])
            ins[k].start()
            ins[k] = (ins[k], extra[n])
        body(*ins, *rest)

    return pl.pallas_call(
        wrapped,
        out_shape=outs,
        in_specs=[pl.BlockSpec(memory_space=m) for m in spaces],
        out_specs=tuple(pl.BlockSpec(memory_space=pltpu.VMEM) for _ in outs),
        scratch_shapes=list(scratch) + buffers + waits,
        compiler_params=pltpu.CompilerParams(vmem_limit_bytes=VMEM_LIMIT),
        cost_estimate=pl.CostEstimate(flops=flops, bytes_accessed=size, transcendentals=0),
        name=name,
    )(*[pltpu.with_memory_space_constraint(a, m) if m is pltpu.HBM or k in pinned else a for k, (a, m) in enumerate(zip(args, spaces))])


def ready(operand):
    operand[0].wait()
    return operand[1]


def fill_hot(hot, columns):
    height, count = columns.shape
    columns = columns.astype(BF16)
    lane = iota((height, TILE), 1).astype(F32).astype(BF16)
    one, zero = jnp.ones((height, TILE), BF16), jnp.zeros((height, TILE), BF16)
    for k in range(count):
        hot[k * height : (k + 1) * height, :] = jnp.where(lane == columns[:, k : k + 1], one, zero)


def coefficients(blocks, compress):
    width = BLK * RANK
    every = dot_nt(blocks, compress[...].reshape(width, TILE))
    owner = iota((INC, width), 1) // RANK
    coef = jnp.zeros((INC, width), F32)
    for s in range(BLK):
        coef = jnp.where(owner == s, every[s * INC : (s + 1) * INC], coef)
    return coef


def far_up_body(value, compress, coupling, source, owner, place, out_ref, blocks, turned, spread, pick, terms):
    coupling = ready(coupling)
    turned[...] = coupling[...].astype(F32).T
    value, compress = ready(value), ready(compress)
    for s in range(BLK):
        blocks[s * INC : (s + 1) * INC, :] = block(value, s)
    coef = coefficients(blocks[...], compress)
    width = BLK * RANK
    keep = (iota((RANK, width), 1) % RANK) == iota((RANK, width), 0)
    for i in range(INC):
        spread[i * RANK : (i + 1) * RANK, :] = jnp.where(keep, coef[i : i + 1, :], 0.0).astype(BF16)
    source = ready(source)
    tiles = source.shape[1]
    pick[...] = dot(spread[...], as_hot((iota((width, tiles), 0) // RANK) == source[...]))

    def step(pair, carry):
        rows = pl.multiple_of(pair * (2 * RANK), 2 * RANK)
        got = pick[pl.ds(rows, 2 * RANK), :]
        first = jnp.zeros((RANK, tiles), F32)
        second = jnp.zeros((RANK, tiles), F32)
        for r in range(RANK):
            factor = turned[r * RANK : (r + 1) * RANK, :]
            first += got[r : r + 1, :] * factor
            second += got[RANK + r : RANK + r + 1, :] * factor
        terms[pl.ds(rows, 2 * RANK), :] = jnp.concatenate([first, second], axis=0).astype(BF16)
        return carry

    lax.fori_loop(0, INC // 2, step, 0)
    targets = out_ref.shape[0]
    owner, place = ready(owner), ready(place)
    select = as_hot(iota((targets, tiles), 0) == owner[...] * BLK + place[...])
    out_ref[...] = dot_nt(select, terms[...]).astype(BF16)


def far_scratch(tiles):
    return [
        pltpu.VMEM((BLK * INC, TILE), BF16),
        pltpu.VMEM((RANK * RANK, tiles), F32),
        pltpu.VMEM((INC * RANK, BLK * RANK), BF16),
        pltpu.VMEM((INC * RANK, tiles), F32),
        pltpu.VMEM((INC * RANK, tiles), BF16),
    ]


def far_down(arrived_ref, spread, expand):
    rows = arrived_ref.shape[0]
    total = jnp.sum(arrived_ref[...].astype(F32).reshape(rows // BLK, BLK, INC * RANK), axis=0)
    width = INC * RANK
    keep = (iota((INC, width), 1) // RANK) == iota((INC, width), 0)
    for b in range(BLK):
        spread[b * INC : (b + 1) * INC, :] = jnp.where(keep, total[b : b + 1, :], 0.0).astype(BF16)
    fold = as_hot((iota((width, RANK), 0) % RANK) == iota((width, RANK), 1))
    sums = dot(spread[...], fold).astype(BF16)
    expand = ready(expand)
    return [dot(sums[b * INC : (b + 1) * INC, :], expand[b]) for b in range(BLK)]


def order(owner, index, ranks, owners, window, high_out, low_out, bounds_out, rows_out):
    before = as_hot(iota((TILE, TILE), 0) < iota((TILE, TILE), 1))
    number = iota((owners, TILE), 0)
    count = jnp.zeros((owners, 1), F32)
    begin = jnp.zeros((owners, 1), F32)
    hots, carries = [], []
    for c in range(BLK):
        names = block(owner, c)
        hot = (number == names).astype(F32)
        hots.append(hot)
        carries.append(count)
        count = count + jnp.sum(hot, axis=1, keepdims=True)
        begin = begin + jnp.sum((names < number).astype(F32), axis=1, keepdims=True)
    for c in range(BLK):
        rank = dot(hots[c].astype(BF16), before)
        ranks[c : c + 1, :] = jnp.sum(hots[c] * (rank + carries[c] + begin), axis=0, keepdims=True)
    spots = ranks[...].astype(I32)
    high_out[...] = spots // TILE
    low_out[...] = (spots % TILE).astype(F32).T
    pair = iota((owners, 2), 1)
    bounds_out[...] = jnp.where(pair == 0, begin, count).astype(I32)
    row = iota((IDX_ROWS, NP_DEV), 0)
    index = index[...]
    digits = jnp.where(row % 2 == 0, index // TILE, index % TILE)
    rows_out[...] = jnp.where(row < 2 * (window // LANES), digits, 0).astype(F32).astype(BF16)


def prepare_body(
    target, origin, own, inner, outer, inverse, lower, upper, owner, index, tiles_ref,
    near_out, lower_out, upper_out, inner_edge, outer_edge, high_out, low_out, bounds_out, rows_out,
    cells, total, products, ranks, tiles, arrivals,
):
    count = tiles_ref.shape[0]
    copies = []
    for c in range(count // NEAR_CHUNK):
        part = pl.ds(c * NEAR_CHUNK, NEAR_CHUNK)
        copy = pltpu.make_async_copy(tiles_ref.at[part], tiles.at[part], arrivals.at[c])
        copy.start()
        copies.append(copy)
    owner, index = ready(owner), ready(index)
    window = max(LANES, -(-(2 * NP_DEV // bounds_out.shape[0]) // LANES) * LANES)
    order(owner, index, ranks, bounds_out.shape[0], window, high_out, low_out, bounds_out, rows_out)
    inverse, lower, upper = ready(inverse), ready(lower), ready(upper)
    for b in range(BLK):
        lower_out[b] = dot(lower[b], inverse[b]).astype(BF16)
        upper_out[b] = dot(upper[b], inverse[b]).astype(BF16)
    position = lax.axis_index("surf")
    even = position % 2 == 0

    @pl.when(even)
    def _():
        inner_edge[...] = upper_out[BLK - 1]
        outer_edge[...] = lower_out[0]
        cells[0] = block(outer, BLK - 1)
        cells[BLK + 1] = block(inner, 0)

    @pl.when(jnp.logical_not(even))
    def _():
        inner_edge[...] = lower_out[0]
        outer_edge[...] = upper_out[BLK - 1]
        cells[0] = block(inner, BLK - 1)
        cells[BLK + 1] = block(outer, 0)

    own = ready(own)
    for b in range(BLK):
        cells[b + 1] = block(own, b)
    total[...] = jnp.zeros_like(total)
    target, origin = ready(target), ready(origin)
    start = position * BLK - 1
    for c, copy in enumerate(copies):
        copy.wait()
        for k in range(c * NEAR_CHUNK, (c + 1) * NEAR_CHUNK):
            products[k] = dot(cells[origin[k] - start], tiles[k])
    for k in range(count):
        total[target[k]] += products[k]
    for b in range(BLK):
        near_out[:, b * TILE : (b + 1) * TILE] = total[b]


def solve_body(
    arrived_ref, near_ref, expand, inverse, lower_ref, upper_ref,
    start_out, next_out, inner_out, outer_out, notes, spread,
):
    far = far_down(arrived_ref, spread, expand)
    inverse = ready(inverse)
    start, low = [], []
    for b in range(BLK):
        field = (block(near_ref, b) + far[b]).astype(BF16)
        value = dot(field, inverse[b])
        start.append(value)
        low.append(value.astype(BF16))
        start_out[:, b * TILE : (b + 1) * TILE] = value
    after = []
    for b in range(BLK):
        value = start[b]
        if b > 0:
            value = value - dot(low[b - 1], lower_ref[b])
        if b < BLK - 1:
            value = value - dot(low[b + 1], upper_ref[b])
        after.append(value)
        next_out[:, b * TILE : (b + 1) * TILE] = value
    last = BLK - 1
    odd = lax.axis_index("surf") % 2
    notes[0, 0] = low[last]
    notes[0, 1] = after[last].astype(BF16)
    notes[0, 2] = (start[last] - dot(after[last - 1].astype(BF16), lower_ref[last])).astype(BF16)
    notes[1, 0] = low[0]
    notes[1, 1] = after[0].astype(BF16)
    notes[1, 2] = (start[0] - dot(after[1].astype(BF16), upper_ref[0])).astype(BF16)
    inner_out[...] = notes[odd]
    outer_out[...] = notes[1 - odd]


def finish_body(
    start_ref, next_ref, inner_note, outer_note, inner_edge, outer_edge, lower_ref, upper_ref,
    weight, index_rows, high_ref, low_ref, bounds_ref, send_ref,
    notes, edges, spread, hot, ordered,
):
    fill_hot(hot, low_ref[...])
    last = BLK - 1
    position = lax.axis_index("surf")
    odd = position % 2
    notes[0] = inner_note[...]
    notes[1] = outer_note[...]
    edges[0] = inner_edge[...]
    edges[1] = outer_edge[...]
    from_left, from_right = notes.at[1 - odd], notes.at[odd]
    upper_left, lower_right = edges.at[1 - odd], edges.at[odd]
    has_left = (position > 0).astype(F32)
    has_right = (position < lax.axis_size("surf") - 1).astype(F32)
    start = [block(start_ref, b) for b in range(BLK)]
    low = [start[0].astype(BF16), start[last].astype(BF16)]
    now = [block(next_ref, b) for b in range(BLK)]
    beside_left = (from_left[1].astype(F32) - dot(low[0], upper_left[...])) * has_left
    beside_right = (from_right[1].astype(F32) - dot(low[1], lower_right[...])) * has_right
    now[0] = now[0] - dot(from_left[0], lower_ref[0]) * has_left
    now[last] = now[last] - dot(from_right[0], upper_ref[last]) * has_right

    def sweep(values, left, right):
        values = [v.astype(BF16) for v in values]
        chain = [left.astype(BF16)] + values + [right.astype(BF16)]
        return values, [
            start[b] - dot(chain[b], lower_ref[b]) - dot(chain[b + 2], upper_ref[b])
            for b in range(BLK)
        ]

    values, then = sweep(now, beside_left, beside_right)
    beside_left = (from_left[2].astype(F32) - dot(values[0], upper_left[...])) * has_left
    beside_right = (from_right[2].astype(F32) - dot(values[last], lower_right[...])) * has_right
    values, then = sweep(then, beside_left, beside_right)
    weight = ready(weight)
    rows = INC + IDX_ROWS
    for b in range(BLK):
        solved = then[b].astype(BF16).astype(F32)
        shares = solved * block(weight, b)
        every = jnp.concatenate([shares.astype(BF16), block(index_rows, b)], axis=0)
        high = high_ref[b : b + 1, :].astype(F32).astype(BF16)
        for h in range(BLK):
            spread[h * rows : (h + 1) * rows, b * TILE : (b + 1) * TILE] = jnp.where(
                high == h, every, jnp.zeros_like(every)
            )
    sorted_rows = dot(spread[...], hot[...])
    for h in range(BLK):
        ordered[:, h * TILE : (h + 1) * TILE] = sorted_rows[h * rows : (h + 1) * rows]
    owners = send_ref.shape[0]
    pieces = (send_ref.shape[1] - TAIL) // INC
    wide = (pieces + 1) * LANES
    ordered[:, NP_DEV:] = jnp.zeros((rows, ordered.shape[1] - NP_DEV), F32)
    row = iota((TAIL, LANES), 0)
    slot = iota((TAIL, LANES), 1) + (row // 2) * LANES
    for o in range(owners):
        begin = bounds_ref[o, 0]
        base = pl.multiple_of((begin // LANES) * LANES, LANES)
        piece = pltpu.roll(ordered[:, pl.ds(base, wide)], wide - (begin - base), 1)
        parts = [piece[:INC, j * LANES : (j + 1) * LANES] for j in range(pieces)]
        tail = piece[INC : INC + TAIL, :LANES]
        for j in range(1, pieces):
            tail = jnp.where(row // 2 == j, piece[INC : INC + TAIL, j * LANES : (j + 1) * LANES], tail)
        tail = jnp.where(slot >= bounds_ref[o, 1], -16.0, tail)
        send_ref[o] = jnp.concatenate(parts + [tail], axis=0).astype(BF16)


def gather_body(
    arrived_ref, compress, couple_ref, field_out, out_ref, index, spread, hot,
):
    owners, rows, _ = arrived_ref.shape
    pieces = (rows - TAIL) // INC
    for e in range(owners):
        tail = arrived_ref[e].astype(F32)[INC * pieces :]
        marks = tail.astype(BF16)
        for j in range(pieces):
            k = e * pieces + j
            part = arrived_ref[e, j * INC : (j + 1) * INC, :]
            high = marks[2 * j : 2 * j + 1]
            index[k : k + 1, :] = tail[2 * j + 1 : 2 * j + 2]
            for h in range(BLK):
                spread[h * INC : (h + 1) * INC, k * LANES : (k + 1) * LANES] = jnp.where(
                    high == h, part, jnp.zeros_like(part)
                )
    fill_hot(hot, index[...].T)
    field = dot(spread[...], hot[...]).astype(BF16)
    for b in range(BLK):
        field_out[b] = field[b * INC : (b + 1) * INC]
    coef = coefficients(field, ready(compress)).astype(BF16)
    for o in range(out_ref.shape[0]):
        out_ref[o] = dot(coef, block(couple_ref, o)).astype(BF16)


def couple_body(coupling, source, owner, place, out_ref, total, lanes):
    tiles, width = lanes.shape[0], BLK * RANK
    flat = RANK * RANK
    total[...] = jnp.zeros_like(total)
    coupling = ready(coupling)
    lanes[...] = coupling[...].astype(F32)
    keep = (iota((RANK, flat), 1) % RANK) == iota((RANK, flat), 0)
    fold = as_hot((iota((flat, width), 0) // RANK) == (iota((flat, width), 1) % RANK))
    number = iota((RANK, width), 1) // RANK
    source, owner, place = ready(source), ready(owner), ready(place)
    group = 8

    def step(c, carry):
        begin = pl.multiple_of(c * group, group)
        rows = lanes[pl.ds(begin, group), :]
        tall = [jnp.where(keep, rows[k : k + 1], 0.0).astype(BF16) for k in range(group)]
        turned = dot(jnp.concatenate(tall, axis=0), fold)
        for k in range(group):
            f = begin + k
            tile = jnp.where(number == source[0, f], turned[k * RANK : (k + 1) * RANK], 0.0)
            total[owner[0, f] * BLK + place[0, f]] += tile
        return carry

    lax.fori_loop(0, tiles // group, step, 0)
    for o in range(out_ref.shape[1] // TILE):
        part = total[o * BLK : (o + 1) * BLK].reshape(TILE, width)
        out_ref[:, o * TILE : (o + 1) * TILE] = part.T.astype(BF16)


def self_body(field_ref, tiles, out_ref):
    tiles = ready(tiles)
    for b in range(BLK):
        out_ref[:, b * TILE : (b + 1) * TILE] = dot(field_ref[b], tiles[b])


def answer_body(arrived_ref, near_ref, expand, out_ref, spread):
    total = jnp.sum(arrived_ref[...].astype(F32), axis=0)
    number = iota(total.shape, 1) // RANK
    for b in range(BLK):
        spread[b * INC : (b + 1) * INC, :] = jnp.where(number == b, total, 0.0).astype(BF16)
    far = dot(spread[...], ready(expand)[...].reshape(BLK * RANK, TILE))
    for b in range(BLK):
        out_ref[:, b * TILE : (b + 1) * TILE] = (
            block(near_ref, b) + far[b * INC : (b + 1) * INC]
        ).astype(BF16)


def swap(inner, outer, surf_count):
    pairs = [(i, i ^ 1) for i in range(surf_count)]
    others = [(0, 0), (surf_count - 1, surf_count - 1)]
    for i in range(1, surf_count - 1, 2):
        others += [(i, i + 1), (i + 1, i)]
    return lax.ppermute(inner, "surf", pairs), lax.ppermute(outer, "surf", others)


def exchange(array, surf_count):
    shape = array.shape
    array = array.reshape((surf_count, shape[0] // surf_count) + shape[1:])
    array = lax.all_to_all(array, "surf", split_axis=0, concat_axis=0, tiled=True)
    return array.reshape(shape)


def shards(
    currents, near_tiles, near_target, near_source, primal_compress, primal_expand, primal_coupling,
    far_source, far_owner, far_block, gram_inverse, gram_lower, gram_upper, refine_weight,
    dual_owner, dual_index, dual_self, dual_compress, dual_expand, dual_coupling,
):
    surf_count = lax.axis_size("surf")
    tiles = far_source.shape[0]
    near_count = near_tiles.shape[0]
    targets = surf_count * BLK
    capacity = max(2, 2 * NP_DEV // surf_count)
    pieces = -(-capacity // LANES)
    lists = (far_source.reshape(1, tiles), far_owner.reshape(1, tiles), far_block.reshape(1, tiles))
    square = ((TILE, TILE), BF16)
    cube = ((BLK, TILE, TILE), BF16)

    inner, outer = swap(currents, currents, surf_count)
    (partial,) = call(
        far_up_body,
        [((targets, INC * RANK), BF16)],
        (currents, primal_compress, primal_coupling) + lists,
        scratch=far_scratch(tiles),
        held=(2, 0, 1, 3, 4, 5),
        flops=10**11,
        name="far_up",
    )
    arrived = exchange(partial, surf_count)

    near_part, lower, upper, inner_edge, outer_edge, high, low, bounds, index_rows = call(
        prepare_body,
        [
            ((INC, NP_DEV), F32), cube, cube, square, square, ((BLK, TILE), I32),
            ((TILE, BLK), F32), ((surf_count, 2), I32), ((IDX_ROWS, NP_DEV), BF16),
        ],
        (
            near_target, near_source, currents, inner, outer, gram_inverse, gram_lower,
            gram_upper, dual_owner.reshape(1, NP_DEV), dual_index.reshape(1, NP_DEV), near_tiles,
        ),
        scratch=[
            pltpu.VMEM((BLK + 2, INC, TILE), BF16),
            pltpu.VMEM((BLK, INC, TILE), F32),
            pltpu.VMEM((near_count, INC, TILE), F32),
            pltpu.VMEM((BLK, TILE), F32),
            pltpu.VMEM(near_tiles.shape, BF16),
            pltpu.SemaphoreType.DMA((near_count // NEAR_CHUNK,)),
        ],
        held=(8, 9, 5, 6, 7, 2, 0, 1),
        far=(10,),
        small=(0, 1),
        kept=(0, 8),
        flops=10**11,
        name="prepare",
    )
    inner_edge, outer_edge = swap(inner_edge, outer_edge, surf_count)

    start, after, inner_note, outer_note = call(
        solve_body,
        [((INC, NP_DEV), F32)] * 2 + [((3, INC, TILE), BF16)] * 2,
        (arrived, near_part, primal_expand, gram_inverse, lower, upper),
        scratch=[
            pltpu.VMEM((2, 3, INC, TILE), BF16),
            pltpu.VMEM((BLK * INC, INC * RANK), BF16),
        ],
        held=(2, 3),
        pinned=(1,),
        name="solve",
    )
    inner_note, outer_note = swap(inner_note, outer_note, surf_count)
    rows = INC + IDX_ROWS
    (send,) = call(
        finish_body,
        [((surf_count, INC * pieces + TAIL, LANES), BF16)],
        (
            start, after, inner_note, outer_note, inner_edge, outer_edge, lower, upper,
            refine_weight.reshape(1, NP_DEV), index_rows, high, low, bounds,
        ),
        scratch=[
            pltpu.VMEM((2, 3, INC, TILE), BF16),
            pltpu.VMEM((2, TILE, TILE), BF16),
            pltpu.VMEM((BLK * rows, NP_DEV), BF16),
            pltpu.VMEM((NP_DEV, TILE), BF16),
            pltpu.VMEM((rows, NP_DEV + (pieces + 1) * LANES), F32),
        ],
        smem=(12,),
        held=(8,),
        pinned=(9,),
        name="finish",
    )
    shares = lax.all_to_all(send, "surf", split_axis=0, concat_axis=0, tiled=True)
    slots = surf_count * pieces * LANES
    (couple,) = call(
        couple_body,
        [((BLK * RANK, targets * RANK), BF16)],
        (dual_coupling,) + lists,
        scratch=[pltpu.VMEM((targets, RANK, BLK * RANK), F32), pltpu.VMEM((tiles, INC * RANK), F32)],
        held=(0, 1, 2, 3),
        small=(1, 2, 3),
        flops=10**10,
        name="couple",
    )
    field, partial = call(
        gather_body,
        [((BLK, INC, TILE), BF16), ((surf_count, INC, BLK * RANK), BF16)],
        (shares, dual_compress, couple),
        scratch=[
            pltpu.VMEM((surf_count * pieces, LANES), F32),
            pltpu.VMEM((BLK * INC, slots), BF16),
            pltpu.VMEM((slots, TILE), BF16),
        ],
        held=(1,),
        name="gather",
    )
    arrived = lax.all_to_all(partial, "surf", split_axis=0, concat_axis=0, tiled=True)
    (near_dual,) = call(
        self_body, [((INC, NP_DEV), F32)], (field, dual_self), held=(1,), name="self_part"
    )
    (response,) = call(
        answer_body,
        [((INC, NP_DEV), BF16)],
        (arrived, near_dual, dual_expand),
        scratch=[pltpu.VMEM((BLK * INC, BLK * RANK), BF16)],
        held=(2,),
        name="answer",
    )
    return response


def solution(mesh):
    both = ("groups", "surf")
    row, flat = P(None, both), P(both)
    cube, flat2 = P(both, None, None), P(both, None)
    return jax.shard_map(
        shards,
        mesh=mesh,
        in_specs=(
            row, cube, flat, flat, cube, cube, flat2, flat, flat2, flat, cube, cube, cube, flat,
            flat2, flat, cube, cube, cube, flat2,
        ),
        out_specs=row,
        check_vma=False,
    )
```

```python
import jax
import jax.numpy as jnp
from jax import lax
from jax.experimental import pallas as pl
from jax.experimental.pallas import tpu as pltpu
from jax.sharding import PartitionSpec as P

TILE = 256
INC = 32
RANK = 32
BLK = 8
NP_DEV = 2048
LANES = 128
IDX_ROWS = 16
TAIL = 8
NEAR_CHUNK = 8
F32 = jnp.float32
BF16 = jnp.bfloat16
I32 = jnp.int32
NT = (((1,), (1,)), ((), ()))
VMEM_LIMIT = 36 * 1024 * 1024
PRODUCT_COST = 10**9
NEAR_COST = 10**9


def dot(a, b):
    return jnp.dot(a, b, preferred_element_type=F32)


def dot_nt(a, b):
    return lax.dot_general(a, b, NT, preferred_element_type=F32)


def iota(shape, dim):
    return lax.broadcasted_iota(I32, shape, dim)


def block(array, i):
    return array[:, i * TILE : (i + 1) * TILE]


def as_hot(mask):
    return mask.astype(F32).astype(BF16)


def call(body, outs, args, scratch=(), smem=(), held=(), far=(), small=(), pinned=(), kept=(), flops=0, name=None):
    spaces = [
        pltpu.SMEM if k in smem else pltpu.HBM if k in held or k in far else pltpu.VMEM
        for k in range(len(args))
    ]
    size = sum(a.size * a.dtype.itemsize for a in args)
    outs = tuple(
        pltpu.VMEM(s, d) if k in kept else jax.ShapeDtypeStruct(s, d)
        for k, (s, d) in enumerate(outs)
    )
    buffers = [
        (pltpu.SMEM if k in small else pltpu.VMEM)(args[k].shape, args[k].dtype) for k in held
    ]
    waits = [pltpu.SemaphoreType.DMA(()) for _ in held]

    def wrapped(*refs):
        ins = list(refs[: len(args)])
        rest = refs[len(args) : len(refs) - 2 * len(held)]
        extra = refs[len(refs) - 2 * len(held) :]
        for n, k in enumerate(held):
            ins[k] = pltpu.make_async_copy(ins[k], extra[n], extra[len(held) + n])
            ins[k].start()
            ins[k] = (ins[k], extra[n])
        body(*ins, *rest)

    return pl.pallas_call(
        wrapped,
        out_shape=outs,
        in_specs=[pl.BlockSpec(memory_space=m) for m in spaces],
        out_specs=tuple(pl.BlockSpec(memory_space=pltpu.VMEM) for _ in outs),
        scratch_shapes=list(scratch) + buffers + waits,
        compiler_params=pltpu.CompilerParams(vmem_limit_bytes=VMEM_LIMIT),
        cost_estimate=pl.CostEstimate(flops=flops, bytes_accessed=size, transcendentals=0),
        name=name,
    )(*[pltpu.with_memory_space_constraint(a, m) if m is pltpu.HBM or k in pinned else a for k, (a, m) in enumerate(zip(args, spaces))])


def ready(operand):
    operand[0].wait()
    return operand[1]


def fill_hot(hot, columns):
    height, count = columns.shape
    columns = columns.astype(BF16)
    lane = iota((height, TILE), 1).astype(F32).astype(BF16)
    one, zero = jnp.ones((height, TILE), BF16), jnp.zeros((height, TILE), BF16)
    for k in range(count):
        hot[k * height : (k + 1) * height, :] = jnp.where(lane == columns[:, k : k + 1], one, zero)


def coefficients(blocks, compress):
    width = BLK * RANK
    every = dot_nt(blocks, compress[...].reshape(width, TILE))
    owner = iota((INC, width), 1) // RANK
    coef = jnp.zeros((INC, width), F32)
    for s in range(BLK):
        coef = jnp.where(owner == s, every[s * INC : (s + 1) * INC], coef)
    return coef


def far_up_body(
    value, compress, coupling, source, owner, place, inverse_ref, lower_ref, upper_ref,
    out_ref, inner_out, outer_out, blocks, turned, spread, pick, terms, waits,
):
    even = lax.axis_index("surf") % 2 == 0
    last = BLK - 1

    def message(to_right, out, first):
        edge, beside = (last, upper_ref) if to_right else (0, lower_ref)
        return [
            pltpu.make_async_copy(beside.at[edge], out.at[pl.ds(INC, TILE)], waits.at[first]),
            pltpu.make_async_copy(
                inverse_ref.at[edge], out.at[pl.ds(INC + TILE, TILE)], waits.at[first + 1]
            ),
        ]

    @pl.when(even)
    def _():
        for copy in message(True, inner_out, 0) + message(False, outer_out, 2):
            copy.start()

    @pl.when(jnp.logical_not(even))
    def _():
        for copy in message(False, inner_out, 0) + message(True, outer_out, 2):
            copy.start()

    coupling = ready(coupling)
    turned[...] = coupling[...].astype(F32).T
    value, compress = ready(value), ready(compress)
    for s in range(BLK):
        blocks[s * INC : (s + 1) * INC, :] = block(value, s)

    @pl.when(even)
    def _():
        inner_out[0:INC, :] = block(value, last)
        outer_out[0:INC, :] = block(value, 0)

    @pl.when(jnp.logical_not(even))
    def _():
        inner_out[0:INC, :] = block(value, 0)
        outer_out[0:INC, :] = block(value, last)

    coef = coefficients(blocks[...], compress)
    width = BLK * RANK
    keep = (iota((RANK, width), 1) % RANK) == iota((RANK, width), 0)
    for i in range(INC):
        spread[i * RANK : (i + 1) * RANK, :] = jnp.where(keep, coef[i : i + 1, :], 0.0).astype(BF16)
    source = ready(source)
    tiles = source.shape[1]
    pick[...] = dot(spread[...], as_hot((iota((width, tiles), 0) // RANK) == source[...]))

    def step(pair, carry):
        rows = pl.multiple_of(pair * (2 * RANK), 2 * RANK)
        got = pick[pl.ds(rows, 2 * RANK), :]
        first = jnp.zeros((RANK, tiles), F32)
        second = jnp.zeros((RANK, tiles), F32)
        for r in range(RANK):
            factor = turned[r * RANK : (r + 1) * RANK, :]
            first += got[r : r + 1, :] * factor
            second += got[RANK + r : RANK + r + 1, :] * factor
        terms[pl.ds(rows, 2 * RANK), :] = jnp.concatenate([first, second], axis=0).astype(BF16)
        return carry

    lax.fori_loop(0, INC // 2, step, 0)
    targets = out_ref.shape[0]
    owner, place = ready(owner), ready(place)
    select = as_hot(iota((targets, tiles), 0) == owner[...] * BLK + place[...])
    out_ref[...] = dot_nt(select, terms[...]).astype(BF16)

    @pl.when(even)
    def _():
        for copy in message(True, inner_out, 0) + message(False, outer_out, 2):
            copy.wait()

    @pl.when(jnp.logical_not(even))
    def _():
        for copy in message(False, inner_out, 0) + message(True, outer_out, 2):
            copy.wait()


def far_scratch(tiles):
    return [
        pltpu.VMEM((BLK * INC, TILE), BF16),
        pltpu.VMEM((RANK * RANK, tiles), F32),
        pltpu.VMEM((INC * RANK, BLK * RANK), BF16),
        pltpu.VMEM((INC * RANK, tiles), F32),
        pltpu.VMEM((INC * RANK, tiles), BF16),
    ]


def far_sums(arrived_ref, spread):
    rows = arrived_ref.shape[0]
    total = jnp.sum(arrived_ref[...].astype(F32).reshape(rows // BLK, BLK, INC * RANK), axis=0)
    width = INC * RANK
    keep = (iota((INC, width), 1) // RANK) == iota((INC, width), 0)
    for b in range(BLK):
        spread[b * INC : (b + 1) * INC, :] = jnp.where(keep, total[b : b + 1, :], 0.0).astype(BF16)
    fold = as_hot((iota((width, RANK), 0) % RANK) == iota((width, RANK), 1))
    return dot(spread[...], fold).astype(BF16)


def order(owner, index, ranks, owners, window, high_out, low_out, bounds_out, rows_out):
    before = as_hot(iota((TILE, TILE), 0) < iota((TILE, TILE), 1))
    number = iota((owners, TILE), 0)
    count = jnp.zeros((owners, 1), F32)
    begin = jnp.zeros((owners, 1), F32)
    hots, carries = [], []
    for c in range(BLK):
        names = block(owner, c)
        hot = (number == names).astype(F32)
        hots.append(hot)
        carries.append(count)
        count = count + jnp.sum(hot, axis=1, keepdims=True)
        begin = begin + jnp.sum((names < number).astype(F32), axis=1, keepdims=True)
    for c in range(BLK):
        rank = dot(hots[c].astype(BF16), before)
        ranks[c : c + 1, :] = jnp.sum(hots[c] * (rank + carries[c] + begin), axis=0, keepdims=True)
    spots = ranks[...].astype(I32)
    high_out[...] = spots // TILE
    low_out[...] = (spots % TILE).astype(F32).T
    pair = iota((owners, 2), 1)
    bounds_out[...] = jnp.where(pair == 0, begin, count).astype(I32)
    row = iota((IDX_ROWS, NP_DEV), 0)
    index = index[...]
    digits = jnp.where(row % 2 == 0, index // TILE, index % TILE)
    rows_out[...] = jnp.where(row < 2 * (window // LANES), digits, 0).astype(F32).astype(BF16)


def products_body(
    inverse, lower, upper, expand, owner, index,
    lower_out, upper_out, expand_out, high_out, low_out, bounds_out, rows_out, ranks,
):
    owner, index = ready(owner), ready(index)
    window = max(LANES, -(-(2 * NP_DEV // bounds_out.shape[0]) // LANES) * LANES)
    order(owner, index, ranks, bounds_out.shape[0], window, high_out, low_out, bounds_out, rows_out)
    inverse, lower, upper, expand = ready(inverse), ready(lower), ready(upper), ready(expand)
    for b in range(BLK):
        lower_out[b] = dot(lower[b], inverse[b]).astype(BF16)
        upper_out[b] = dot(upper[b], inverse[b]).astype(BF16)
        expand_out[b] = dot(expand[b], inverse[b]).astype(BF16)


def near_body(
    target, origin, own, inner_ref, outer_ref, inverse, tiles_ref,
    near_out, edges_out, cells, total, products, pair, tiles, arrivals,
):
    count = tiles_ref.shape[0]
    copies = []
    for c in range(count // NEAR_CHUNK):
        part = pl.ds(c * NEAR_CHUNK, NEAR_CHUNK)
        copy = pltpu.make_async_copy(tiles_ref.at[part], tiles.at[part], arrivals.at[c])
        copy.start()
        copies.append(copy)
    position = lax.axis_index("surf")
    odd = position % 2
    pair[0] = inner_ref[...]
    pair[1] = outer_ref[...]
    from_left, from_right = pair.at[1 - odd], pair.at[odd]
    cells[0] = from_left[0:INC, :]
    cells[BLK + 1] = from_right[0:INC, :]
    for n, message in enumerate((from_left, from_right)):
        edges_out[n] = dot(message[INC : INC + TILE, :], message[INC + TILE :, :]).astype(BF16)
    own, target, origin = ready(own), ready(target), ready(origin)
    for b in range(BLK):
        cells[b + 1] = block(own, b)
    total[...] = jnp.zeros_like(total)
    start = position * BLK - 1
    for c, copy in enumerate(copies):
        copy.wait()
        for k in range(c * NEAR_CHUNK, (c + 1) * NEAR_CHUNK):
            products[k] = dot(cells[origin[k] - start], tiles[k])
    for k in range(count):
        total[target[k]] += products[k]
    inverse = ready(inverse)
    for b in range(BLK):
        near_out[:, b * TILE : (b + 1) * TILE] = dot(total[b].astype(BF16), inverse[b])


def solve_body(
    arrived_ref, near_ref, expand_ref, lower_ref, upper_ref,
    start_out, next_out, inner_out, outer_out, notes, spread,
):
    sums = far_sums(arrived_ref, spread)
    start, low = [], []
    for b in range(BLK):
        value = block(near_ref, b) + dot(sums[b * INC : (b + 1) * INC, :], expand_ref[b])
        start.append(value)
        low.append(value.astype(BF16))
        start_out[:, b * TILE : (b + 1) * TILE] = value
    after = []
    for b in range(BLK):
        value = start[b]
        if b > 0:
            value = value - dot(low[b - 1], lower_ref[b])
        if b < BLK - 1:
            value = value - dot(low[b + 1], upper_ref[b])
        after.append(value)
        next_out[:, b * TILE : (b + 1) * TILE] = value
    last = BLK - 1
    odd = lax.axis_index("surf") % 2
    notes[0, 0] = low[last]
    notes[0, 1] = after[last].astype(BF16)
    notes[0, 2] = (start[last] - dot(after[last - 1].astype(BF16), lower_ref[last])).astype(BF16)
    notes[1, 0] = low[0]
    notes[1, 1] = after[0].astype(BF16)
    notes[1, 2] = (start[0] - dot(after[1].astype(BF16), upper_ref[0])).astype(BF16)
    inner_out[...] = notes[odd]
    outer_out[...] = notes[1 - odd]


def finish_body(
    start_ref, next_ref, inner_note, outer_note, edges, lower_ref, upper_ref,
    weight, index_rows, high_ref, low_ref, bounds_ref, send_ref,
    notes, spread, hot, ordered,
):
    fill_hot(hot, low_ref[...])
    last = BLK - 1
    position = lax.axis_index("surf")
    odd = position % 2
    notes[0] = inner_note[...]
    notes[1] = outer_note[...]
    from_left, from_right = notes.at[1 - odd], notes.at[odd]
    upper_left, lower_right = edges.at[0], edges.at[1]
    has_left = (position > 0).astype(F32)
    has_right = (position < lax.axis_size("surf") - 1).astype(F32)
    start = [block(start_ref, b) for b in range(BLK)]
    low = [start[0].astype(BF16), start[last].astype(BF16)]
    now = [block(next_ref, b) for b in range(BLK)]
    beside_left = (from_left[1].astype(F32) - dot(low[0], upper_left[...])) * has_left
    beside_right = (from_right[1].astype(F32) - dot(low[1], lower_right[...])) * has_right
    now[0] = now[0] - dot(from_left[0], lower_ref[0]) * has_left
    now[last] = now[last] - dot(from_right[0], upper_ref[last]) * has_right

    def sweep(values, left, right):
        values = [v.astype(BF16) for v in values]
        chain = [left.astype(BF16)] + values + [right.astype(BF16)]
        return values, [
            start[b] - dot(chain[b], lower_ref[b]) - dot(chain[b + 2], upper_ref[b])
            for b in range(BLK)
        ]

    values, then = sweep(now, beside_left, beside_right)
    beside_left = (from_left[2].astype(F32) - dot(values[0], upper_left[...])) * has_left
    beside_right = (from_right[2].astype(F32) - dot(values[last], lower_right[...])) * has_right
    values, then = sweep(then, beside_left, beside_right)
    weight = ready(weight)
    rows = INC + IDX_ROWS
    for b in range(BLK):
        solved = then[b].astype(BF16).astype(F32)
        shares = solved * block(weight, b)
        every = jnp.concatenate([shares.astype(BF16), block(index_rows, b)], axis=0)
        high = high_ref[b : b + 1, :].astype(F32).astype(BF16)
        for h in range(BLK):
            spread[h * rows : (h + 1) * rows, b * TILE : (b + 1) * TILE] = jnp.where(
                high == h, every, jnp.zeros_like(every)
            )
    sorted_rows = dot(spread[...], hot[...])
    for h in range(BLK):
        ordered[:, h * TILE : (h + 1) * TILE] = sorted_rows[h * rows : (h + 1) * rows]
    owners = send_ref.shape[0]
    pieces = (send_ref.shape[1] - TAIL) // INC
    wide = (pieces + 1) * LANES
    ordered[:, NP_DEV:] = jnp.zeros((rows, ordered.shape[1] - NP_DEV), F32)
    row = iota((TAIL, LANES), 0)
    slot = iota((TAIL, LANES), 1) + (row // 2) * LANES
    for o in range(owners):
        begin = bounds_ref[o, 0]
        base = pl.multiple_of((begin // LANES) * LANES, LANES)
        piece = pltpu.roll(ordered[:, pl.ds(base, wide)], wide - (begin - base), 1)
        parts = [piece[:INC, j * LANES : (j + 1) * LANES] for j in range(pieces)]
        tail = piece[INC : INC + TAIL, :LANES]
        for j in range(1, pieces):
            tail = jnp.where(row // 2 == j, piece[INC : INC + TAIL, j * LANES : (j + 1) * LANES], tail)
        tail = jnp.where(slot >= bounds_ref[o, 1], -16.0, tail)
        send_ref[o] = jnp.concatenate(parts + [tail], axis=0).astype(BF16)


def gather_body(
    arrived_ref, compress, couple_ref, field_out, out_ref, index, spread, hot,
):
    owners, rows, _ = arrived_ref.shape
    pieces = (rows - TAIL) // INC
    for e in range(owners):
        tail = arrived_ref[e].astype(F32)[INC * pieces :]
        marks = tail.astype(BF16)
        for j in range(pieces):
            k = e * pieces + j
            part = arrived_ref[e, j * INC : (j + 1) * INC, :]
            high = marks[2 * j : 2 * j + 1]
            index[k : k + 1, :] = tail[2 * j + 1 : 2 * j + 2]
            for h in range(BLK):
                spread[h * INC : (h + 1) * INC, k * LANES : (k + 1) * LANES] = jnp.where(
                    high == h, part, jnp.zeros_like(part)
                )
    fill_hot(hot, index[...].T)
    field = dot(spread[...], hot[...]).astype(BF16)
    for b in range(BLK):
        field_out[b] = field[b * INC : (b + 1) * INC]
    coef = coefficients(field, compress).astype(BF16)
    for o in range(out_ref.shape[0]):
        out_ref[o] = dot(coef, block(couple_ref, o)).astype(BF16)


def couple_body(coupling, source, owner, place, basis, out_ref, basis_out, total, lanes):
    tiles, width = lanes.shape[0], BLK * RANK
    flat = RANK * RANK
    total[...] = jnp.zeros_like(total)
    coupling = ready(coupling)
    lanes[...] = coupling[...].astype(F32)
    keep = (iota((RANK, flat), 1) % RANK) == iota((RANK, flat), 0)
    fold = as_hot((iota((flat, width), 0) // RANK) == (iota((flat, width), 1) % RANK))
    number = iota((RANK, width), 1) // RANK
    source, owner, place = ready(source), ready(owner), ready(place)
    group = 8

    def step(c, carry):
        begin = pl.multiple_of(c * group, group)
        rows = lanes[pl.ds(begin, group), :]
        tall = [jnp.where(keep, rows[k : k + 1], 0.0).astype(BF16) for k in range(group)]
        turned = dot(jnp.concatenate(tall, axis=0), fold)
        for k in range(group):
            f = begin + k
            tile = jnp.where(number == source[0, f], turned[k * RANK : (k + 1) * RANK], 0.0)
            total[owner[0, f] * BLK + place[0, f]] += tile
        return carry

    lax.fori_loop(0, tiles // group, step, 0)
    for o in range(out_ref.shape[1] // TILE):
        part = total[o * BLK : (o + 1) * BLK].reshape(TILE, width)
        out_ref[:, o * TILE : (o + 1) * TILE] = part.T.astype(BF16)
    basis_out[...] = ready(basis)[...]


def self_body(field_ref, tiles, basis, out_ref, basis_out):
    basis_out[...] = ready(basis)[...]
    tiles = ready(tiles)
    for b in range(BLK):
        out_ref[:, b * TILE : (b + 1) * TILE] = dot(field_ref[b], tiles[b])


def answer_body(arrived_ref, near_ref, expand, out_ref, spread):
    total = jnp.sum(arrived_ref[...].astype(F32), axis=0)
    number = iota(total.shape, 1) // RANK
    for b in range(BLK):
        spread[b * INC : (b + 1) * INC, :] = jnp.where(number == b, total, 0.0).astype(BF16)
    far = dot(spread[...], expand[...].reshape(BLK * RANK, TILE))
    for b in range(BLK):
        out_ref[:, b * TILE : (b + 1) * TILE] = (
            block(near_ref, b) + far[b * INC : (b + 1) * INC]
        ).astype(BF16)


def swap(inner, outer, surf_count):
    pairs = [(i, i ^ 1) for i in range(surf_count)]
    others = [(0, 0), (surf_count - 1, surf_count - 1)]
    for i in range(1, surf_count - 1, 2):
        others += [(i, i + 1), (i + 1, i)]
    return lax.ppermute(inner, "surf", pairs), lax.ppermute(outer, "surf", others)


def exchange(array, surf_count):
    shape = array.shape
    array = array.reshape((surf_count, shape[0] // surf_count) + shape[1:])
    array = lax.all_to_all(array, "surf", split_axis=0, concat_axis=0, tiled=True)
    return array.reshape(shape)


def shards(
    currents, near_tiles, near_target, near_source, primal_compress, primal_expand, primal_coupling,
    far_source, far_owner, far_block, gram_inverse, gram_lower, gram_upper, refine_weight,
    dual_owner, dual_index, dual_self, dual_compress, dual_expand, dual_coupling,
):
    surf_count = lax.axis_size("surf")
    tiles = far_source.shape[0]
    near_count = near_tiles.shape[0]
    targets = surf_count * BLK
    capacity = max(2, 2 * NP_DEV // surf_count)
    pieces = -(-capacity // LANES)
    lists = (far_source.reshape(1, tiles), far_owner.reshape(1, tiles), far_block.reshape(1, tiles))
    cube = ((BLK, TILE, TILE), BF16)

    message = ((INC + 2 * TILE, TILE), BF16)
    partial, inner, outer = call(
        far_up_body,
        [((targets, INC * RANK), BF16), message, message],
        (currents, primal_compress, primal_coupling) + lists + (gram_inverse, gram_lower, gram_upper),
        scratch=far_scratch(tiles) + [pltpu.SemaphoreType.DMA((4,))],
        held=(2, 0, 1, 3, 4, 5),
        far=(6, 7, 8),
        name="far_up",
    )
    arrived = exchange(partial, surf_count)
    inner, outer = swap(inner, outer, surf_count)
    lower, upper, expanded, high, low, bounds, index_rows = call(
        products_body,
        [
            cube, cube, ((BLK, RANK, TILE), BF16), ((BLK, TILE), I32), ((TILE, BLK), F32),
            ((surf_count, 2), I32), ((IDX_ROWS, NP_DEV), BF16),
        ],
        (
            gram_inverse, gram_lower, gram_upper, primal_expand,
            dual_owner.reshape(1, NP_DEV), dual_index.reshape(1, NP_DEV),
        ),
        scratch=[pltpu.VMEM((BLK, TILE), F32)],
        held=(4, 5, 0, 1, 2, 3),
        flops=PRODUCT_COST,
        name="products",
    )
    near_part, edges = call(
        near_body,
        [((INC, NP_DEV), F32), ((2, TILE, TILE), BF16)],
        (near_target, near_source, currents, inner, outer, gram_inverse, near_tiles),
        scratch=[
            pltpu.VMEM((BLK + 2, INC, TILE), BF16),
            pltpu.VMEM((BLK, INC, TILE), F32),
            pltpu.VMEM((near_count, INC, TILE), F32),
            pltpu.VMEM((2,) + message[0], BF16),
            pltpu.VMEM(near_tiles.shape, BF16),
            pltpu.SemaphoreType.DMA((near_count // NEAR_CHUNK,)),
        ],
        held=(2, 0, 1, 5),
        far=(6,),
        small=(0, 1),
        flops=NEAR_COST,
        name="near",
    )
    start, after, inner_note, outer_note = call(
        solve_body,
        [((INC, NP_DEV), F32)] * 2 + [((3, INC, TILE), BF16)] * 2,
        (arrived, near_part, expanded, lower, upper),
        scratch=[
            pltpu.VMEM((2, 3, INC, TILE), BF16),
            pltpu.VMEM((BLK * INC, INC * RANK), BF16),
        ],
        name="solve",
    )
    inner_note, outer_note = swap(inner_note, outer_note, surf_count)
    rows = INC + IDX_ROWS
    (send,) = call(
        finish_body,
        [((surf_count, INC * pieces + TAIL, LANES), BF16)],
        (
            start, after, inner_note, outer_note, edges, lower, upper,
            refine_weight.reshape(1, NP_DEV), index_rows, high, low, bounds,
        ),
        scratch=[
            pltpu.VMEM((2, 3, INC, TILE), BF16),
            pltpu.VMEM((BLK * rows, NP_DEV), BF16),
            pltpu.VMEM((NP_DEV, TILE), BF16),
            pltpu.VMEM((rows, NP_DEV + (pieces + 1) * LANES), F32),
        ],
        smem=(11,),
        held=(7,),
        name="finish",
    )
    shares = lax.all_to_all(send, "surf", split_axis=0, concat_axis=0, tiled=True)
    slots = surf_count * pieces * LANES
    couple, compress = call(
        couple_body,
        [((BLK * RANK, targets * RANK), BF16), (dual_compress.shape, BF16)],
        (dual_coupling,) + lists + (dual_compress,),
        scratch=[pltpu.VMEM((targets, RANK, BLK * RANK), F32), pltpu.VMEM((tiles, INC * RANK), F32)],
        held=(0, 1, 2, 3, 4),
        small=(1, 2, 3),
        flops=10**10,
        name="couple",
    )
    field, partial = call(
        gather_body,
        [((BLK, INC, TILE), BF16), ((surf_count, INC, BLK * RANK), BF16)],
        (shares, compress, couple),
        scratch=[
            pltpu.VMEM((surf_count * pieces, LANES), F32),
            pltpu.VMEM((BLK * INC, slots), BF16),
            pltpu.VMEM((slots, TILE), BF16),
        ],
        name="gather",
    )
    arrived = lax.all_to_all(partial, "surf", split_axis=0, concat_axis=0, tiled=True)
    near_dual, expand = call(
        self_body,
        [((INC, NP_DEV), F32), (dual_expand.shape, BF16)],
        (field, dual_self, dual_expand),
        held=(2, 1),
        name="self_part",
    )
    (response,) = call(
        answer_body,
        [((INC, NP_DEV), BF16)],
        (arrived, near_dual, expand),
        scratch=[pltpu.VMEM((BLK * INC, BLK * RANK), BF16)],
        name="answer",
    )
    return response


def solution(mesh):
    both = ("groups", "surf")
    row, flat = P(None, both), P(both)
    cube, flat2 = P(both, None, None), P(both, None)
    return jax.shard_map(
        shards,
        mesh=mesh,
        in_specs=(
            row, cube, flat, flat, cube, cube, flat2, flat, flat2, flat, cube, cube, cube, flat,
            flat2, flat, cube, cube, cube, flat2,
        ),
        out_specs=row,
        check_vma=False,
    )
```

```python
import jax
import jax.numpy as jnp
from jax import lax
from jax.experimental import pallas as pl
from jax.experimental.pallas import tpu as pltpu
from jax.sharding import PartitionSpec as P

TILE = 256
INC = 32
RANK = 32
BLK = 8
NP_DEV = 2048
LANES = 128
IDX_ROWS = 16
TAIL = 8
NEAR_CHUNK = 8
F32 = jnp.float32
BF16 = jnp.bfloat16
I32 = jnp.int32
NT = (((1,), (1,)), ((), ()))
VMEM_LIMIT = 36 * 1024 * 1024
PRODUCT_COST = 10**9
NEAR_COST = 10**9


def dot(a, b):
    return jnp.dot(a, b, preferred_element_type=F32)


def dot_nt(a, b):
    return lax.dot_general(a, b, NT, preferred_element_type=F32)


def iota(shape, dim):
    return lax.broadcasted_iota(I32, shape, dim)


def block(array, i):
    return array[:, i * TILE : (i + 1) * TILE]


def as_hot(mask):
    return mask.astype(F32).astype(BF16)


def call(body, outs, args, scratch=(), smem=(), held=(), far=(), small=(), pinned=(), kept=(), flops=0, name=None):
    spaces = [
        pltpu.SMEM if k in smem else pltpu.HBM if k in held or k in far else pltpu.VMEM
        for k in range(len(args))
    ]
    size = sum(a.size * a.dtype.itemsize for a in args)
    outs = tuple(
        pltpu.VMEM(s, d) if k in kept else jax.ShapeDtypeStruct(s, d)
        for k, (s, d) in enumerate(outs)
    )
    buffers = [
        (pltpu.SMEM if k in small else pltpu.VMEM)(args[k].shape, args[k].dtype) for k in held
    ]
    waits = [pltpu.SemaphoreType.DMA(()) for _ in held]

    def wrapped(*refs):
        ins = list(refs[: len(args)])
        rest = refs[len(args) : len(refs) - 2 * len(held)]
        extra = refs[len(refs) - 2 * len(held) :]
        for n, k in enumerate(held):
            ins[k] = pltpu.make_async_copy(ins[k], extra[n], extra[len(held) + n])
            ins[k].start()
            ins[k] = (ins[k], extra[n])
        body(*ins, *rest)

    return pl.pallas_call(
        wrapped,
        out_shape=outs,
        in_specs=[pl.BlockSpec(memory_space=m) for m in spaces],
        out_specs=tuple(pl.BlockSpec(memory_space=pltpu.VMEM) for _ in outs),
        scratch_shapes=list(scratch) + buffers + waits,
        compiler_params=pltpu.CompilerParams(vmem_limit_bytes=VMEM_LIMIT),
        cost_estimate=pl.CostEstimate(flops=flops, bytes_accessed=size, transcendentals=0),
        name=name,
    )(*[pltpu.with_memory_space_constraint(a, m) if m is pltpu.HBM or k in pinned else a for k, (a, m) in enumerate(zip(args, spaces))])


def ready(operand):
    operand[0].wait()
    return operand[1]


def fill_hot(hot, columns):
    height, count = columns.shape
    columns = columns.astype(BF16)
    lane = iota((height, TILE), 1).astype(F32).astype(BF16)
    one, zero = jnp.ones((height, TILE), BF16), jnp.zeros((height, TILE), BF16)
    for k in range(count):
        hot[k * height : (k + 1) * height, :] = jnp.where(lane == columns[:, k : k + 1], one, zero)


def coefficients(blocks, compress):
    width = BLK * RANK
    every = dot_nt(blocks, compress[...].reshape(width, TILE))
    owner = iota((INC, width), 1) // RANK
    coef = jnp.zeros((INC, width), F32)
    for s in range(BLK):
        coef = jnp.where(owner == s, every[s * INC : (s + 1) * INC], coef)
    return coef


def far_up_body(
    value, compress, coupling, source, owner, place,
    out_ref, inner_out, outer_out, blocks, turned, spread, pick, terms,
):
    coupling = ready(coupling)
    turned[...] = coupling[...].astype(F32).T
    value, compress = ready(value), ready(compress)
    for s in range(BLK):
        blocks[s * INC : (s + 1) * INC, :] = block(value, s)

    odd = lax.axis_index("surf") % 2
    inner_out[...] = blocks[pl.ds(pl.multiple_of((1 - odd) * ((BLK - 1) * INC), INC), INC), :]
    outer_out[...] = blocks[pl.ds(pl.multiple_of(odd * ((BLK - 1) * INC), INC), INC), :]

    coef = coefficients(blocks[...], compress)
    width = BLK * RANK
    keep = (iota((RANK, width), 1) % RANK) == iota((RANK, width), 0)
    for i in range(INC):
        spread[i * RANK : (i + 1) * RANK, :] = jnp.where(keep, coef[i : i + 1, :], 0.0).astype(BF16)
    source = ready(source)
    tiles = source.shape[1]
    pick[...] = dot(spread[...], as_hot((iota((width, tiles), 0) // RANK) == source[...]))

    def step(pair, carry):
        rows = pl.multiple_of(pair * (2 * RANK), 2 * RANK)
        got = pick[pl.ds(rows, 2 * RANK), :]
        first = jnp.zeros((RANK, tiles), F32)
        second = jnp.zeros((RANK, tiles), F32)
        for r in range(RANK):
            factor = turned[r * RANK : (r + 1) * RANK, :]
            first += got[r : r + 1, :] * factor
            second += got[RANK + r : RANK + r + 1, :] * factor
        terms[pl.ds(rows, 2 * RANK), :] = jnp.concatenate([first, second], axis=0).astype(BF16)
        return carry

    lax.fori_loop(0, INC // 2, step, 0)
    targets = out_ref.shape[0]
    owner, place = ready(owner), ready(place)
    select = as_hot(iota((targets, tiles), 0) == owner[...] * BLK + place[...])
    out_ref[...] = dot_nt(select, terms[...]).astype(BF16)


def far_scratch(tiles):
    return [
        pltpu.VMEM((BLK * INC, TILE), BF16),
        pltpu.VMEM((RANK * RANK, tiles), F32),
        pltpu.VMEM((INC * RANK, BLK * RANK), BF16),
        pltpu.VMEM((INC * RANK, tiles), F32),
        pltpu.VMEM((INC * RANK, tiles), BF16),
    ]


def far_sums(arrived_ref, spread):
    rows = arrived_ref.shape[0]
    total = jnp.sum(arrived_ref[...].astype(F32).reshape(rows // BLK, BLK, INC * RANK), axis=0)
    width = INC * RANK
    keep = (iota((INC, width), 1) // RANK) == iota((INC, width), 0)
    for b in range(BLK):
        spread[b * INC : (b + 1) * INC, :] = jnp.where(keep, total[b : b + 1, :], 0.0).astype(BF16)
    fold = as_hot((iota((width, RANK), 0) % RANK) == iota((width, RANK), 1))
    return dot(spread[...], fold).astype(BF16)


def order_body(owner, index, high_out, hot_out, bounds_out, rows_out, ranks):
    owner, index = ready(owner), ready(index)
    owners = bounds_out.shape[0]
    pieces = -(-max(2, 2 * NP_DEV // owners) // LANES)
    before = as_hot(iota((TILE, TILE), 0) < iota((TILE, TILE), 1))
    number = iota((owners, TILE), 0)
    count = jnp.zeros((owners, 1), F32)
    begin = jnp.zeros((owners, 1), F32)
    hots, carries = [], []
    for c in range(BLK):
        names = block(owner, c)
        hot = (number == names).astype(F32)
        hots.append(hot)
        carries.append(count)
        count = count + jnp.sum(hot, axis=1, keepdims=True)
        begin = begin + jnp.sum((names < number).astype(F32), axis=1, keepdims=True)
    for c in range(BLK):
        rank = dot(hots[c].astype(BF16), before)
        ranks[c : c + 1, :] = jnp.sum(hots[c] * (rank + carries[c] + begin), axis=0, keepdims=True)
    spots = ranks[...].astype(I32)
    high_out[...] = spots // TILE
    fill_hot(hot_out, (spots % TILE).astype(F32).T)
    pair = iota((owners, 2), 1)
    bounds_out[...] = jnp.where(pair == 0, begin, count).astype(I32)
    row = iota((IDX_ROWS, NP_DEV), 0)
    index = index[...]
    digits = jnp.where(row % 2 == 0, index // TILE, index % TILE)
    rows_out[...] = jnp.where(row < 2 * pieces, digits, 0).astype(F32).astype(BF16)


def products_body(
    inverse, lower, upper, expand, lower_out, upper_out, expand_out,
):
    inverse, lower, upper, expand = ready(inverse), ready(lower), ready(upper), ready(expand)
    for b in range(BLK):
        lower_out[b] = dot(lower[b], inverse[b]).astype(BF16)
        upper_out[b] = dot(upper[b], inverse[b]).astype(BF16)
        expand_out[b] = dot(expand[b], inverse[b]).astype(BF16)


def near_body(
    target, origin, own, inner_ref, outer_ref, inverse, tiles_ref,
    near_out, cells, total, products, pair, tiles, arrivals,
):
    count = tiles_ref.shape[0]
    copies = []
    for c in range(count // NEAR_CHUNK):
        part = pl.ds(c * NEAR_CHUNK, NEAR_CHUNK)
        copy = pltpu.make_async_copy(tiles_ref.at[part], tiles.at[part], arrivals.at[c])
        copy.start()
        copies.append(copy)
    position = lax.axis_index("surf")
    odd = position % 2
    pair[0] = inner_ref[...]
    pair[1] = outer_ref[...]
    cells[0] = pair[1 - odd]
    cells[BLK + 1] = pair[odd]
    own, target, origin = ready(own), ready(target), ready(origin)
    for b in range(BLK):
        cells[b + 1] = block(own, b)
    total[...] = jnp.zeros_like(total)
    start = position * BLK - 1
    for c, copy in enumerate(copies):
        copy.wait()
        for k in range(c * NEAR_CHUNK, (c + 1) * NEAR_CHUNK):
            products[k] = dot(cells[origin[k] - start], tiles[k])
    for k in range(count):
        total[target[k]] += products[k]
    inverse = ready(inverse)
    for b in range(BLK):
        near_out[:, b * TILE : (b + 1) * TILE] = dot(total[b].astype(BF16), inverse[b])


def solve_body(
    arrived_ref, near_ref, expand_ref, lower_ref, upper_ref,
    start_out, next_out, inner_out, outer_out, notes, spread,
):
    sums = far_sums(arrived_ref, spread)
    start, low = [], []
    for b in range(BLK):
        value = block(near_ref, b) + dot(sums[b * INC : (b + 1) * INC, :], expand_ref[b])
        start.append(value)
        low.append(value.astype(BF16))
        start_out[:, b * TILE : (b + 1) * TILE] = value
    after = []
    for b in range(BLK):
        value = start[b]
        if b > 0:
            value = value - dot(low[b - 1], lower_ref[b])
        if b < BLK - 1:
            value = value - dot(low[b + 1], upper_ref[b])
        after.append(value)
        next_out[:, b * TILE : (b + 1) * TILE] = value
    last = BLK - 1
    odd = lax.axis_index("surf") % 2
    for n, (edge, inside, away, back) in enumerate(
        ((last, last - 1, lower_ref, upper_ref), (0, 1, upper_ref, lower_ref))
    ):
        feedless = start[edge] - dot(after[inside].astype(BF16), away[edge])
        notes[n, 0:INC, :] = low[edge]
        notes[n, INC : 2 * INC, :] = after[edge].astype(BF16)
        notes[n, 2 * INC : 3 * INC, :] = feedless.astype(BF16)
        notes[n, 3 * INC :, :] = back[edge]
    inner_out[...] = notes[odd]
    outer_out[...] = notes[1 - odd]


def middle_body(start_ref, next_ref, lower_ref, upper_ref, second_out, third_out):
    last = BLK - 1
    now = [block(next_ref, b).astype(BF16) for b in range(BLK)]
    second = []
    for b in range(BLK):
        value = block(start_ref, b)
        if b > 1:
            value = value - dot(now[b - 1], lower_ref[b])
        if b < last - 1:
            value = value - dot(now[b + 1], upper_ref[b])
        second.append(value.astype(BF16))
        second_out[:, b * TILE : (b + 1) * TILE] = value
    for b in range(BLK):
        value = block(start_ref, b)
        if 2 < b < last:
            value = value - dot(second[b - 1], lower_ref[b])
        if 0 < b < last - 2:
            value = value - dot(second[b + 1], upper_ref[b])
        third_out[:, b * TILE : (b + 1) * TILE] = value


def finish_body(
    start_ref, next_ref, second_ref, third_ref, inner_note, outer_note, lower_ref, upper_ref,
    weight, index_rows, high_ref, hot_ref, bounds_ref, send_ref,
    notes, spread, ordered,
):
    position = lax.axis_index("surf")
    odd = position % 2
    notes[0] = inner_note[...]
    notes[1] = outer_note[...]
    then = [block(third_ref, b) for b in range(BLK)]
    for left in (True, False):
        n = 1 - odd if left else odd
        exists = (position > 0) if left else (position < lax.axis_size("surf") - 1)
        exists = exists.astype(F32)
        edge, step = (0, 1) if left else (BLK - 1, -1)
        toward, away = (lower_ref, upper_ref) if left else (upper_ref, lower_ref)
        one, two = edge + step, edge + 2 * step
        first = block(start_ref, edge).astype(BF16)
        beyond = notes[n, 3 * INC :, :]
        beside = notes[n, INC : 2 * INC, :].astype(F32) - dot(first, beyond)
        beside = (beside * exists).astype(BF16)
        now = block(next_ref, edge) - dot(notes[n, 0:INC, :], toward[edge]) * exists
        now = now.astype(BF16)
        beside_next = notes[n, 2 * INC : 3 * INC, :].astype(F32) - dot(now, beyond)
        beside_next = (beside_next * exists).astype(BF16)
        second = (block(second_ref, edge) - dot(beside, toward[edge])).astype(BF16)
        second_one = (block(second_ref, one) - dot(now, toward[one])).astype(BF16)
        then[edge] = then[edge] - dot(beside_next, toward[edge]) - dot(second_one, away[edge])
        then[one] = then[one] - dot(second, toward[one])
        then[two] = then[two] - dot(second_one, toward[two])
    weight = ready(weight)
    rows = INC + IDX_ROWS
    for b in range(BLK):
        solved = then[b].astype(BF16).astype(F32)
        shares = solved * block(weight, b)
        every = jnp.concatenate([shares.astype(BF16), block(index_rows, b)], axis=0)
        high = high_ref[b : b + 1, :].astype(F32).astype(BF16)
        for h in range(BLK):
            spread[h * rows : (h + 1) * rows, b * TILE : (b + 1) * TILE] = jnp.where(
                high == h, every, jnp.zeros_like(every)
            )
    sorted_rows = dot(spread[...], hot_ref[...])
    for h in range(BLK):
        ordered[:, h * TILE : (h + 1) * TILE] = sorted_rows[h * rows : (h + 1) * rows]
    owners = send_ref.shape[0]
    pieces = (send_ref.shape[1] - TAIL) // INC
    wide = (pieces + 1) * LANES
    ordered[:, NP_DEV:] = jnp.zeros((rows, ordered.shape[1] - NP_DEV), F32)
    row = iota((TAIL, LANES), 0)
    slot = iota((TAIL, LANES), 1) + (row // 2) * LANES
    for o in range(owners):
        begin = bounds_ref[o, 0]
        base = pl.multiple_of((begin // LANES) * LANES, LANES)
        piece = pltpu.roll(ordered[:, pl.ds(base, wide)], wide - (begin - base), 1)
        parts = [piece[:INC, j * LANES : (j + 1) * LANES] for j in range(pieces)]
        tail = piece[INC : INC + TAIL, :LANES]
        for j in range(1, pieces):
            tail = jnp.where(row // 2 == j, piece[INC : INC + TAIL, j * LANES : (j + 1) * LANES], tail)
        tail = jnp.where(slot >= bounds_ref[o, 1], -16.0, tail)
        send_ref[o] = jnp.concatenate(parts + [tail], axis=0).astype(BF16)


def gather_body(
    arrived_ref, compress, couple_ref, field_out, out_ref, index, spread, hot,
):
    owners, rows, _ = arrived_ref.shape
    pieces = (rows - TAIL) // INC
    for e in range(owners):
        tail = arrived_ref[e].astype(F32)[INC * pieces :]
        marks = tail.astype(BF16)
        for j in range(pieces):
            k = e * pieces + j
            part = arrived_ref[e, j * INC : (j + 1) * INC, :]
            high = marks[2 * j : 2 * j + 1]
            index[k : k + 1, :] = tail[2 * j + 1 : 2 * j + 2]
            for h in range(BLK):
                spread[h * INC : (h + 1) * INC, k * LANES : (k + 1) * LANES] = jnp.where(
                    high == h, part, jnp.zeros_like(part)
                )
    fill_hot(hot, index[...].T)
    field = dot(spread[...], hot[...]).astype(BF16)
    for b in range(BLK):
        field_out[b] = field[b * INC : (b + 1) * INC]
    coef = coefficients(field, compress).astype(BF16)
    for o in range(out_ref.shape[0]):
        out_ref[o] = dot(coef, block(couple_ref, o)).astype(BF16)


def couple_body(coupling, source, owner, place, basis, out_ref, basis_out, total, lanes):
    tiles, width = lanes.shape[0], BLK * RANK
    flat = RANK * RANK
    total[...] = jnp.zeros_like(total)
    coupling = ready(coupling)
    lanes[...] = coupling[...].astype(F32)
    keep = (iota((RANK, flat), 1) % RANK) == iota((RANK, flat), 0)
    fold = as_hot((iota((flat, width), 0) // RANK) == (iota((flat, width), 1) % RANK))
    number = iota((RANK, width), 1) // RANK
    source, owner, place = ready(source), ready(owner), ready(place)
    group = 8

    def step(c, carry):
        begin = pl.multiple_of(c * group, group)
        rows = lanes[pl.ds(begin, group), :]
        tall = [jnp.where(keep, rows[k : k + 1], 0.0).astype(BF16) for k in range(group)]
        turned = dot(jnp.concatenate(tall, axis=0), fold)
        for k in range(group):
            f = begin + k
            tile = jnp.where(number == source[0, f], turned[k * RANK : (k + 1) * RANK], 0.0)
            total[owner[0, f] * BLK + place[0, f]] += tile
        return carry

    lax.fori_loop(0, tiles // group, step, 0)
    for o in range(out_ref.shape[1] // TILE):
        part = total[o * BLK : (o + 1) * BLK].reshape(TILE, width)
        out_ref[:, o * TILE : (o + 1) * TILE] = part.T.astype(BF16)
    basis_out[...] = ready(basis)[...]


def self_body(field_ref, tiles, basis, out_ref, basis_out):
    basis_out[...] = ready(basis)[...]
    tiles = ready(tiles)
    for b in range(BLK):
        out_ref[:, b * TILE : (b + 1) * TILE] = dot(field_ref[b], tiles[b])


def answer_body(arrived_ref, near_ref, expand, out_ref, spread):
    total = jnp.sum(arrived_ref[...].astype(F32), axis=0)
    number = iota(total.shape, 1) // RANK
    for b in range(BLK):
        spread[b * INC : (b + 1) * INC, :] = jnp.where(number == b, total, 0.0).astype(BF16)
    far = dot(spread[...], expand[...].reshape(BLK * RANK, TILE))
    for b in range(BLK):
        out_ref[:, b * TILE : (b + 1) * TILE] = (
            block(near_ref, b) + far[b * INC : (b + 1) * INC]
        ).astype(BF16)


def swap(inner, outer, surf_count):
    pairs = [(i, i ^ 1) for i in range(surf_count)]
    others = [(0, 0), (surf_count - 1, surf_count - 1)]
    for i in range(1, surf_count - 1, 2):
        others += [(i, i + 1), (i + 1, i)]
    return lax.ppermute(inner, "surf", pairs), lax.ppermute(outer, "surf", others)


def exchange(array, surf_count):
    shape = array.shape
    array = array.reshape((surf_count, shape[0] // surf_count) + shape[1:])
    array = lax.all_to_all(array, "surf", split_axis=0, concat_axis=0, tiled=True)
    return array.reshape(shape)


def shards(
    currents, near_tiles, near_target, near_source, primal_compress, primal_expand, primal_coupling,
    far_source, far_owner, far_block, gram_inverse, gram_lower, gram_upper, refine_weight,
    dual_owner, dual_index, dual_self, dual_compress, dual_expand, dual_coupling,
):
    surf_count = lax.axis_size("surf")
    tiles = far_source.shape[0]
    near_count = near_tiles.shape[0]
    targets = surf_count * BLK
    capacity = max(2, 2 * NP_DEV // surf_count)
    pieces = -(-capacity // LANES)
    lists = (far_source.reshape(1, tiles), far_owner.reshape(1, tiles), far_block.reshape(1, tiles))
    cube = ((BLK, TILE, TILE), BF16)

    message = ((INC, TILE), BF16)
    note = ((3 * INC + TILE, TILE), BF16)
    partial, inner, outer = call(
        far_up_body,
        [((targets, INC * RANK), BF16), message, message],
        (currents, primal_compress, primal_coupling) + lists,
        scratch=far_scratch(tiles),
        held=(2, 0, 1, 3, 4, 5),
        name="far_up",
    )
    arrived = exchange(partial, surf_count)
    inner, outer = swap(inner, outer, surf_count)
    lower, upper, expanded = call(
        products_body,
        [cube, cube, ((BLK, RANK, TILE), BF16)],
        (gram_inverse, gram_lower, gram_upper, primal_expand),
        held=(0, 1, 2, 3),
        flops=PRODUCT_COST,
        name="products",
    )
    (near_part,) = call(
        near_body,
        [((INC, NP_DEV), F32)],
        (near_target, near_source, currents, inner, outer, gram_inverse, near_tiles),
        scratch=[
            pltpu.VMEM((BLK + 2, INC, TILE), BF16),
            pltpu.VMEM((BLK, INC, TILE), F32),
            pltpu.VMEM((near_count, INC, TILE), F32),
            pltpu.VMEM((2,) + message[0], BF16),
            pltpu.VMEM(near_tiles.shape, BF16),
            pltpu.SemaphoreType.DMA((near_count // NEAR_CHUNK,)),
        ],
        held=(2, 0, 1, 5),
        far=(6,),
        small=(0, 1),
        flops=NEAR_COST,
        name="near",
    )
    start, after, inner_note, outer_note = call(
        solve_body,
        [((INC, NP_DEV), F32)] * 2 + [note] * 2,
        (arrived, near_part, expanded, lower, upper),
        scratch=[
            pltpu.VMEM((2,) + note[0], BF16),
            pltpu.VMEM((BLK * INC, INC * RANK), BF16),
        ],
        name="solve",
    )
    inner_note, outer_note = swap(inner_note, outer_note, surf_count)
    rows = INC + IDX_ROWS
    high, hot, bounds, index_rows = call(
        order_body,
        [
            ((BLK, TILE), I32), ((NP_DEV, TILE), BF16), ((surf_count, 2), I32),
            ((IDX_ROWS, NP_DEV), BF16),
        ],
        (dual_owner.reshape(1, NP_DEV), dual_index.reshape(1, NP_DEV)),
        scratch=[pltpu.VMEM((BLK, TILE), F32)],
        held=(0, 1),
        flops=10**9,
        name="order",
    )
    second, third = call(
        middle_body,
        [((INC, NP_DEV), F32)] * 2,
        (start, after, lower, upper),
        flops=10**9,
        name="middle",
    )
    (send,) = call(
        finish_body,
        [((surf_count, INC * pieces + TAIL, LANES), BF16)],
        (
            start, after, second, third, inner_note, outer_note, lower, upper,
            refine_weight.reshape(1, NP_DEV), index_rows, high, hot, bounds,
        ),
        scratch=[
            pltpu.VMEM((2,) + note[0], BF16),
            pltpu.VMEM((BLK * rows, NP_DEV), BF16),
            pltpu.VMEM((rows, NP_DEV + (pieces + 1) * LANES), F32),
        ],
        smem=(12,),
        held=(8,),
        name="finish",
    )
    shares = lax.all_to_all(send, "surf", split_axis=0, concat_axis=0, tiled=True)
    slots = surf_count * pieces * LANES
    couple, compress = call(
        couple_body,
        [((BLK * RANK, targets * RANK), BF16), (dual_compress.shape, BF16)],
        (dual_coupling,) + lists + (dual_compress,),
        scratch=[pltpu.VMEM((targets, RANK, BLK * RANK), F32), pltpu.VMEM((tiles, INC * RANK), F32)],
        held=(0, 1, 2, 3, 4),
        small=(1, 2, 3),
        flops=10**10,
        name="couple",
    )
    field, partial = call(
        gather_body,
        [((BLK, INC, TILE), BF16), ((surf_count, INC, BLK * RANK), BF16)],
        (shares, compress, couple),
        scratch=[
            pltpu.VMEM((surf_count * pieces, LANES), F32),
            pltpu.VMEM((BLK * INC, slots), BF16),
            pltpu.VMEM((slots, TILE), BF16),
        ],
        name="gather",
    )
    arrived = lax.all_to_all(partial, "surf", split_axis=0, concat_axis=0, tiled=True)
    near_dual, expand = call(
        self_body,
        [((INC, NP_DEV), F32), (dual_expand.shape, BF16)],
        (field, dual_self, dual_expand),
        held=(2, 1),
        name="self_part",
    )
    (response,) = call(
        answer_body,
        [((INC, NP_DEV), BF16)],
        (arrived, near_dual, expand),
        scratch=[pltpu.VMEM((BLK * INC, BLK * RANK), BF16)],
        name="answer",
    )
    return response


def solution(mesh):
    both = ("groups", "surf")
    row, flat = P(None, both), P(both)
    cube, flat2 = P(both, None, None), P(both, None)
    return jax.shard_map(
        shards,
        mesh=mesh,
        in_specs=(
            row, cube, flat, flat, cube, cube, flat2, flat, flat2, flat, cube, cube, cube, flat,
            flat2, flat, cube, cube, cube, flat2,
        ),
        out_specs=row,
        check_vma=False,
    )
```

```python
import jax
import jax.numpy as jnp
from jax import lax
from jax.experimental import pallas as pl
from jax.experimental.pallas import tpu as pltpu
from jax.sharding import PartitionSpec as P

TILE = 256
INC = 32
RANK = 32
BLK = 8
NP_DEV = 2048
LANES = 128
IDX_ROWS = 16
TAIL = 8
NEAR_CHUNK = 8
F32 = jnp.float32
BF16 = jnp.bfloat16
I32 = jnp.int32
NT = (((1,), (1,)), ((), ()))
VMEM_LIMIT = 36 * 1024 * 1024


def dot(a, b):
    return jnp.dot(a, b, preferred_element_type=F32)


def dot_nt(a, b):
    return lax.dot_general(a, b, NT, preferred_element_type=F32)


def iota(shape, dim):
    return lax.broadcasted_iota(I32, shape, dim)


def block(array, i):
    return array[:, i * TILE : (i + 1) * TILE]


def as_hot(mask):
    return mask.astype(F32).astype(BF16)


def call(body, outs, args, scratch=(), smem=(), held=(), far=(), small=(), streamed=(), flops=0, name=None):
    spaces = [
        pltpu.SMEM if k in smem else pltpu.HBM if k in held or k in far else pltpu.VMEM
        for k in range(len(args))
    ]
    size = sum(a.size * a.dtype.itemsize for a in args)
    outs = tuple(
        jax.ShapeDtypeStruct(s, d) for s, d in outs
    )
    buffers = [
        (pltpu.SMEM if k in small else pltpu.VMEM)(args[k].shape, args[k].dtype) for k in held
    ]
    waits = [pltpu.SemaphoreType.DMA(()) for _ in held]

    def wrapped(*refs):
        ins = list(refs[: len(args)])
        rest = refs[len(args) : len(refs) - 2 * len(held)]
        extra = refs[len(refs) - 2 * len(held) :]
        for n, k in enumerate(held):
            ins[k] = pltpu.make_async_copy(ins[k], extra[n], extra[len(held) + n])
            ins[k].start()
            ins[k] = (ins[k], extra[n])
        body(*ins, *rest)

    return pl.pallas_call(
        wrapped,
        out_shape=outs,
        in_specs=[pl.BlockSpec(memory_space=m) for m in spaces],
        out_specs=tuple(
            pl.BlockSpec(memory_space=pl.ANY if k in streamed else pltpu.VMEM)
            for k in range(len(outs))
        ),
        scratch_shapes=list(scratch) + buffers + waits,
        compiler_params=pltpu.CompilerParams(vmem_limit_bytes=VMEM_LIMIT),
        cost_estimate=pl.CostEstimate(flops=flops, bytes_accessed=size, transcendentals=0),
        name=name,
    )(*[pltpu.with_memory_space_constraint(a, m) if m is pltpu.HBM else a for a, m in zip(args, spaces)])


def ready(operand):
    operand[0].wait()
    return operand[1]


def fill_hot(hot, columns):
    height, count = columns.shape
    columns = columns.astype(BF16)
    lane = iota((height, TILE), 1).astype(F32).astype(BF16)
    one, zero = jnp.ones((height, TILE), BF16), jnp.zeros((height, TILE), BF16)
    for k in range(count):
        hot[k * height : (k + 1) * height, :] = jnp.where(lane == columns[:, k : k + 1], one, zero)


def coefficients(blocks, compress):
    width = BLK * RANK
    every = dot_nt(blocks, compress[...].reshape(width, TILE))
    owner = iota((INC, width), 1) // RANK
    coef = jnp.zeros((INC, width), F32)
    for s in range(BLK):
        coef = jnp.where(owner == s, every[s * INC : (s + 1) * INC], coef)
    return coef


def far_up_body(
    value, compress, coupling, source, owner, place,
    out_ref, blocks, turned, spread, pick, terms,
):
    coupling = ready(coupling)
    turned[...] = coupling[...].astype(F32).T
    value, compress = ready(value), ready(compress)
    for s in range(BLK):
        blocks[s * INC : (s + 1) * INC, :] = block(value, s)
    coef = coefficients(blocks[...], compress)
    width = BLK * RANK
    keep = (iota((RANK, width), 1) % RANK) == iota((RANK, width), 0)
    for i in range(INC):
        spread[i * RANK : (i + 1) * RANK, :] = jnp.where(keep, coef[i : i + 1, :], 0.0).astype(BF16)
    source = ready(source)
    tiles = source.shape[1]
    pick[...] = dot(spread[...], as_hot((iota((width, tiles), 0) // RANK) == source[...]))

    def step(pair, carry):
        rows = pl.multiple_of(pair * (2 * RANK), 2 * RANK)
        got = pick[pl.ds(rows, 2 * RANK), :]
        first = jnp.zeros((RANK, tiles), F32)
        second = jnp.zeros((RANK, tiles), F32)
        for r in range(RANK):
            factor = turned[r * RANK : (r + 1) * RANK, :]
            first += got[r : r + 1, :] * factor
            second += got[RANK + r : RANK + r + 1, :] * factor
        terms[pl.ds(rows, 2 * RANK), :] = jnp.concatenate([first, second], axis=0).astype(BF16)
        return carry

    lax.fori_loop(0, INC // 2, step, 0)
    targets = out_ref.shape[0]
    owner, place = ready(owner), ready(place)
    select = as_hot(iota((targets, tiles), 0) == owner[...] * BLK + place[...])
    out_ref[...] = dot_nt(select, terms[...]).astype(BF16)


def far_scratch(tiles):
    return [
        pltpu.VMEM((BLK * INC, TILE), BF16),
        pltpu.VMEM((RANK * RANK, tiles), F32),
        pltpu.VMEM((INC * RANK, BLK * RANK), BF16),
        pltpu.VMEM((INC * RANK, tiles), F32),
        pltpu.VMEM((INC * RANK, tiles), BF16),
    ]


def far_sums(arrived_ref, spread):
    rows = arrived_ref.shape[0]
    total = jnp.sum(arrived_ref[...].astype(F32).reshape(rows // BLK, BLK, INC * RANK), axis=0)
    width = INC * RANK
    keep = (iota((INC, width), 1) // RANK) == iota((INC, width), 0)
    for b in range(BLK):
        spread[b * INC : (b + 1) * INC, :] = jnp.where(keep, total[b : b + 1, :], 0.0).astype(BF16)
    fold = as_hot((iota((width, RANK), 0) % RANK) == iota((width, RANK), 1))
    return dot(spread[...], fold).astype(BF16)


def order_body(owner, index, high_out, hot_out, bounds_out, rows_out, ranks):
    owner, index = ready(owner), ready(index)
    owners = bounds_out.shape[0]
    pieces = -(-max(2, 2 * NP_DEV // owners) // LANES)
    before = as_hot(iota((TILE, TILE), 0) < iota((TILE, TILE), 1))
    number = iota((owners, TILE), 0)
    count = jnp.zeros((owners, 1), F32)
    begin = jnp.zeros((owners, 1), F32)
    hots, carries = [], []
    for c in range(BLK):
        names = block(owner, c)
        hot = (number == names).astype(F32)
        hots.append(hot)
        carries.append(count)
        count = count + jnp.sum(hot, axis=1, keepdims=True)
        begin = begin + jnp.sum((names < number).astype(F32), axis=1, keepdims=True)
    for c in range(BLK):
        rank = dot(hots[c].astype(BF16), before)
        ranks[c : c + 1, :] = jnp.sum(hots[c] * (rank + carries[c] + begin), axis=0, keepdims=True)
    spots = ranks[...].astype(I32)
    high_out[...] = spots // TILE
    fill_hot(hot_out, (spots % TILE).astype(F32).T)
    pair = iota((owners, 2), 1)
    bounds_out[...] = jnp.where(pair == 0, begin, count).astype(I32)
    row = iota((IDX_ROWS, NP_DEV), 0)
    index = index[...]
    digits = jnp.where(row % 2 == 0, index // TILE, index % TILE)
    rows_out[...] = jnp.where(row < 2 * pieces, digits, 0).astype(F32).astype(BF16)


def prepare_body(
    target, origin, own, inner_ref, outer_ref, inverse, lower, upper, expand, tiles_ref,
    near_out, lower_out, upper_out, expand_out, cells, total, products, pair, tiles, arrivals,
):
    count = tiles_ref.shape[0]
    copies = []
    for c in range(count // NEAR_CHUNK):
        part = pl.ds(c * NEAR_CHUNK, NEAR_CHUNK)
        copy = pltpu.make_async_copy(tiles_ref.at[part], tiles.at[part], arrivals.at[c])
        copy.start()
        copies.append(copy)
    position = lax.axis_index("surf")
    odd = position % 2
    pair[0] = inner_ref[...]
    pair[1] = outer_ref[...]
    cells[0] = pair[1 - odd, :, NP_DEV - TILE :]
    cells[BLK + 1] = pair[odd, :, :TILE]
    inverse, lower, upper, expand = ready(inverse), ready(lower), ready(upper), ready(expand)
    for b in range(BLK):
        lower_out[b] = dot(lower[b], inverse[b]).astype(BF16)
        upper_out[b] = dot(upper[b], inverse[b]).astype(BF16)
        expand_out[b] = dot(expand[b], inverse[b]).astype(BF16)
    own, target, origin = ready(own), ready(target), ready(origin)
    for b in range(BLK):
        cells[b + 1] = block(own, b)
    total[...] = jnp.zeros_like(total)
    start = position * BLK - 1
    for c, copy in enumerate(copies):
        copy.wait()
        for k in range(c * NEAR_CHUNK, (c + 1) * NEAR_CHUNK):
            products[k] = dot(cells[origin[k] - start], tiles[k])
    for k in range(count):
        total[target[k]] += products[k]
    for b in range(BLK):
        near_out[:, b * TILE : (b + 1) * TILE] = dot(total[b].astype(BF16), inverse[b])


def solve_body(
    arrived_ref, near_ref, expand_ref, lower_ref, upper_ref,
    start_out, next_out, inner_out, outer_out, notes, spread,
):
    sums = far_sums(arrived_ref, spread)
    start, low = [], []
    for b in range(BLK):
        value = block(near_ref, b) + dot(sums[b * INC : (b + 1) * INC, :], expand_ref[b])
        start.append(value)
        low.append(value.astype(BF16))
        start_out[:, b * TILE : (b + 1) * TILE] = value
    after = []
    for b in range(BLK):
        value = start[b]
        if b > 0:
            value = value - dot(low[b - 1], lower_ref[b])
        if b < BLK - 1:
            value = value - dot(low[b + 1], upper_ref[b])
        after.append(value)
        next_out[:, b * TILE : (b + 1) * TILE] = value
    last = BLK - 1
    odd = lax.axis_index("surf") % 2
    for n, (edge, inside, away, back) in enumerate(
        ((last, last - 1, lower_ref, upper_ref), (0, 1, upper_ref, lower_ref))
    ):
        feedless = start[edge] - dot(after[inside].astype(BF16), away[edge])
        notes[n, 0:INC, :] = low[edge]
        notes[n, INC : 2 * INC, :] = after[edge].astype(BF16)
        notes[n, 2 * INC : 3 * INC, :] = feedless.astype(BF16)
        notes[n, 3 * INC :, :] = back[edge]
    inner_out[...] = notes[odd]
    outer_out[...] = notes[1 - odd]


def middle_body(start_ref, next_ref, lower_ref, upper_ref, second_out, third_out):
    last = BLK - 1
    now = [block(next_ref, b).astype(BF16) for b in range(BLK)]
    second = []
    for b in range(BLK):
        value = block(start_ref, b)
        if b > 1:
            value = value - dot(now[b - 1], lower_ref[b])
        if b < last - 1:
            value = value - dot(now[b + 1], upper_ref[b])
        second.append(value.astype(BF16))
        second_out[:, b * TILE : (b + 1) * TILE] = value
    for b in range(BLK):
        value = block(start_ref, b)
        if 2 < b < last:
            value = value - dot(second[b - 1], lower_ref[b])
        if 0 < b < last - 2:
            value = value - dot(second[b + 1], upper_ref[b])
        third_out[:, b * TILE : (b + 1) * TILE] = value


def finish_body(
    start_ref, next_ref, second_ref, third_ref, inner_note, outer_note, lower_ref, upper_ref,
    weight, index_rows, high_ref, hot_ref, bounds_ref, send_ref,
    notes, spread, ordered, stage, sent,
):
    position = lax.axis_index("surf")
    odd = position % 2
    notes[0] = inner_note[...]
    notes[1] = outer_note[...]
    then = [block(third_ref, b) for b in range(BLK)]
    for left in (True, False):
        n = 1 - odd if left else odd
        exists = (position > 0) if left else (position < lax.axis_size("surf") - 1)
        exists = exists.astype(F32)
        edge, step = (0, 1) if left else (BLK - 1, -1)
        toward, away = (lower_ref, upper_ref) if left else (upper_ref, lower_ref)
        one, two = edge + step, edge + 2 * step
        first = block(start_ref, edge).astype(BF16)
        beyond = notes[n, 3 * INC :, :]
        beside = notes[n, INC : 2 * INC, :].astype(F32) - dot(first, beyond)
        beside = (beside * exists).astype(BF16)
        now = block(next_ref, edge) - dot(notes[n, 0:INC, :], toward[edge]) * exists
        now = now.astype(BF16)
        beside_next = notes[n, 2 * INC : 3 * INC, :].astype(F32) - dot(now, beyond)
        beside_next = (beside_next * exists).astype(BF16)
        second = (block(second_ref, edge) - dot(beside, toward[edge])).astype(BF16)
        second_one = (block(second_ref, one) - dot(now, toward[one])).astype(BF16)
        then[edge] = then[edge] - dot(beside_next, toward[edge]) - dot(second_one, away[edge])
        then[one] = then[one] - dot(second, toward[one])
        then[two] = then[two] - dot(second_one, toward[two])
    weight = ready(weight)
    rows = INC + IDX_ROWS
    for b in range(BLK):
        solved = then[b].astype(BF16).astype(F32)
        shares = solved * block(weight, b)
        every = jnp.concatenate([shares.astype(BF16), block(index_rows, b)], axis=0)
        high = high_ref[b : b + 1, :].astype(F32).astype(BF16)
        for h in range(BLK):
            spread[h * rows : (h + 1) * rows, b * TILE : (b + 1) * TILE] = jnp.where(
                high == h, every, jnp.zeros_like(every)
            )
    sorted_rows = dot(spread[...], hot_ref[...])
    for h in range(BLK):
        ordered[:, h * TILE : (h + 1) * TILE] = sorted_rows[h * rows : (h + 1) * rows]
    owners = send_ref.shape[0]
    pieces = (send_ref.shape[1] - TAIL) // INC
    wide = (pieces + 1) * LANES
    ordered[:, NP_DEV:] = jnp.zeros((rows, ordered.shape[1] - NP_DEV), F32)
    row = iota((TAIL, LANES), 0)
    slot = iota((TAIL, LANES), 1) + (row // 2) * LANES
    for o in range(owners):
        begin = bounds_ref[o, 0]
        base = pl.multiple_of((begin // LANES) * LANES, LANES)
        piece = pltpu.roll(ordered[:, pl.ds(base, wide)], wide - (begin - base), 1)
        parts = [piece[:INC, j * LANES : (j + 1) * LANES] for j in range(pieces)]
        tail = piece[INC : INC + TAIL, :LANES]
        for j in range(1, pieces):
            tail = jnp.where(row // 2 == j, piece[INC : INC + TAIL, j * LANES : (j + 1) * LANES], tail)
        tail = jnp.where(slot >= bounds_ref[o, 1], -16.0, tail)
        stage[o] = jnp.concatenate(parts + [tail], axis=0).astype(BF16)
        pltpu.make_async_copy(stage.at[o], send_ref.at[o], sent.at[o]).start()
    for o in range(owners):
        pltpu.make_async_copy(stage.at[o], send_ref.at[o], sent.at[o]).wait()


def gather_body(
    arrived_ref, compress, couple_ref, field_out, out_ref, index, spread, hot, stage, sent,
):
    owners, rows, _ = arrived_ref.shape
    pieces = (rows - TAIL) // INC
    for e in range(owners):
        tail = arrived_ref[e].astype(F32)[INC * pieces :]
        marks = tail.astype(BF16)
        for j in range(pieces):
            k = e * pieces + j
            part = arrived_ref[e, j * INC : (j + 1) * INC, :]
            high = marks[2 * j : 2 * j + 1]
            index[k : k + 1, :] = tail[2 * j + 1 : 2 * j + 2]
            for h in range(BLK):
                spread[h * INC : (h + 1) * INC, k * LANES : (k + 1) * LANES] = jnp.where(
                    high == h, part, jnp.zeros_like(part)
                )
    fill_hot(hot, index[...].T)
    field = dot(spread[...], hot[...]).astype(BF16)
    for b in range(BLK):
        field_out[b] = field[b * INC : (b + 1) * INC]
    coef = coefficients(field, compress).astype(BF16)
    for o in range(out_ref.shape[0]):
        stage[o] = dot(coef, block(couple_ref, o)).astype(BF16)
        pltpu.make_async_copy(stage.at[o], out_ref.at[o], sent.at[o]).start()
    for o in range(out_ref.shape[0]):
        pltpu.make_async_copy(stage.at[o], out_ref.at[o], sent.at[o]).wait()


def couple_body(coupling, source, owner, place, basis, out_ref, basis_out, total, lanes):
    tiles, width = lanes.shape[0], BLK * RANK
    flat = RANK * RANK
    total[...] = jnp.zeros_like(total)
    coupling = ready(coupling)
    lanes[...] = coupling[...].astype(F32)
    keep = (iota((RANK, flat), 1) % RANK) == iota((RANK, flat), 0)
    fold = as_hot((iota((flat, width), 0) // RANK) == (iota((flat, width), 1) % RANK))
    number = iota((RANK, width), 1) // RANK
    source, owner, place = ready(source), ready(owner), ready(place)
    group = 8

    def step(c, carry):
        begin = pl.multiple_of(c * group, group)
        rows = lanes[pl.ds(begin, group), :]
        tall = [jnp.where(keep, rows[k : k + 1], 0.0).astype(BF16) for k in range(group)]
        turned = dot(jnp.concatenate(tall, axis=0), fold)
        for k in range(group):
            f = begin + k
            tile = jnp.where(number == source[0, f], turned[k * RANK : (k + 1) * RANK], 0.0)
            total[owner[0, f] * BLK + place[0, f]] += tile
        return carry

    lax.fori_loop(0, tiles // group, step, 0)
    for o in range(out_ref.shape[1] // TILE):
        part = total[o * BLK : (o + 1) * BLK].reshape(TILE, width)
        out_ref[:, o * TILE : (o + 1) * TILE] = part.T.astype(BF16)
    basis_out[...] = ready(basis)[...]


def self_body(field_ref, tiles, basis, out_ref, basis_out):
    basis_out[...] = ready(basis)[...]
    tiles = ready(tiles)
    for b in range(BLK):
        out_ref[:, b * TILE : (b + 1) * TILE] = dot(field_ref[b], tiles[b])


def answer_body(arrived_ref, near_ref, expand, out_ref, spread):
    total = jnp.sum(arrived_ref[...].astype(F32), axis=0)
    number = iota(total.shape, 1) // RANK
    for b in range(BLK):
        spread[b * INC : (b + 1) * INC, :] = jnp.where(number == b, total, 0.0).astype(BF16)
    far = dot(spread[...], expand[...].reshape(BLK * RANK, TILE))
    for b in range(BLK):
        out_ref[:, b * TILE : (b + 1) * TILE] = (
            block(near_ref, b) + far[b * INC : (b + 1) * INC]
        ).astype(BF16)


def swap(inner, outer, surf_count):
    pairs = [(i, i ^ 1) for i in range(surf_count)]
    others = [(0, 0), (surf_count - 1, surf_count - 1)]
    for i in range(1, surf_count - 1, 2):
        others += [(i, i + 1), (i + 1, i)]
    return lax.ppermute(inner, "surf", pairs), lax.ppermute(outer, "surf", others)


def exchange(array, surf_count):
    shape = array.shape
    array = array.reshape((surf_count, shape[0] // surf_count) + shape[1:])
    array = lax.all_to_all(array, "surf", split_axis=0, concat_axis=0, tiled=True)
    return array.reshape(shape)


def shards(
    currents, near_tiles, near_target, near_source, primal_compress, primal_expand, primal_coupling,
    far_source, far_owner, far_block, gram_inverse, gram_lower, gram_upper, refine_weight,
    dual_owner, dual_index, dual_self, dual_compress, dual_expand, dual_coupling,
):
    surf_count = lax.axis_size("surf")
    tiles = far_source.shape[0]
    near_count = near_tiles.shape[0]
    targets = surf_count * BLK
    capacity = max(2, 2 * NP_DEV // surf_count)
    pieces = -(-capacity // LANES)
    lists = (far_source.reshape(1, tiles), far_owner.reshape(1, tiles), far_block.reshape(1, tiles))
    cube = ((BLK, TILE, TILE), BF16)

    note = ((3 * INC + TILE, TILE), BF16)
    inner, outer = swap(currents, currents, surf_count)
    (partial,) = call(
        far_up_body,
        [((targets, INC * RANK), BF16)],
        (currents, primal_compress, primal_coupling) + lists,
        scratch=far_scratch(tiles),
        held=(2, 0, 1, 3, 4, 5),
        flops=10**11,
        name="far_up",
    )
    arrived = exchange(partial, surf_count)
    near_part, lower, upper, expanded = call(
        prepare_body,
        [((INC, NP_DEV), F32), cube, cube, ((BLK, RANK, TILE), BF16)],
        (
            near_target, near_source, currents, inner, outer, gram_inverse, gram_lower, gram_upper,
            primal_expand, near_tiles,
        ),
        scratch=[
            pltpu.VMEM((BLK + 2, INC, TILE), BF16),
            pltpu.VMEM((BLK, INC, TILE), F32),
            pltpu.VMEM((near_count, INC, TILE), F32),
            pltpu.VMEM((2,) + currents.shape, BF16),
            pltpu.VMEM(near_tiles.shape, BF16),
            pltpu.SemaphoreType.DMA((near_count // NEAR_CHUNK,)),
        ],
        held=(5, 6, 7, 8, 2, 0, 1),
        far=(9,),
        small=(0, 1),
        flops=10**11,
        name="prepare",
    )
    start, after, inner_note, outer_note = call(
        solve_body,
        [((INC, NP_DEV), F32)] * 2 + [note] * 2,
        (arrived, near_part, expanded, lower, upper),
        scratch=[
            pltpu.VMEM((2,) + note[0], BF16),
            pltpu.VMEM((BLK * INC, INC * RANK), BF16),
        ],
        name="solve",
    )
    inner_note, outer_note = swap(inner_note, outer_note, surf_count)
    rows = INC + IDX_ROWS
    high, hot, bounds, index_rows = call(
        order_body,
        [
            ((BLK, TILE), I32), ((NP_DEV, TILE), BF16), ((surf_count, 2), I32),
            ((IDX_ROWS, NP_DEV), BF16),
        ],
        (dual_owner.reshape(1, NP_DEV), dual_index.reshape(1, NP_DEV)),
        scratch=[pltpu.VMEM((BLK, TILE), F32)],
        held=(0, 1),
        flops=10**9,
        name="order",
    )
    second, third = call(
        middle_body,
        [((INC, NP_DEV), F32)] * 2,
        (start, after, lower, upper),
        flops=10**9,
        name="middle",
    )
    (send,) = call(
        finish_body,
        [((surf_count, INC * pieces + TAIL, LANES), BF16)],
        (
            start, after, second, third, inner_note, outer_note, lower, upper,
            refine_weight.reshape(1, NP_DEV), index_rows, high, hot, bounds,
        ),
        scratch=[
            pltpu.VMEM((2,) + note[0], BF16),
            pltpu.VMEM((BLK * rows, NP_DEV), BF16),
            pltpu.VMEM((rows, NP_DEV + (pieces + 1) * LANES), F32),
            pltpu.VMEM((surf_count, INC * pieces + TAIL, LANES), BF16),
            pltpu.SemaphoreType.DMA((surf_count,)),
        ],
        streamed=(0,),
        smem=(12,),
        held=(8,),
        name="finish",
    )
    shares = lax.all_to_all(send, "surf", split_axis=0, concat_axis=0, tiled=True)
    slots = surf_count * pieces * LANES
    couple, compress = call(
        couple_body,
        [((BLK * RANK, targets * RANK), BF16), (dual_compress.shape, BF16)],
        (dual_coupling,) + lists + (dual_compress,),
        scratch=[pltpu.VMEM((targets, RANK, BLK * RANK), F32), pltpu.VMEM((tiles, INC * RANK), F32)],
        held=(0, 1, 2, 3, 4),
        small=(1, 2, 3),
        flops=10**10,
        name="couple",
    )
    field, partial = call(
        gather_body,
        [((BLK, INC, TILE), BF16), ((surf_count, INC, BLK * RANK), BF16)],
        (shares, compress, couple),
        scratch=[
            pltpu.VMEM((surf_count * pieces, LANES), F32),
            pltpu.VMEM((BLK * INC, slots), BF16),
            pltpu.VMEM((slots, TILE), BF16),
            pltpu.VMEM((surf_count, INC, BLK * RANK), BF16),
            pltpu.SemaphoreType.DMA((surf_count,)),
        ],
        streamed=(1,),
        name="gather",
    )
    arrived = lax.all_to_all(partial, "surf", split_axis=0, concat_axis=0, tiled=True)
    near_dual, expand = call(
        self_body,
        [((INC, NP_DEV), F32), (dual_expand.shape, BF16)],
        (field, dual_self, dual_expand),
        held=(2, 1),
        name="self_part",
    )
    (response,) = call(
        answer_body,
        [((INC, NP_DEV), BF16)],
        (arrived, near_dual, expand),
        scratch=[pltpu.VMEM((BLK * INC, BLK * RANK), BF16)],
        name="answer",
    )
    return response


def solution(mesh):
    both = ("groups", "surf")
    row, flat = P(None, both), P(both)
    cube, flat2 = P(both, None, None), P(both, None)
    return jax.shard_map(
        shards,
        mesh=mesh,
        in_specs=(
            row, cube, flat, flat, cube, cube, flat2, flat, flat2, flat, cube, cube, cube, flat,
            flat2, flat, cube, cube, cube, flat2,
        ),
        out_specs=row,
        check_vma=False,
    )
```

```python
import jax
import jax.numpy as jnp
from jax import lax
from jax.experimental import pallas as pl
from jax.experimental.pallas import tpu as pltpu
from jax.sharding import PartitionSpec as P

TILE = 256
INC = 32
RANK = 32
BLK = 8
NP_DEV = 2048
LANES = 128
IDX_ROWS = 16
TAIL = 8
NEAR_CHUNK = 8
F32 = jnp.float32
BF16 = jnp.bfloat16
I32 = jnp.int32
NT = (((1,), (1,)), ((), ()))
VMEM_LIMIT = 36 * 1024 * 1024


def dot(a, b):
    return jnp.dot(a, b, preferred_element_type=F32)


def dot_nt(a, b):
    return lax.dot_general(a, b, NT, preferred_element_type=F32)


def iota(shape, dim):
    return lax.broadcasted_iota(I32, shape, dim)


def block(array, i):
    return array[:, i * TILE : (i + 1) * TILE]


def as_hot(mask):
    return mask.astype(F32).astype(BF16)


def call(body, outs, args, scratch=(), smem=(), held=(), far=(), small=(), streamed=(), flops=0, name=None):
    spaces = [
        pltpu.SMEM if k in smem else pltpu.HBM if k in held or k in far else pltpu.VMEM
        for k in range(len(args))
    ]
    size = sum(a.size * a.dtype.itemsize for a in args)
    outs = tuple(
        jax.ShapeDtypeStruct(s, d) for s, d in outs
    )
    buffers = [
        (pltpu.SMEM if k in small else pltpu.VMEM)(args[k].shape, args[k].dtype) for k in held
    ]
    waits = [pltpu.SemaphoreType.DMA(()) for _ in held]

    def wrapped(*refs):
        ins = list(refs[: len(args)])
        rest = refs[len(args) : len(refs) - 2 * len(held)]
        extra = refs[len(refs) - 2 * len(held) :]
        for n, k in enumerate(held):
            ins[k] = pltpu.make_async_copy(ins[k], extra[n], extra[len(held) + n])
            ins[k].start()
            ins[k] = (ins[k], extra[n])
        body(*ins, *rest)

    return pl.pallas_call(
        wrapped,
        out_shape=outs,
        in_specs=[pl.BlockSpec(memory_space=m) for m in spaces],
        out_specs=tuple(
            pl.BlockSpec(memory_space=pl.ANY if k in streamed else pltpu.VMEM)
            for k in range(len(outs))
        ),
        scratch_shapes=list(scratch) + buffers + waits,
        compiler_params=pltpu.CompilerParams(vmem_limit_bytes=VMEM_LIMIT),
        cost_estimate=pl.CostEstimate(flops=flops, bytes_accessed=size, transcendentals=0),
        name=name,
    )(*[pltpu.with_memory_space_constraint(a, m) if m is pltpu.HBM else a for a, m in zip(args, spaces)])


def ready(operand):
    operand[0].wait()
    return operand[1]


def fill_hot(hot, columns):
    height, count = columns.shape
    columns = columns.astype(BF16)
    lane = iota((height, TILE), 1).astype(F32).astype(BF16)
    one, zero = jnp.ones((height, TILE), BF16), jnp.zeros((height, TILE), BF16)
    for k in range(count):
        hot[k * height : (k + 1) * height, :] = jnp.where(lane == columns[:, k : k + 1], one, zero)


def coefficients(blocks, compress):
    width = BLK * RANK
    every = dot_nt(blocks, compress[...].reshape(width, TILE))
    owner = iota((INC, width), 1) // RANK
    coef = jnp.zeros((INC, width), F32)
    for s in range(BLK):
        coef = jnp.where(owner == s, every[s * INC : (s + 1) * INC], coef)
    return coef


def far_up_body(
    value, compress, coupling, source, owner, place,
    out_ref, blocks, turned, spread, pick, terms,
):
    coupling = ready(coupling)
    turned[...] = coupling[...].astype(F32).T
    value, compress = ready(value), ready(compress)
    for s in range(BLK):
        blocks[s * INC : (s + 1) * INC, :] = block(value, s)
    coef = coefficients(blocks[...], compress)
    width = BLK * RANK
    keep = (iota((RANK, width), 1) % RANK) == iota((RANK, width), 0)
    for i in range(INC):
        spread[i * RANK : (i + 1) * RANK, :] = jnp.where(keep, coef[i : i + 1, :], 0.0).astype(BF16)
    source = ready(source)
    tiles = source.shape[1]
    pick[...] = dot(spread[...], as_hot((iota((width, tiles), 0) // RANK) == source[...]))

    def step(pair, carry):
        rows = pl.multiple_of(pair * (2 * RANK), 2 * RANK)
        got = pick[pl.ds(rows, 2 * RANK), :]
        first = jnp.zeros((RANK, tiles), F32)
        second = jnp.zeros((RANK, tiles), F32)
        for r in range(RANK):
            factor = turned[r * RANK : (r + 1) * RANK, :]
            first += got[r : r + 1, :] * factor
            second += got[RANK + r : RANK + r + 1, :] * factor
        terms[pl.ds(rows, 2 * RANK), :] = jnp.concatenate([first, second], axis=0).astype(BF16)
        return carry

    lax.fori_loop(0, INC // 2, step, 0)
    targets = out_ref.shape[0]
    owner, place = ready(owner), ready(place)
    select = as_hot(iota((targets, tiles), 0) == owner[...] * BLK + place[...])
    out_ref[...] = dot_nt(select, terms[...]).astype(BF16)


def far_scratch(tiles):
    return [
        pltpu.VMEM((BLK * INC, TILE), BF16),
        pltpu.VMEM((RANK * RANK, tiles), F32),
        pltpu.VMEM((INC * RANK, BLK * RANK), BF16),
        pltpu.VMEM((INC * RANK, tiles), F32),
        pltpu.VMEM((INC * RANK, tiles), BF16),
    ]


def far_sums(arrived_ref, spread):
    rows = arrived_ref.shape[0]
    total = jnp.sum(arrived_ref[...].astype(F32).reshape(rows // BLK, BLK, INC * RANK), axis=0)
    width = INC * RANK
    keep = (iota((INC, width), 1) // RANK) == iota((INC, width), 0)
    for b in range(BLK):
        spread[b * INC : (b + 1) * INC, :] = jnp.where(keep, total[b : b + 1, :], 0.0).astype(BF16)
    fold = as_hot((iota((width, RANK), 0) % RANK) == iota((width, RANK), 1))
    return dot(spread[...], fold).astype(BF16)


def order_body(owner, index, weight, high_out, hot_out, bounds_out, rows_out, weight_out, ranks):
    owner, index = ready(owner), ready(index)
    owners = bounds_out.shape[0]
    pieces = -(-max(2, 2 * NP_DEV // owners) // LANES)
    before = as_hot(iota((TILE, TILE), 0) < iota((TILE, TILE), 1))
    number = iota((owners, TILE), 0)
    count = jnp.zeros((owners, 1), F32)
    begin = jnp.zeros((owners, 1), F32)
    hots, carries = [], []
    for c in range(BLK):
        names = block(owner, c)
        hot = (number == names).astype(F32)
        hots.append(hot)
        carries.append(count)
        count = count + jnp.sum(hot, axis=1, keepdims=True)
        begin = begin + jnp.sum((names < number).astype(F32), axis=1, keepdims=True)
    for c in range(BLK):
        rank = dot(hots[c].astype(BF16), before)
        ranks[c : c + 1, :] = jnp.sum(hots[c] * (rank + carries[c] + begin), axis=0, keepdims=True)
    spots = ranks[...].astype(I32)
    high_out[...] = spots // TILE
    fill_hot(hot_out, (spots % TILE).astype(F32).T)
    pair = iota((owners, 2), 1)
    bounds_out[...] = jnp.where(pair == 0, begin, count).astype(I32)
    row = iota((IDX_ROWS, NP_DEV), 0)
    index = index[...]
    digits = jnp.where(row % 2 == 0, index // TILE, index % TILE)
    rows_out[...] = jnp.where(row < 2 * pieces, digits, 0).astype(F32).astype(BF16)
    weight_out[...] = ready(weight)[...]


def prepare_body(
    target, origin, own, inner_ref, outer_ref, inverse, lower, upper, expand, tiles_ref,
    near_out, lower_out, upper_out, expand_out, cells, total, products, pair, tiles, arrivals,
):
    count = tiles_ref.shape[0]
    copies = []
    for c in range(count // NEAR_CHUNK):
        part = pl.ds(c * NEAR_CHUNK, NEAR_CHUNK)
        copy = pltpu.make_async_copy(tiles_ref.at[part], tiles.at[part], arrivals.at[c])
        copy.start()
        copies.append(copy)
    position = lax.axis_index("surf")
    odd = position % 2
    pair[0] = inner_ref[...]
    pair[1] = outer_ref[...]
    cells[0] = pair[1 - odd, :, NP_DEV - TILE :]
    cells[BLK + 1] = pair[odd, :, :TILE]
    inverse, lower, upper, expand = ready(inverse), ready(lower), ready(upper), ready(expand)
    for b in range(BLK):
        lower_out[b] = dot(lower[b], inverse[b]).astype(BF16)
        upper_out[b] = dot(upper[b], inverse[b]).astype(BF16)
        expand_out[b] = dot(expand[b], inverse[b]).astype(BF16)
    own, target, origin = ready(own), ready(target), ready(origin)
    for b in range(BLK):
        cells[b + 1] = block(own, b)
    total[...] = jnp.zeros_like(total)
    start = position * BLK - 1
    for c, copy in enumerate(copies):
        copy.wait()
        for k in range(c * NEAR_CHUNK, (c + 1) * NEAR_CHUNK):
            products[k] = dot(cells[origin[k] - start], tiles[k])
    for k in range(count):
        total[target[k]] += products[k]
    for b in range(BLK):
        near_out[:, b * TILE : (b + 1) * TILE] = dot(total[b].astype(BF16), inverse[b])


def solve_body(
    arrived_ref, near_ref, expand_ref, lower_ref, upper_ref,
    start_out, next_out, inner_out, outer_out, notes, spread,
):
    sums = far_sums(arrived_ref, spread)
    start, low = [], []
    for b in range(BLK):
        value = block(near_ref, b) + dot(sums[b * INC : (b + 1) * INC, :], expand_ref[b])
        start.append(value)
        low.append(value.astype(BF16))
        start_out[:, b * TILE : (b + 1) * TILE] = value
    after = []
    for b in range(BLK):
        value = start[b]
        if b > 0:
            value = value - dot(low[b - 1], lower_ref[b])
        if b < BLK - 1:
            value = value - dot(low[b + 1], upper_ref[b])
        after.append(value)
        next_out[:, b * TILE : (b + 1) * TILE] = value
    last = BLK - 1
    odd = lax.axis_index("surf") % 2
    for n, (edge, inside, away, back) in enumerate(
        ((last, last - 1, lower_ref, upper_ref), (0, 1, upper_ref, lower_ref))
    ):
        feedless = start[edge] - dot(after[inside].astype(BF16), away[edge])
        notes[n, 0:INC, :] = low[edge]
        notes[n, INC : 2 * INC, :] = after[edge].astype(BF16)
        notes[n, 2 * INC : 3 * INC, :] = feedless.astype(BF16)
        notes[n, 3 * INC :, :] = back[edge]
    inner_out[...] = notes[odd]
    outer_out[...] = notes[1 - odd]


def middle_body(start_ref, next_ref, lower_ref, upper_ref, second_out, third_out):
    last = BLK - 1
    now = [block(next_ref, b).astype(BF16) for b in range(BLK)]
    second = []
    for b in range(BLK):
        value = block(start_ref, b)
        if b > 1:
            value = value - dot(now[b - 1], lower_ref[b])
        if b < last - 1:
            value = value - dot(now[b + 1], upper_ref[b])
        second.append(value.astype(BF16))
        second_out[:, b * TILE : (b + 1) * TILE] = value
    for b in range(BLK):
        value = block(start_ref, b)
        if 2 < b < last:
            value = value - dot(second[b - 1], lower_ref[b])
        if 0 < b < last - 2:
            value = value - dot(second[b + 1], upper_ref[b])
        third_out[:, b * TILE : (b + 1) * TILE] = value


def finish_body(
    start_ref, next_ref, second_ref, third_ref, inner_note, outer_note, lower_ref, upper_ref,
    weight, index_rows, high_ref, hot_ref, bounds_ref, send_ref,
    notes, spread, ordered, stage, sent,
):
    position = lax.axis_index("surf")
    odd = position % 2
    notes[0] = inner_note[...]
    notes[1] = outer_note[...]
    then = [block(third_ref, b) for b in range(BLK)]
    for left in (True, False):
        n = 1 - odd if left else odd
        exists = (position > 0) if left else (position < lax.axis_size("surf") - 1)
        exists = exists.astype(F32)
        edge, step = (0, 1) if left else (BLK - 1, -1)
        toward, away = (lower_ref, upper_ref) if left else (upper_ref, lower_ref)
        one, two = edge + step, edge + 2 * step
        first = block(start_ref, edge).astype(BF16)
        beyond = notes[n, 3 * INC :, :]
        beside = notes[n, INC : 2 * INC, :].astype(F32) - dot(first, beyond)
        beside = (beside * exists).astype(BF16)
        now = block(next_ref, edge) - dot(notes[n, 0:INC, :], toward[edge]) * exists
        now = now.astype(BF16)
        beside_next = notes[n, 2 * INC : 3 * INC, :].astype(F32) - dot(now, beyond)
        beside_next = (beside_next * exists).astype(BF16)
        second = (block(second_ref, edge) - dot(beside, toward[edge])).astype(BF16)
        second_one = (block(second_ref, one) - dot(now, toward[one])).astype(BF16)
        then[edge] = then[edge] - dot(beside_next, toward[edge]) - dot(second_one, away[edge])
        then[one] = then[one] - dot(second, toward[one])
        then[two] = then[two] - dot(second_one, toward[two])
    rows = INC + IDX_ROWS
    for b in range(BLK):
        solved = then[b].astype(BF16).astype(F32)
        shares = solved * block(weight, b)
        every = jnp.concatenate([shares.astype(BF16), block(index_rows, b)], axis=0)
        high = high_ref[b : b + 1, :].astype(F32).astype(BF16)
        for h in range(BLK):
            spread[h * rows : (h + 1) * rows, b * TILE : (b + 1) * TILE] = jnp.where(
                high == h, every, jnp.zeros_like(every)
            )
    sorted_rows = dot(spread[...], hot_ref[...])
    for h in range(BLK):
        ordered[:, h * TILE : (h + 1) * TILE] = sorted_rows[h * rows : (h + 1) * rows]
    owners = send_ref.shape[0]
    pieces = (send_ref.shape[1] - TAIL) // INC
    wide = (pieces + 1) * LANES
    ordered[:, NP_DEV:] = jnp.zeros((rows, ordered.shape[1] - NP_DEV), F32)
    row = iota((TAIL, LANES), 0)
    slot = iota((TAIL, LANES), 1) + (row // 2) * LANES
    for o in range(owners):
        begin = bounds_ref[o, 0]
        base = pl.multiple_of((begin // LANES) * LANES, LANES)
        piece = pltpu.roll(ordered[:, pl.ds(base, wide)], wide - (begin - base), 1)
        parts = [piece[:INC, j * LANES : (j + 1) * LANES] for j in range(pieces)]
        tail = piece[INC : INC + TAIL, :LANES]
        for j in range(1, pieces):
            tail = jnp.where(row // 2 == j, piece[INC : INC + TAIL, j * LANES : (j + 1) * LANES], tail)
        tail = jnp.where(slot >= bounds_ref[o, 1], -16.0, tail)
        stage[o] = jnp.concatenate(parts + [tail], axis=0).astype(BF16)
        pltpu.make_async_copy(stage.at[o], send_ref.at[o], sent.at[o]).start()
    for o in range(owners):
        pltpu.make_async_copy(stage.at[o], send_ref.at[o], sent.at[o]).wait()


def gather_body(
    arrived_ref, compress, couple_ref, field_out, coef_out, give_out, index, spread, hot,
):
    owners, rows, _ = arrived_ref.shape
    pieces = (rows - TAIL) // INC
    for e in range(owners):
        tail = arrived_ref[e].astype(F32)[INC * pieces :]
        marks = tail.astype(BF16)
        for j in range(pieces):
            k = e * pieces + j
            part = arrived_ref[e, j * INC : (j + 1) * INC, :]
            high = marks[2 * j : 2 * j + 1]
            index[k : k + 1, :] = tail[2 * j + 1 : 2 * j + 2]
            for h in range(BLK):
                spread[h * INC : (h + 1) * INC, k * LANES : (k + 1) * LANES] = jnp.where(
                    high == h, part, jnp.zeros_like(part)
                )
    fill_hot(hot, index[...].T)
    field = dot(spread[...], hot[...]).astype(BF16)
    for b in range(BLK):
        field_out[b] = field[b * INC : (b + 1) * INC]
    coef = coefficients(field, compress).astype(BF16)
    coef_out[...] = coef
    other = 1 - lax.axis_index("surf") % 2
    for c in range(give_out.shape[0]):
        give_out[c] = dot(coef, owner_columns(couple_ref, c, other)).astype(BF16)


def owner_columns(couple_ref, chip, core):
    return couple_ref[:, pl.ds(pl.multiple_of((2 * chip + core) * TILE, TILE), TILE)]


def own_body(coef_ref, couple_ref, out_ref):
    core = lax.axis_index("surf") % 2
    for c in range(out_ref.shape[0]):
        out_ref[c] = dot(coef_ref[...], owner_columns(couple_ref, c, core))


def merge_body(own_ref, got_ref, out_ref):
    out_ref[...] = (own_ref[...] + got_ref[...].astype(F32)).astype(BF16)


def couple_body(coupling, source, owner, place, basis, out_ref, basis_out, total, lanes):
    tiles, width = lanes.shape[0], BLK * RANK
    flat = RANK * RANK
    total[...] = jnp.zeros_like(total)
    coupling = ready(coupling)
    lanes[...] = coupling[...].astype(F32)
    keep = (iota((RANK, flat), 1) % RANK) == iota((RANK, flat), 0)
    fold = as_hot((iota((flat, width), 0) // RANK) == (iota((flat, width), 1) % RANK))
    number = iota((RANK, width), 1) // RANK
    source, owner, place = ready(source), ready(owner), ready(place)
    group = 8

    def step(c, carry):
        begin = pl.multiple_of(c * group, group)
        rows = lanes[pl.ds(begin, group), :]
        tall = [jnp.where(keep, rows[k : k + 1], 0.0).astype(BF16) for k in range(group)]
        turned = dot(jnp.concatenate(tall, axis=0), fold)
        for k in range(group):
            f = begin + k
            tile = jnp.where(number == source[0, f], turned[k * RANK : (k + 1) * RANK], 0.0)
            total[owner[0, f] * BLK + place[0, f]] += tile
        return carry

    lax.fori_loop(0, tiles // group, step, 0)
    for o in range(out_ref.shape[1] // TILE):
        part = total[o * BLK : (o + 1) * BLK].reshape(TILE, width)
        out_ref[:, o * TILE : (o + 1) * TILE] = part.T.astype(BF16)
    basis_out[...] = ready(basis)[...]


def self_body(field_ref, tiles, basis, out_ref, basis_out):
    basis_out[...] = ready(basis)[...]
    tiles = ready(tiles)
    for b in range(BLK):
        out_ref[:, b * TILE : (b + 1) * TILE] = dot(field_ref[b], tiles[b])


def answer_body(arrived_ref, near_ref, expand, out_ref, spread):
    total = jnp.sum(arrived_ref[...].astype(F32), axis=0)
    number = iota(total.shape, 1) // RANK
    for b in range(BLK):
        spread[b * INC : (b + 1) * INC, :] = jnp.where(number == b, total, 0.0).astype(BF16)
    far = dot(spread[...], expand[...].reshape(BLK * RANK, TILE))
    for b in range(BLK):
        out_ref[:, b * TILE : (b + 1) * TILE] = (
            block(near_ref, b) + far[b * INC : (b + 1) * INC]
        ).astype(BF16)


def swap(inner, outer, surf_count):
    pairs = [(i, i ^ 1) for i in range(surf_count)]
    others = [(0, 0), (surf_count - 1, surf_count - 1)]
    for i in range(1, surf_count - 1, 2):
        others += [(i, i + 1), (i + 1, i)]
    return lax.ppermute(inner, "surf", pairs), lax.ppermute(outer, "surf", others)


def exchange(array, surf_count):
    shape = array.shape
    array = array.reshape((surf_count, shape[0] // surf_count) + shape[1:])
    array = lax.all_to_all(array, "surf", split_axis=0, concat_axis=0, tiled=True)
    return array.reshape(shape)


def shards(
    currents, near_tiles, near_target, near_source, primal_compress, primal_expand, primal_coupling,
    far_source, far_owner, far_block, gram_inverse, gram_lower, gram_upper, refine_weight,
    dual_owner, dual_index, dual_self, dual_compress, dual_expand, dual_coupling,
):
    surf_count = lax.axis_size("surf")
    tiles = far_source.shape[0]
    near_count = near_tiles.shape[0]
    targets = surf_count * BLK
    capacity = max(2, 2 * NP_DEV // surf_count)
    pieces = -(-capacity // LANES)
    lists = (far_source.reshape(1, tiles), far_owner.reshape(1, tiles), far_block.reshape(1, tiles))
    cube = ((BLK, TILE, TILE), BF16)

    note = ((3 * INC + TILE, TILE), BF16)
    inner, outer = swap(currents, currents, surf_count)
    (partial,) = call(
        far_up_body,
        [((targets, INC * RANK), BF16)],
        (currents, primal_compress, primal_coupling) + lists,
        scratch=far_scratch(tiles),
        held=(2, 0, 1, 3, 4, 5),
        flops=10**11,
        name="far_up",
    )
    arrived = exchange(partial, surf_count)
    near_part, lower, upper, expanded = call(
        prepare_body,
        [((INC, NP_DEV), F32), cube, cube, ((BLK, RANK, TILE), BF16)],
        (
            near_target, near_source, currents, inner, outer, gram_inverse, gram_lower, gram_upper,
            primal_expand, near_tiles,
        ),
        scratch=[
            pltpu.VMEM((BLK + 2, INC, TILE), BF16),
            pltpu.VMEM((BLK, INC, TILE), F32),
            pltpu.VMEM((near_count, INC, TILE), F32),
            pltpu.VMEM((2,) + currents.shape, BF16),
            pltpu.VMEM(near_tiles.shape, BF16),
            pltpu.SemaphoreType.DMA((near_count // NEAR_CHUNK,)),
        ],
        held=(5, 6, 7, 8, 2, 0, 1),
        far=(9,),
        small=(0, 1),
        flops=10**11,
        name="prepare",
    )
    start, after, inner_note, outer_note = call(
        solve_body,
        [((INC, NP_DEV), F32)] * 2 + [note] * 2,
        (arrived, near_part, expanded, lower, upper),
        scratch=[
            pltpu.VMEM((2,) + note[0], BF16),
            pltpu.VMEM((BLK * INC, INC * RANK), BF16),
        ],
        name="solve",
    )
    inner_note, outer_note = swap(inner_note, outer_note, surf_count)
    rows = INC + IDX_ROWS
    high, hot, bounds, index_rows, weight = call(
        order_body,
        [
            ((BLK, TILE), I32), ((NP_DEV, TILE), BF16), ((surf_count, 2), I32),
            ((IDX_ROWS, NP_DEV), BF16), ((1, NP_DEV), F32),
        ],
        (
            dual_owner.reshape(1, NP_DEV), dual_index.reshape(1, NP_DEV),
            refine_weight.reshape(1, NP_DEV),
        ),
        scratch=[pltpu.VMEM((BLK, TILE), F32)],
        held=(0, 1, 2),
        flops=10**9,
        name="order",
    )
    second, third = call(
        middle_body,
        [((INC, NP_DEV), F32)] * 2,
        (start, after, lower, upper),
        flops=10**9,
        name="middle",
    )
    (send,) = call(
        finish_body,
        [((surf_count, INC * pieces + TAIL, LANES), BF16)],
        (
            start, after, second, third, inner_note, outer_note, lower, upper,
            weight, index_rows, high, hot, bounds,
        ),
        scratch=[
            pltpu.VMEM((2,) + note[0], BF16),
            pltpu.VMEM((BLK * rows, NP_DEV), BF16),
            pltpu.VMEM((rows, NP_DEV + (pieces + 1) * LANES), F32),
            pltpu.VMEM((surf_count, INC * pieces + TAIL, LANES), BF16),
            pltpu.SemaphoreType.DMA((surf_count,)),
        ],
        streamed=(0,),
        smem=(12,),
        name="finish",
    )
    shares = lax.all_to_all(send, "surf", split_axis=0, concat_axis=0, tiled=True)
    slots = surf_count * pieces * LANES
    couple, compress = call(
        couple_body,
        [((BLK * RANK, targets * RANK), BF16), (dual_compress.shape, BF16)],
        (dual_coupling,) + lists + (dual_compress,),
        scratch=[pltpu.VMEM((targets, RANK, BLK * RANK), F32), pltpu.VMEM((tiles, INC * RANK), F32)],
        held=(0, 1, 2, 3, 4),
        small=(1, 2, 3),
        flops=10**10,
        name="couple",
    )
    half = (surf_count // 2, INC, BLK * RANK)
    field, coef, give = call(
        gather_body,
        [((BLK, INC, TILE), BF16), ((INC, BLK * RANK), BF16), (half, BF16)],
        (shares, compress, couple),
        scratch=[
            pltpu.VMEM((surf_count * pieces, LANES), F32),
            pltpu.VMEM((BLK * INC, slots), BF16),
            pltpu.VMEM((slots, TILE), BF16),
        ],
        name="gather",
    )
    got = lax.ppermute(give, "surf", [(i, i ^ 1) for i in range(surf_count)])
    (own,) = call(own_body, [(half, F32)], (coef, couple), flops=10**9, name="own")
    (merged,) = call(merge_body, [(half, BF16)], (own, got), name="merge")
    arrived = lax.all_to_all(
        merged,
        "surf",
        split_axis=0,
        concat_axis=0,
        tiled=True,
        axis_index_groups=[list(range(core, surf_count, 2)) for core in range(2)],
    )
    near_dual, expand = call(
        self_body,
        [((INC, NP_DEV), F32), (dual_expand.shape, BF16)],
        (field, dual_self, dual_expand),
        held=(2, 1),
        name="self_part",
    )
    (response,) = call(
        answer_body,
        [((INC, NP_DEV), BF16)],
        (arrived, near_dual, expand),
        scratch=[pltpu.VMEM((BLK * INC, BLK * RANK), BF16)],
        name="answer",
    )
    return response


def solution(mesh):
    both = ("groups", "surf")
    row, flat = P(None, both), P(both)
    cube, flat2 = P(both, None, None), P(both, None)
    return jax.shard_map(
        shards,
        mesh=mesh,
        in_specs=(
            row, cube, flat, flat, cube, cube, flat2, flat, flat2, flat, cube, cube, cube, flat,
            flat2, flat, cube, cube, cube, flat2,
        ),
        out_specs=row,
        check_vma=False,
    )
```

```python
import jax
import jax.numpy as jnp
from jax import lax
from jax.experimental import pallas as pl
from jax.experimental.pallas import tpu as pltpu
from jax.sharding import PartitionSpec as P

TILE = 256
INC = 32
RANK = 32
BLK = 8
NP_DEV = 2048
LANES = 128
IDX_ROWS = 16
TAIL = 8
NEAR_CHUNK = 8
F32 = jnp.float32
BF16 = jnp.bfloat16
I32 = jnp.int32
NT = (((1,), (1,)), ((), ()))
VMEM_LIMIT = 36 * 1024 * 1024


def dot(a, b):
    return jnp.dot(a, b, preferred_element_type=F32)


def dot_nt(a, b):
    return lax.dot_general(a, b, NT, preferred_element_type=F32)


def iota(shape, dim):
    return lax.broadcasted_iota(I32, shape, dim)


def block(array, i):
    return array[:, i * TILE : (i + 1) * TILE]


def as_hot(mask):
    return mask.astype(F32).astype(BF16)


def call(body, outs, args, scratch=(), smem=(), held=(), far=(), small=(), streamed=(), flops=0, name=None):
    spaces = [
        pltpu.SMEM if k in smem else pltpu.HBM if k in held or k in far else pltpu.VMEM
        for k in range(len(args))
    ]
    size = sum(a.size * a.dtype.itemsize for a in args)
    outs = tuple(
        jax.ShapeDtypeStruct(s, d) for s, d in outs
    )
    buffers = [
        (pltpu.SMEM if k in small else pltpu.VMEM)(args[k].shape, args[k].dtype) for k in held
    ]
    waits = [pltpu.SemaphoreType.DMA(()) for _ in held]

    def wrapped(*refs):
        ins = list(refs[: len(args)])
        rest = refs[len(args) : len(refs) - 2 * len(held)]
        extra = refs[len(refs) - 2 * len(held) :]
        for n, k in enumerate(held):
            ins[k] = pltpu.make_async_copy(ins[k], extra[n], extra[len(held) + n])
            ins[k].start()
            ins[k] = (ins[k], extra[n])
        body(*ins, *rest)

    return pl.pallas_call(
        wrapped,
        out_shape=outs,
        in_specs=[pl.BlockSpec(memory_space=m) for m in spaces],
        out_specs=tuple(
            pl.BlockSpec(memory_space=pl.ANY if k in streamed else pltpu.VMEM)
            for k in range(len(outs))
        ),
        scratch_shapes=list(scratch) + buffers + waits,
        compiler_params=pltpu.CompilerParams(vmem_limit_bytes=VMEM_LIMIT),
        cost_estimate=pl.CostEstimate(flops=flops, bytes_accessed=size, transcendentals=0),
        name=name,
    )(*[pltpu.with_memory_space_constraint(a, m) if m is pltpu.HBM else a for a, m in zip(args, spaces)])


def ready(operand):
    operand[0].wait()
    return operand[1]


def fill_hot(hot, columns):
    height, count = columns.shape
    columns = columns.astype(BF16)
    lane = iota((height, TILE), 1).astype(F32).astype(BF16)
    one, zero = jnp.ones((height, TILE), BF16), jnp.zeros((height, TILE), BF16)
    for k in range(count):
        hot[k * height : (k + 1) * height, :] = jnp.where(lane == columns[:, k : k + 1], one, zero)


def coefficients(blocks, compress):
    width = BLK * RANK
    every = dot_nt(blocks, compress[...].reshape(width, TILE))
    owner = iota((INC, width), 1) // RANK
    coef = jnp.zeros((INC, width), F32)
    for s in range(BLK):
        coef = jnp.where(owner == s, every[s * INC : (s + 1) * INC], coef)
    return coef


def far_up_body(
    value, compress, coupling, source, owner, place,
    out_ref, blocks, turned, spread, pick, terms,
):
    coupling = ready(coupling)
    turned[...] = coupling[...].astype(F32).T
    value, compress = ready(value), ready(compress)
    for s in range(BLK):
        blocks[s * INC : (s + 1) * INC, :] = block(value, s)
    coef = coefficients(blocks[...], compress)
    width = BLK * RANK
    keep = (iota((RANK, width), 1) % RANK) == iota((RANK, width), 0)
    for i in range(INC):
        spread[i * RANK : (i + 1) * RANK, :] = jnp.where(keep, coef[i : i + 1, :], 0.0).astype(BF16)
    source = ready(source)
    tiles = source.shape[1]
    pick[...] = dot(spread[...], as_hot((iota((width, tiles), 0) // RANK) == source[...]))

    def step(pair, carry):
        rows = pl.multiple_of(pair * (2 * RANK), 2 * RANK)
        got = pick[pl.ds(rows, 2 * RANK), :]
        first = jnp.zeros((RANK, tiles), F32)
        second = jnp.zeros((RANK, tiles), F32)
        for r in range(RANK):
            factor = turned[r * RANK : (r + 1) * RANK, :]
            first += got[r : r + 1, :] * factor
            second += got[RANK + r : RANK + r + 1, :] * factor
        terms[pl.ds(rows, 2 * RANK), :] = jnp.concatenate([first, second], axis=0).astype(BF16)
        return carry

    lax.fori_loop(0, INC // 2, step, 0)
    targets = out_ref.shape[0]
    owner, place = ready(owner), ready(place)
    select = as_hot(iota((targets, tiles), 0) == owner[...] * BLK + place[...])
    out_ref[...] = dot_nt(select, terms[...]).astype(BF16)


def far_scratch(tiles):
    return [
        pltpu.VMEM((BLK * INC, TILE), BF16),
        pltpu.VMEM((RANK * RANK, tiles), F32),
        pltpu.VMEM((INC * RANK, BLK * RANK), BF16),
        pltpu.VMEM((INC * RANK, tiles), F32),
        pltpu.VMEM((INC * RANK, tiles), BF16),
    ]


def far_sums(arrived_ref, spread):
    rows = arrived_ref.shape[0]
    total = jnp.sum(arrived_ref[...].astype(F32).reshape(rows // BLK, BLK, INC * RANK), axis=0)
    width = INC * RANK
    keep = (iota((INC, width), 1) // RANK) == iota((INC, width), 0)
    for b in range(BLK):
        spread[b * INC : (b + 1) * INC, :] = jnp.where(keep, total[b : b + 1, :], 0.0).astype(BF16)
    fold = as_hot((iota((width, RANK), 0) % RANK) == iota((width, RANK), 1))
    return dot(spread[...], fold).astype(BF16)


def order_body(owner, index, weight, _, high_out, hot_out, bounds_out, rows_out, weight_out, ranks):
    owner, index = ready(owner), ready(index)
    owners = bounds_out.shape[0]
    pieces = -(-max(2, 2 * NP_DEV // owners) // LANES)
    before = as_hot(iota((TILE, TILE), 0) < iota((TILE, TILE), 1))
    number = iota((owners, TILE), 0)
    count = jnp.zeros((owners, 1), F32)
    begin = jnp.zeros((owners, 1), F32)
    hots, carries = [], []
    for c in range(BLK):
        names = block(owner, c)
        hot = (number == names).astype(F32)
        hots.append(hot)
        carries.append(count)
        count = count + jnp.sum(hot, axis=1, keepdims=True)
        begin = begin + jnp.sum((names < number).astype(F32), axis=1, keepdims=True)
    for c in range(BLK):
        rank = dot(hots[c].astype(BF16), before)
        ranks[c : c + 1, :] = jnp.sum(hots[c] * (rank + carries[c] + begin), axis=0, keepdims=True)
    spots = ranks[...].astype(I32)
    high_out[...] = spots // TILE
    fill_hot(hot_out, (spots % TILE).astype(F32).T)
    pair = iota((owners, 2), 1)
    bounds_out[...] = jnp.where(pair == 0, begin, count).astype(I32)
    row = iota((IDX_ROWS, NP_DEV), 0)
    index = index[...]
    digits = jnp.where(row % 2 == 0, index // TILE, index % TILE)
    rows_out[...] = jnp.where(row < 2 * pieces, digits, 0).astype(F32).astype(BF16)
    weight_out[...] = ready(weight)[...]


def prepare_body(
    target, origin, own, inner_ref, outer_ref, inverse, lower, upper, expand, tiles_ref,
    near_out, lower_out, upper_out, expand_out, cells, total, products, pair, tiles, arrivals,
):
    count = tiles_ref.shape[0]
    copies = []
    for c in range(count // NEAR_CHUNK):
        part = pl.ds(c * NEAR_CHUNK, NEAR_CHUNK)
        copy = pltpu.make_async_copy(tiles_ref.at[part], tiles.at[part], arrivals.at[c])
        copy.start()
        copies.append(copy)
    position = lax.axis_index("surf")
    odd = position % 2
    pair[0] = inner_ref[...]
    pair[1] = outer_ref[...]
    cells[0] = pair[1 - odd, :, NP_DEV - TILE :]
    cells[BLK + 1] = pair[odd, :, :TILE]
    inverse, lower, upper, expand = ready(inverse), ready(lower), ready(upper), ready(expand)
    for b in range(BLK):
        lower_out[b] = dot(lower[b], inverse[b]).astype(BF16)
        upper_out[b] = dot(upper[b], inverse[b]).astype(BF16)
        expand_out[b] = dot(expand[b], inverse[b]).astype(BF16)
    own, target, origin = ready(own), ready(target), ready(origin)
    for b in range(BLK):
        cells[b + 1] = block(own, b)
    total[...] = jnp.zeros_like(total)
    start = position * BLK - 1
    for c, copy in enumerate(copies):
        copy.wait()
        for k in range(c * NEAR_CHUNK, (c + 1) * NEAR_CHUNK):
            products[k] = dot(cells[origin[k] - start], tiles[k])
    for k in range(count):
        total[target[k]] += products[k]
    for b in range(BLK):
        near_out[:, b * TILE : (b + 1) * TILE] = dot(total[b].astype(BF16), inverse[b])


def solve_body(
    arrived_ref, near_ref, expand_ref, lower_ref, upper_ref,
    start_out, next_out, inner_out, outer_out, notes, spread,
):
    sums = far_sums(arrived_ref, spread)
    start, low = [], []
    for b in range(BLK):
        value = block(near_ref, b) + dot(sums[b * INC : (b + 1) * INC, :], expand_ref[b])
        start.append(value)
        low.append(value.astype(BF16))
        start_out[:, b * TILE : (b + 1) * TILE] = value
    after = []
    for b in range(BLK):
        value = start[b]
        if b > 0:
            value = value - dot(low[b - 1], lower_ref[b])
        if b < BLK - 1:
            value = value - dot(low[b + 1], upper_ref[b])
        after.append(value)
        next_out[:, b * TILE : (b + 1) * TILE] = value
    last = BLK - 1
    odd = lax.axis_index("surf") % 2
    for n, (edge, inside, away, back) in enumerate(
        ((last, last - 1, lower_ref, upper_ref), (0, 1, upper_ref, lower_ref))
    ):
        feedless = start[edge] - dot(after[inside].astype(BF16), away[edge])
        notes[n, 0:INC, :] = low[edge]
        notes[n, INC : 2 * INC, :] = after[edge].astype(BF16)
        notes[n, 2 * INC : 3 * INC, :] = feedless.astype(BF16)
        notes[n, 3 * INC :, :] = back[edge]
    inner_out[...] = notes[odd]
    outer_out[...] = notes[1 - odd]


def middle_body(start_ref, next_ref, lower_ref, upper_ref, second_out, third_out):
    last = BLK - 1
    now = [block(next_ref, b).astype(BF16) for b in range(BLK)]
    second = []
    for b in range(BLK):
        value = block(start_ref, b)
        if b > 1:
            value = value - dot(now[b - 1], lower_ref[b])
        if b < last - 1:
            value = value - dot(now[b + 1], upper_ref[b])
        second.append(value.astype(BF16))
        second_out[:, b * TILE : (b + 1) * TILE] = value
    for b in range(BLK):
        value = block(start_ref, b)
        if 2 < b < last:
            value = value - dot(second[b - 1], lower_ref[b])
        if 0 < b < last - 2:
            value = value - dot(second[b + 1], upper_ref[b])
        third_out[:, b * TILE : (b + 1) * TILE] = value


def finish_body(
    start_ref, next_ref, second_ref, third_ref, inner_note, outer_note, lower_ref, upper_ref,
    weight, tails_ref, high_ref, hot_ref, bounds_ref, send_ref,
    notes, spread, ordered, stage, sent,
):
    position = lax.axis_index("surf")
    odd = position % 2
    notes[0] = inner_note[...]
    notes[1] = outer_note[...]
    then = [block(third_ref, b) for b in range(BLK)]
    for left in (True, False):
        n = 1 - odd if left else odd
        exists = (position > 0) if left else (position < lax.axis_size("surf") - 1)
        exists = exists.astype(F32)
        edge, step = (0, 1) if left else (BLK - 1, -1)
        toward, away = (lower_ref, upper_ref) if left else (upper_ref, lower_ref)
        one, two = edge + step, edge + 2 * step
        first = block(start_ref, edge).astype(BF16)
        beyond = notes[n, 3 * INC :, :]
        beside = notes[n, INC : 2 * INC, :].astype(F32) - dot(first, beyond)
        beside = (beside * exists).astype(BF16)
        now = block(next_ref, edge) - dot(notes[n, 0:INC, :], toward[edge]) * exists
        now = now.astype(BF16)
        beside_next = notes[n, 2 * INC : 3 * INC, :].astype(F32) - dot(now, beyond)
        beside_next = (beside_next * exists).astype(BF16)
        second = (block(second_ref, edge) - dot(beside, toward[edge])).astype(BF16)
        second_one = (block(second_ref, one) - dot(now, toward[one])).astype(BF16)
        then[edge] = then[edge] - dot(beside_next, toward[edge]) - dot(second_one, away[edge])
        then[one] = then[one] - dot(second, toward[one])
        then[two] = then[two] - dot(second_one, toward[two])
    for b in range(BLK):
        solved = then[b].astype(BF16).astype(F32)
        shares = (solved * block(weight, b)).astype(BF16)
        by_high_digit(spread, shares, high_ref, b)
    put_in_order(ordered, spread, hot_ref)
    owners = send_ref.shape[0]
    pieces = (send_ref.shape[1] - TAIL) // INC
    for o in range(owners):
        piece = owner_window(ordered, bounds_ref[o, 0], pieces)
        parts = [piece[:, j * LANES : (j + 1) * LANES] for j in range(pieces)]
        stage[o] = jnp.concatenate(parts + [tails_ref[o]], axis=0).astype(BF16)
        pltpu.make_async_copy(stage.at[o], send_ref.at[o], sent.at[o]).start()
    for o in range(owners):
        pltpu.make_async_copy(stage.at[o], send_ref.at[o], sent.at[o]).wait()


def by_high_digit(spread, values, high_ref, b):
    rows = values.shape[0]
    high = high_ref[b : b + 1, :].astype(F32).astype(BF16)
    for h in range(BLK):
        spread[h * rows : (h + 1) * rows, b * TILE : (b + 1) * TILE] = jnp.where(
            high == h, values, jnp.zeros_like(values)
        )


def put_in_order(ordered, spread, hot_ref):
    rows = ordered.shape[0]
    sorted_rows = dot(spread[...], hot_ref[...])
    for h in range(BLK):
        ordered[:, h * TILE : (h + 1) * TILE] = sorted_rows[h * rows : (h + 1) * rows]
    ordered[:, NP_DEV:] = jnp.zeros((rows, ordered.shape[1] - NP_DEV), F32)


def owner_window(ordered, begin, pieces):
    wide = (pieces + 1) * LANES
    base = pl.multiple_of((begin // LANES) * LANES, LANES)
    return pltpu.roll(ordered[:, pl.ds(base, wide)], wide - (begin - base), 1)


def tails_body(index_rows, high_ref, hot_ref, bounds_ref, out_ref, spread, ordered):
    for b in range(BLK):
        by_high_digit(spread, block(index_rows, b), high_ref, b)
    put_in_order(ordered, spread, hot_ref)
    pieces = ordered.shape[1] // LANES - NP_DEV // LANES - 1
    row = iota((TAIL, LANES), 0)
    slot = iota((TAIL, LANES), 1) + (row // 2) * LANES
    for o in range(out_ref.shape[0]):
        piece = owner_window(ordered, bounds_ref[o, 0], pieces)
        tail = piece[:TAIL, :LANES]
        for j in range(1, pieces):
            tail = jnp.where(row // 2 == j, piece[:TAIL, j * LANES : (j + 1) * LANES], tail)
        out_ref[o] = jnp.where(slot >= bounds_ref[o, 1], -16.0, tail)


def gather_body(
    arrived_ref, compress, couple_ref, field_out, coef_out, give_out, index, spread, hot,
):
    owners, rows, _ = arrived_ref.shape
    pieces = (rows - TAIL) // INC
    for e in range(owners):
        tail = arrived_ref[e].astype(F32)[INC * pieces :]
        marks = tail.astype(BF16)
        for j in range(pieces):
            k = e * pieces + j
            part = arrived_ref[e, j * INC : (j + 1) * INC, :]
            high = marks[2 * j : 2 * j + 1]
            index[k : k + 1, :] = tail[2 * j + 1 : 2 * j + 2]
            for h in range(BLK):
                spread[h * INC : (h + 1) * INC, k * LANES : (k + 1) * LANES] = jnp.where(
                    high == h, part, jnp.zeros_like(part)
                )
    fill_hot(hot, index[...].T)
    field = dot(spread[...], hot[...]).astype(BF16)
    for b in range(BLK):
        field_out[b] = field[b * INC : (b + 1) * INC]
    coef = coefficients(field, compress).astype(BF16)
    coef_out[...] = coef
    other = 1 - lax.axis_index("surf") % 2
    for c in range(give_out.shape[0]):
        give_out[c] = dot(coef, owner_columns(couple_ref, c, other)).astype(BF16)


def owner_columns(couple_ref, chip, core):
    return couple_ref[:, pl.ds(pl.multiple_of((2 * chip + core) * TILE, TILE), TILE)]


def own_body(coef_ref, couple_ref, out_ref):
    core = lax.axis_index("surf") % 2
    for c in range(out_ref.shape[0]):
        out_ref[c] = dot(coef_ref[...], owner_columns(couple_ref, c, core))


def merge_body(own_ref, got_ref, out_ref):
    out_ref[...] = (own_ref[...] + got_ref[...].astype(F32)).astype(BF16)


def couple_body(coupling, source, owner, place, basis, out_ref, basis_out, total, lanes):
    tiles, width = lanes.shape[0], BLK * RANK
    flat = RANK * RANK
    total[...] = jnp.zeros_like(total)
    coupling = ready(coupling)
    lanes[...] = coupling[...].astype(F32)
    keep = (iota((RANK, flat), 1) % RANK) == iota((RANK, flat), 0)
    fold = as_hot((iota((flat, width), 0) // RANK) == (iota((flat, width), 1) % RANK))
    number = iota((RANK, width), 1) // RANK
    source, owner, place = ready(source), ready(owner), ready(place)
    group = 8

    def step(c, carry):
        begin = pl.multiple_of(c * group, group)
        rows = lanes[pl.ds(begin, group), :]
        tall = [jnp.where(keep, rows[k : k + 1], 0.0).astype(BF16) for k in range(group)]
        turned = dot(jnp.concatenate(tall, axis=0), fold)
        for k in range(group):
            f = begin + k
            tile = jnp.where(number == source[0, f], turned[k * RANK : (k + 1) * RANK], 0.0)
            total[owner[0, f] * BLK + place[0, f]] += tile
        return carry

    lax.fori_loop(0, tiles // group, step, 0)
    for o in range(out_ref.shape[1] // TILE):
        part = total[o * BLK : (o + 1) * BLK].reshape(TILE, width)
        out_ref[:, o * TILE : (o + 1) * TILE] = part.T.astype(BF16)
    basis_out[...] = ready(basis)[...]


def self_body(field_ref, tiles, basis, out_ref, basis_out):
    basis_out[...] = ready(basis)[...]
    tiles = ready(tiles)
    for b in range(BLK):
        out_ref[:, b * TILE : (b + 1) * TILE] = dot(field_ref[b], tiles[b])


def answer_body(arrived_ref, near_ref, expand, out_ref, spread):
    total = jnp.sum(arrived_ref[...].astype(F32), axis=0)
    number = iota(total.shape, 1) // RANK
    for b in range(BLK):
        spread[b * INC : (b + 1) * INC, :] = jnp.where(number == b, total, 0.0).astype(BF16)
    far = dot(spread[...], expand[...].reshape(BLK * RANK, TILE))
    for b in range(BLK):
        out_ref[:, b * TILE : (b + 1) * TILE] = (
            block(near_ref, b) + far[b * INC : (b + 1) * INC]
        ).astype(BF16)


def swap(inner, outer, surf_count):
    pairs = [(i, i ^ 1) for i in range(surf_count)]
    others = [(0, 0), (surf_count - 1, surf_count - 1)]
    for i in range(1, surf_count - 1, 2):
        others += [(i, i + 1), (i + 1, i)]
    outer = lax.ppermute(outer, "surf", others)
    inner = lax.ppermute(inner, "surf", pairs)
    return inner, outer


def exchange(array, surf_count):
    shape = array.shape
    array = array.reshape((surf_count, shape[0] // surf_count) + shape[1:])
    array = lax.all_to_all(array, "surf", split_axis=0, concat_axis=0, tiled=True)
    return array.reshape(shape)


def shards(
    currents, near_tiles, near_target, near_source, primal_compress, primal_expand, primal_coupling,
    far_source, far_owner, far_block, gram_inverse, gram_lower, gram_upper, refine_weight,
    dual_owner, dual_index, dual_self, dual_compress, dual_expand, dual_coupling,
):
    surf_count = lax.axis_size("surf")
    tiles = far_source.shape[0]
    near_count = near_tiles.shape[0]
    targets = surf_count * BLK
    capacity = max(2, 2 * NP_DEV // surf_count)
    pieces = -(-capacity // LANES)
    lists = (far_source.reshape(1, tiles), far_owner.reshape(1, tiles), far_block.reshape(1, tiles))
    cube = ((BLK, TILE, TILE), BF16)

    note = ((3 * INC + TILE, TILE), BF16)
    inner, outer = swap(currents, currents, surf_count)
    (partial,) = call(
        far_up_body,
        [((targets, INC * RANK), BF16)],
        (currents, primal_compress, primal_coupling) + lists,
        scratch=far_scratch(tiles),
        held=(2, 0, 1, 3, 4, 5),
        flops=10**11,
        name="far_up",
    )
    arrived = exchange(partial, surf_count)
    near_part, lower, upper, expanded = call(
        prepare_body,
        [((INC, NP_DEV), F32), cube, cube, ((BLK, RANK, TILE), BF16)],
        (
            near_target, near_source, currents, inner, outer, gram_inverse, gram_lower, gram_upper,
            primal_expand, near_tiles,
        ),
        scratch=[
            pltpu.VMEM((BLK + 2, INC, TILE), BF16),
            pltpu.VMEM((BLK, INC, TILE), F32),
            pltpu.VMEM((near_count, INC, TILE), F32),
            pltpu.VMEM((2,) + currents.shape, BF16),
            pltpu.VMEM(near_tiles.shape, BF16),
            pltpu.SemaphoreType.DMA((near_count // NEAR_CHUNK,)),
        ],
        held=(5, 6, 7, 8, 2, 0, 1),
        far=(9,),
        small=(0, 1),
        flops=10**11,
        name="prepare",
    )
    start, after, inner_note, outer_note = call(
        solve_body,
        [((INC, NP_DEV), F32)] * 2 + [note] * 2,
        (arrived, near_part, expanded, lower, upper),
        scratch=[
            pltpu.VMEM((2,) + note[0], BF16),
            pltpu.VMEM((BLK * INC, INC * RANK), BF16),
        ],
        name="solve",
    )
    inner_note, outer_note = swap(inner_note, outer_note, surf_count)
    high, hot, bounds, index_rows, weight = call(
        order_body,
        [
            ((BLK, TILE), I32), ((NP_DEV, TILE), BF16), ((surf_count, 2), I32),
            ((IDX_ROWS, NP_DEV), BF16), ((1, NP_DEV), F32),
        ],
        (
            dual_owner.reshape(1, NP_DEV), dual_index.reshape(1, NP_DEV),
            refine_weight.reshape(1, NP_DEV), start,
        ),
        scratch=[pltpu.VMEM((BLK, TILE), F32)],
        held=(0, 1, 2),
        flops=10**9,
        name="order",
    )
    (tails,) = call(
        tails_body,
        [((surf_count, TAIL, LANES), F32)],
        (index_rows, high, hot, bounds),
        scratch=[
            pltpu.VMEM((BLK * IDX_ROWS, NP_DEV), BF16),
            pltpu.VMEM((IDX_ROWS, NP_DEV + (pieces + 1) * LANES), F32),
        ],
        smem=(3,),
        flops=10**9,
        name="tails",
    )
    second, third = call(
        middle_body,
        [((INC, NP_DEV), F32)] * 2,
        (start, after, lower, upper),
        flops=10**9,
        name="middle",
    )
    (send,) = call(
        finish_body,
        [((surf_count, INC * pieces + TAIL, LANES), BF16)],
        (
            start, after, second, third, inner_note, outer_note, lower, upper,
            weight, tails, high, hot, bounds,
        ),
        scratch=[
            pltpu.VMEM((2,) + note[0], BF16),
            pltpu.VMEM((BLK * INC, NP_DEV), BF16),
            pltpu.VMEM((INC, NP_DEV + (pieces + 1) * LANES), F32),
            pltpu.VMEM((surf_count, INC * pieces + TAIL, LANES), BF16),
            pltpu.SemaphoreType.DMA((surf_count,)),
        ],
        streamed=(0,),
        smem=(12,),
        name="finish",
    )
    shares = lax.all_to_all(send, "surf", split_axis=0, concat_axis=0, tiled=True)
    slots = surf_count * pieces * LANES
    couple, compress = call(
        couple_body,
        [((BLK * RANK, targets * RANK), BF16), (dual_compress.shape, BF16)],
        (dual_coupling,) + lists + (dual_compress,),
        scratch=[pltpu.VMEM((targets, RANK, BLK * RANK), F32), pltpu.VMEM((tiles, INC * RANK), F32)],
        held=(0, 1, 2, 3, 4),
        small=(1, 2, 3),
        flops=10**10,
        name="couple",
    )
    half = (surf_count // 2, INC, BLK * RANK)
    field, coef, give = call(
        gather_body,
        [((BLK, INC, TILE), BF16), ((INC, BLK * RANK), BF16), (half, BF16)],
        (shares, compress, couple),
        scratch=[
            pltpu.VMEM((surf_count * pieces, LANES), F32),
            pltpu.VMEM((BLK * INC, slots), BF16),
            pltpu.VMEM((slots, TILE), BF16),
        ],
        name="gather",
    )
    got = lax.ppermute(give, "surf", [(i, i ^ 1) for i in range(surf_count)])
    (own,) = call(own_body, [(half, F32)], (coef, couple), flops=10**9, name="own")
    (merged,) = call(merge_body, [(half, BF16)], (own, got), name="merge")
    arrived = lax.all_to_all(
        merged,
        "surf",
        split_axis=0,
        concat_axis=0,
        tiled=True,
        axis_index_groups=[list(range(core, surf_count, 2)) for core in range(2)],
    )
    near_dual, expand = call(
        self_body,
        [((INC, NP_DEV), F32), (dual_expand.shape, BF16)],
        (field, dual_self, dual_expand),
        held=(2, 1),
        name="self_part",
    )
    (response,) = call(
        answer_body,
        [((INC, NP_DEV), BF16)],
        (arrived, near_dual, expand),
        scratch=[pltpu.VMEM((BLK * INC, BLK * RANK), BF16)],
        name="answer",
    )
    return response


def solution(mesh):
    both = ("groups", "surf")
    row, flat = P(None, both), P(both)
    cube, flat2 = P(both, None, None), P(both, None)
    return jax.shard_map(
        shards,
        mesh=mesh,
        in_specs=(
            row, cube, flat, flat, cube, cube, flat2, flat, flat2, flat, cube, cube, cube, flat,
            flat2, flat, cube, cube, cube, flat2,
        ),
        out_specs=row,
        check_vma=False,
    )
```

```python
import jax
import jax.numpy as jnp
from jax import lax
from jax.experimental import pallas as pl
from jax.experimental.pallas import tpu as pltpu
from jax.sharding import PartitionSpec as P

TILE = 256
INC = 32
RANK = 32
BLK = 8
NP_DEV = 2048
LANES = 128
IDX_ROWS = 16
TAIL = 8
NEAR_CHUNK = 8
F32 = jnp.float32
BF16 = jnp.bfloat16
I32 = jnp.int32
NT = (((1,), (1,)), ((), ()))
VMEM_LIMIT = 36 * 1024 * 1024


def dot(a, b):
    return jnp.dot(a, b, preferred_element_type=F32)


def dot_nt(a, b):
    return lax.dot_general(a, b, NT, preferred_element_type=F32)


def iota(shape, dim):
    return lax.broadcasted_iota(I32, shape, dim)


def block(array, i):
    return array[:, i * TILE : (i + 1) * TILE]


def as_hot(mask):
    return mask.astype(F32).astype(BF16)


def call(body, outs, args, scratch=(), smem=(), held=(), far=(), small=(), streamed=(), flops=0, name=None):
    spaces = [
        pltpu.SMEM if k in smem else pltpu.HBM if k in held or k in far else pltpu.VMEM
        for k in range(len(args))
    ]
    size = sum(a.size * a.dtype.itemsize for a in args)
    outs = tuple(
        jax.ShapeDtypeStruct(s, d) for s, d in outs
    )
    buffers = [
        (pltpu.SMEM if k in small else pltpu.VMEM)(args[k].shape, args[k].dtype) for k in held
    ]
    waits = [pltpu.SemaphoreType.DMA(()) for _ in held]

    def wrapped(*refs):
        ins = list(refs[: len(args)])
        rest = refs[len(args) : len(refs) - 2 * len(held)]
        extra = refs[len(refs) - 2 * len(held) :]
        for n, k in enumerate(held):
            ins[k] = pltpu.make_async_copy(ins[k], extra[n], extra[len(held) + n])
            ins[k].start()
            ins[k] = (ins[k], extra[n])
        body(*ins, *rest)

    return pl.pallas_call(
        wrapped,
        out_shape=outs,
        in_specs=[pl.BlockSpec(memory_space=m) for m in spaces],
        out_specs=tuple(
            pl.BlockSpec(memory_space=pl.ANY if k in streamed else pltpu.VMEM)
            for k in range(len(outs))
        ),
        scratch_shapes=list(scratch) + buffers + waits,
        compiler_params=pltpu.CompilerParams(vmem_limit_bytes=VMEM_LIMIT),
        cost_estimate=pl.CostEstimate(flops=flops, bytes_accessed=size, transcendentals=0),
        name=name,
    )(*[pltpu.with_memory_space_constraint(a, m) if m is pltpu.HBM else a for a, m in zip(args, spaces)])


def ready(operand):
    operand[0].wait()
    return operand[1]


def fill_hot(hot, columns):
    height, count = columns.shape
    columns = columns.astype(BF16)
    lane = iota((height, TILE), 1).astype(F32).astype(BF16)
    one, zero = jnp.ones((height, TILE), BF16), jnp.zeros((height, TILE), BF16)
    for k in range(count):
        hot[k * height : (k + 1) * height, :] = jnp.where(lane == columns[:, k : k + 1], one, zero)


def coefficients(blocks, compress):
    width = BLK * RANK
    every = dot_nt(blocks, compress[...].reshape(width, TILE))
    owner = iota((INC, width), 1) // RANK
    coef = jnp.zeros((INC, width), F32)
    for s in range(BLK):
        coef = jnp.where(owner == s, every[s * INC : (s + 1) * INC], coef)
    return coef


def far_up_body(
    value, compress, coupling, source, owner, place,
    out_ref, copy_out, blocks, turned, spread, pick, terms, stage, sent,
):
    coupling = ready(coupling)
    turned[...] = coupling[...].astype(F32).T
    value, compress = ready(value), ready(compress)
    copy_out[...] = value[...]
    for s in range(BLK):
        blocks[s * INC : (s + 1) * INC, :] = block(value, s)
    coef = coefficients(blocks[...], compress)
    width = BLK * RANK
    keep = (iota((RANK, width), 1) % RANK) == iota((RANK, width), 0)
    for i in range(INC):
        spread[i * RANK : (i + 1) * RANK, :] = jnp.where(keep, coef[i : i + 1, :], 0.0).astype(BF16)
    source = ready(source)
    tiles = source.shape[1]
    pick[...] = dot(spread[...], as_hot((iota((width, tiles), 0) // RANK) == source[...]))

    def step(pair, carry):
        rows = pl.multiple_of(pair * (2 * RANK), 2 * RANK)
        got = pick[pl.ds(rows, 2 * RANK), :]
        first = jnp.zeros((RANK, tiles), F32)
        second = jnp.zeros((RANK, tiles), F32)
        for r in range(RANK):
            factor = turned[r * RANK : (r + 1) * RANK, :]
            first += got[r : r + 1, :] * factor
            second += got[RANK + r : RANK + r + 1, :] * factor
        terms[pl.ds(rows, 2 * RANK), :] = jnp.concatenate([first, second], axis=0).astype(BF16)
        return carry

    targets = out_ref.shape[0]
    owner, place = ready(owner), ready(place)
    select = as_hot(iota((targets, tiles), 0) == owner[...] * BLK + place[...])
    chunks = 4
    width = INC * RANK // chunks
    copies = []
    for c in range(chunks):
        lax.fori_loop(c * (INC // 2 // chunks), (c + 1) * (INC // 2 // chunks), step, 0)
        part = slice(c * width, (c + 1) * width)
        stage[:, part] = dot_nt(select, terms[part, :]).astype(BF16)
        columns = pl.ds(c * width, width)
        copy = pltpu.make_async_copy(stage.at[:, columns], out_ref.at[:, columns], sent.at[c])
        copy.start()
        copies.append(copy)
    for copy in copies:
        copy.wait()


def far_scratch(tiles):
    return [
        pltpu.VMEM((BLK * INC, TILE), BF16),
        pltpu.VMEM((RANK * RANK, tiles), F32),
        pltpu.VMEM((INC * RANK, BLK * RANK), BF16),
        pltpu.VMEM((INC * RANK, tiles), F32),
        pltpu.VMEM((INC * RANK, tiles), BF16),
    ]


def far_sums(arrived_ref, spread):
    rows = arrived_ref.shape[0]
    total = jnp.sum(arrived_ref[...].astype(F32).reshape(rows // BLK, BLK, INC * RANK), axis=0)
    width = INC * RANK
    keep = (iota((INC, width), 1) // RANK) == iota((INC, width), 0)
    for b in range(BLK):
        spread[b * INC : (b + 1) * INC, :] = jnp.where(keep, total[b : b + 1, :], 0.0).astype(BF16)
    fold = as_hot((iota((width, RANK), 0) % RANK) == iota((width, RANK), 1))
    return dot(spread[...], fold).astype(BF16)


def order_body(owner, index, weight, _, high_out, hot_out, bounds_out, rows_out, weight_out, ranks):
    owner, index = ready(owner), ready(index)
    owners = bounds_out.shape[0]
    pieces = -(-max(2, 2 * NP_DEV // owners) // LANES)
    before = as_hot(iota((TILE, TILE), 0) < iota((TILE, TILE), 1))
    number = iota((owners, TILE), 0)
    count = jnp.zeros((owners, 1), F32)
    begin = jnp.zeros((owners, 1), F32)
    hots, carries = [], []
    for c in range(BLK):
        names = block(owner, c)
        hot = (number == names).astype(F32)
        hots.append(hot)
        carries.append(count)
        count = count + jnp.sum(hot, axis=1, keepdims=True)
        begin = begin + jnp.sum((names < number).astype(F32), axis=1, keepdims=True)
    for c in range(BLK):
        rank = dot(hots[c].astype(BF16), before)
        ranks[c : c + 1, :] = jnp.sum(hots[c] * (rank + carries[c] + begin), axis=0, keepdims=True)
    spots = ranks[...].astype(I32)
    high_out[...] = spots // TILE
    fill_hot(hot_out, (spots % TILE).astype(F32).T)
    pair = iota((owners, 2), 1)
    bounds_out[...] = jnp.where(pair == 0, begin, count).astype(I32)
    row = iota((IDX_ROWS, NP_DEV), 0)
    index = index[...]
    digits = jnp.where(row % 2 == 0, index // TILE, index % TILE)
    rows_out[...] = jnp.where(row < 2 * pieces, digits, 0).astype(F32).astype(BF16)
    weight_out[...] = ready(weight)[...]


def prepare_body(
    target, origin, own, inner_ref, outer_ref, inverse, lower, upper, expand, tiles_ref,
    near_out, lower_out, upper_out, expand_out, cells, total, products, pair, tiles, arrivals,
):
    count = tiles_ref.shape[0]
    copies = []
    for c in range(count // NEAR_CHUNK):
        part = pl.ds(c * NEAR_CHUNK, NEAR_CHUNK)
        copy = pltpu.make_async_copy(tiles_ref.at[part], tiles.at[part], arrivals.at[c])
        copy.start()
        copies.append(copy)
    position = lax.axis_index("surf")
    odd = position % 2
    pair[0] = inner_ref[...]
    pair[1] = outer_ref[...]
    cells[0] = pair[1 - odd, :, NP_DEV - TILE :]
    cells[BLK + 1] = pair[odd, :, :TILE]
    inverse, lower, upper, expand = ready(inverse), ready(lower), ready(upper), ready(expand)
    for b in range(BLK):
        lower_out[b] = dot(lower[b], inverse[b]).astype(BF16)
        upper_out[b] = dot(upper[b], inverse[b]).astype(BF16)
        expand_out[b] = dot(expand[b], inverse[b]).astype(BF16)
    own, target, origin = ready(own), ready(target), ready(origin)
    for b in range(BLK):
        cells[b + 1] = block(own, b)
    total[...] = jnp.zeros_like(total)
    start = position * BLK - 1
    for c, copy in enumerate(copies):
        copy.wait()
        for k in range(c * NEAR_CHUNK, (c + 1) * NEAR_CHUNK):
            products[k] = dot(cells[origin[k] - start], tiles[k])
    for k in range(count):
        total[target[k]] += products[k]
    for b in range(BLK):
        near_out[:, b * TILE : (b + 1) * TILE] = dot(total[b].astype(BF16), inverse[b])


def solve_body(
    arrived_ref, near_ref, expand_ref, lower_ref, upper_ref,
    start_out, next_out, inner_out, outer_out, notes, spread,
):
    sums = far_sums(arrived_ref, spread)
    start, low = [], []
    for b in range(BLK):
        value = block(near_ref, b) + dot(sums[b * INC : (b + 1) * INC, :], expand_ref[b])
        start.append(value)
        low.append(value.astype(BF16))
        start_out[:, b * TILE : (b + 1) * TILE] = value
    after = []
    for b in range(BLK):
        value = start[b]
        if b > 0:
            value = value - dot(low[b - 1], lower_ref[b])
        if b < BLK - 1:
            value = value - dot(low[b + 1], upper_ref[b])
        after.append(value)
        next_out[:, b * TILE : (b + 1) * TILE] = value
    last = BLK - 1
    odd = lax.axis_index("surf") % 2
    for n, (edge, inside, away, back) in enumerate(
        ((last, last - 1, lower_ref, upper_ref), (0, 1, upper_ref, lower_ref))
    ):
        feedless = start[edge] - dot(after[inside].astype(BF16), away[edge])
        notes[n, 0:INC, :] = low[edge]
        notes[n, INC : 2 * INC, :] = after[edge].astype(BF16)
        notes[n, 2 * INC : 3 * INC, :] = feedless.astype(BF16)
        notes[n, 3 * INC :, :] = back[edge]
    inner_out[...] = notes[odd]
    outer_out[...] = notes[1 - odd]


def middle_body(
    start_ref, next_ref, lower_ref, upper_ref, note_ref, second_out, third_out, note_out
):
    note_out[...] = note_ref[...]
    last = BLK - 1
    now = [block(next_ref, b).astype(BF16) for b in range(BLK)]
    second = []
    for b in range(BLK):
        value = block(start_ref, b)
        if b > 1:
            value = value - dot(now[b - 1], lower_ref[b])
        if b < last - 1:
            value = value - dot(now[b + 1], upper_ref[b])
        second.append(value.astype(BF16))
        second_out[:, b * TILE : (b + 1) * TILE] = value
    for b in range(BLK):
        value = block(start_ref, b)
        if 2 < b < last:
            value = value - dot(second[b - 1], lower_ref[b])
        if 0 < b < last - 2:
            value = value - dot(second[b + 1], upper_ref[b])
        third_out[:, b * TILE : (b + 1) * TILE] = value


def finish_body(
    start_ref, next_ref, second_ref, third_ref, inner_note, outer_note, lower_ref, upper_ref,
    weight, tails_ref, high_ref, hot_ref, bounds_ref, send_ref,
    notes, spread, ordered, stage, sent,
):
    position = lax.axis_index("surf")
    odd = position % 2
    notes[0] = inner_note[...]
    notes[1] = outer_note[...]
    then = [block(third_ref, b) for b in range(BLK)]
    for left in (True, False):
        n = 1 - odd if left else odd
        exists = (position > 0) if left else (position < lax.axis_size("surf") - 1)
        exists = exists.astype(F32)
        edge, step = (0, 1) if left else (BLK - 1, -1)
        toward, away = (lower_ref, upper_ref) if left else (upper_ref, lower_ref)
        one, two = edge + step, edge + 2 * step
        first = block(start_ref, edge).astype(BF16)
        beyond = notes[n, 3 * INC :, :]
        beside = notes[n, INC : 2 * INC, :].astype(F32) - dot(first, beyond)
        beside = (beside * exists).astype(BF16)
        now = block(next_ref, edge) - dot(notes[n, 0:INC, :], toward[edge]) * exists
        now = now.astype(BF16)
        beside_next = notes[n, 2 * INC : 3 * INC, :].astype(F32) - dot(now, beyond)
        beside_next = (beside_next * exists).astype(BF16)
        second = (block(second_ref, edge) - dot(beside, toward[edge])).astype(BF16)
        second_one = (block(second_ref, one) - dot(now, toward[one])).astype(BF16)
        then[edge] = then[edge] - dot(beside_next, toward[edge]) - dot(second_one, away[edge])
        then[one] = then[one] - dot(second, toward[one])
        then[two] = then[two] - dot(second_one, toward[two])
    for b in range(BLK):
        solved = then[b].astype(BF16).astype(F32)
        shares = (solved * block(weight, b)).astype(BF16)
        by_high_digit(spread, shares, high_ref, b)
    put_in_order(ordered, spread, hot_ref)
    owners = send_ref.shape[0]
    pieces = (send_ref.shape[1] - TAIL) // INC
    for o in range(owners):
        piece = owner_window(ordered, bounds_ref[o, 0], pieces)
        parts = [piece[:, j * LANES : (j + 1) * LANES] for j in range(pieces)]
        stage[o] = jnp.concatenate(parts + [tails_ref[o]], axis=0).astype(BF16)
        pltpu.make_async_copy(stage.at[o], send_ref.at[o], sent.at[o]).start()
    for o in range(owners):
        pltpu.make_async_copy(stage.at[o], send_ref.at[o], sent.at[o]).wait()


def by_high_digit(spread, values, high_ref, b):
    rows = values.shape[0]
    high = high_ref[b : b + 1, :].astype(F32).astype(BF16)
    for h in range(BLK):
        spread[h * rows : (h + 1) * rows, b * TILE : (b + 1) * TILE] = jnp.where(
            high == h, values, jnp.zeros_like(values)
        )


def put_in_order(ordered, spread, hot_ref):
    rows = ordered.shape[0]
    sorted_rows = dot(spread[...], hot_ref[...])
    for h in range(BLK):
        ordered[:, h * TILE : (h + 1) * TILE] = sorted_rows[h * rows : (h + 1) * rows]
    ordered[:, NP_DEV:] = jnp.zeros((rows, ordered.shape[1] - NP_DEV), F32)


def owner_window(ordered, begin, pieces):
    wide = (pieces + 1) * LANES
    base = pl.multiple_of((begin // LANES) * LANES, LANES)
    return pltpu.roll(ordered[:, pl.ds(base, wide)], wide - (begin - base), 1)


def tails_body(index_rows, high_ref, hot_ref, bounds_ref, out_ref, spread, ordered):
    for b in range(BLK):
        by_high_digit(spread, block(index_rows, b), high_ref, b)
    put_in_order(ordered, spread, hot_ref)
    pieces = ordered.shape[1] // LANES - NP_DEV // LANES - 1
    row = iota((TAIL, LANES), 0)
    slot = iota((TAIL, LANES), 1) + (row // 2) * LANES
    for o in range(out_ref.shape[0]):
        piece = owner_window(ordered, bounds_ref[o, 0], pieces)
        tail = piece[:TAIL, :LANES]
        for j in range(1, pieces):
            tail = jnp.where(row // 2 == j, piece[:TAIL, j * LANES : (j + 1) * LANES], tail)
        out_ref[o] = jnp.where(slot >= bounds_ref[o, 1], -16.0, tail)


def gather_body(
    arrived_ref, compress, couple_ref, field_out, coef_out, give_out, index, spread, hot,
):
    owners, rows, _ = arrived_ref.shape
    pieces = (rows - TAIL) // INC
    for e in range(owners):
        tail = arrived_ref[e].astype(F32)[INC * pieces :]
        marks = tail.astype(BF16)
        for j in range(pieces):
            k = e * pieces + j
            part = arrived_ref[e, j * INC : (j + 1) * INC, :]
            high = marks[2 * j : 2 * j + 1]
            index[k : k + 1, :] = tail[2 * j + 1 : 2 * j + 2]
            for h in range(BLK):
                spread[h * INC : (h + 1) * INC, k * LANES : (k + 1) * LANES] = jnp.where(
                    high == h, part, jnp.zeros_like(part)
                )
    fill_hot(hot, index[...].T)
    field = dot(spread[...], hot[...]).astype(BF16)
    for b in range(BLK):
        field_out[b] = field[b * INC : (b + 1) * INC]
    coef = coefficients(field, compress).astype(BF16)
    coef_out[...] = coef
    other = 1 - lax.axis_index("surf") % 2
    for c in range(give_out.shape[0]):
        give_out[c] = dot(coef, owner_columns(couple_ref, c, other)).astype(BF16)


def owner_columns(couple_ref, chip, core):
    return couple_ref[:, pl.ds(pl.multiple_of((2 * chip + core) * TILE, TILE), TILE)]


def own_body(coef_ref, couple_ref, out_ref):
    core = lax.axis_index("surf") % 2
    for c in range(out_ref.shape[0]):
        out_ref[c] = dot(coef_ref[...], owner_columns(couple_ref, c, core))


def merge_body(own_ref, got_ref, out_ref):
    out_ref[...] = (own_ref[...] + got_ref[...].astype(F32)).astype(BF16)


def couple_body(coupling, source, owner, place, basis, out_ref, basis_out, total, lanes):
    tiles, width = lanes.shape[0], BLK * RANK
    flat = RANK * RANK
    total[...] = jnp.zeros_like(total)
    coupling = ready(coupling)
    lanes[...] = coupling[...].astype(F32)
    keep = (iota((RANK, flat), 1) % RANK) == iota((RANK, flat), 0)
    fold = as_hot((iota((flat, width), 0) // RANK) == (iota((flat, width), 1) % RANK))
    number = iota((RANK, width), 1) // RANK
    source, owner, place = ready(source), ready(owner), ready(place)
    group = 8

    def step(c, carry):
        begin = pl.multiple_of(c * group, group)
        rows = lanes[pl.ds(begin, group), :]
        tall = [jnp.where(keep, rows[k : k + 1], 0.0).astype(BF16) for k in range(group)]
        turned = dot(jnp.concatenate(tall, axis=0), fold)
        for k in range(group):
            f = begin + k
            tile = jnp.where(number == source[0, f], turned[k * RANK : (k + 1) * RANK], 0.0)
            total[owner[0, f] * BLK + place[0, f]] += tile
        return carry

    lax.fori_loop(0, tiles // group, step, 0)
    for o in range(out_ref.shape[1] // TILE):
        part = total[o * BLK : (o + 1) * BLK].reshape(TILE, width)
        out_ref[:, o * TILE : (o + 1) * TILE] = part.T.astype(BF16)
    basis_out[...] = ready(basis)[...]


def self_body(field_ref, tiles, basis, out_ref, basis_out):
    basis_out[...] = ready(basis)[...]
    tiles = ready(tiles)
    for b in range(BLK):
        out_ref[:, b * TILE : (b + 1) * TILE] = dot(field_ref[b], tiles[b])


def answer_body(arrived_ref, near_ref, expand, out_ref, spread):
    total = jnp.sum(arrived_ref[...].astype(F32), axis=0)
    number = iota(total.shape, 1) // RANK
    for b in range(BLK):
        spread[b * INC : (b + 1) * INC, :] = jnp.where(number == b, total, 0.0).astype(BF16)
    far = dot(spread[...], expand[...].reshape(BLK * RANK, TILE))
    for b in range(BLK):
        out_ref[:, b * TILE : (b + 1) * TILE] = (
            block(near_ref, b) + far[b * INC : (b + 1) * INC]
        ).astype(BF16)


def swap_inner(array, surf_count):
    return lax.ppermute(array, "surf", [(i, i ^ 1) for i in range(surf_count)])


def swap_outer(array, surf_count):
    pairs = [(0, 0), (surf_count - 1, surf_count - 1)]
    for i in range(1, surf_count - 1, 2):
        pairs += [(i, i + 1), (i + 1, i)]
    return lax.ppermute(array, "surf", pairs)


def exchange(array, surf_count):
    shape = array.shape
    array = array.reshape((surf_count, shape[0] // surf_count) + shape[1:])
    array = lax.all_to_all(array, "surf", split_axis=0, concat_axis=0, tiled=True)
    return array.reshape(shape)


def shards(
    currents, near_tiles, near_target, near_source, primal_compress, primal_expand, primal_coupling,
    far_source, far_owner, far_block, gram_inverse, gram_lower, gram_upper, refine_weight,
    dual_owner, dual_index, dual_self, dual_compress, dual_expand, dual_coupling,
):
    surf_count = lax.axis_size("surf")
    tiles = far_source.shape[0]
    near_count = near_tiles.shape[0]
    targets = surf_count * BLK
    capacity = max(2, 2 * NP_DEV // surf_count)
    pieces = -(-capacity // LANES)
    lists = (far_source.reshape(1, tiles), far_owner.reshape(1, tiles), far_block.reshape(1, tiles))
    cube = ((BLK, TILE, TILE), BF16)

    note = ((3 * INC + TILE, TILE), BF16)
    outer = swap_outer(currents, surf_count)
    partial, inner = call(
        far_up_body,
        [((targets, INC * RANK), BF16), ((INC, NP_DEV), BF16)],
        (currents, primal_compress, primal_coupling) + lists,
        scratch=far_scratch(tiles)
        + [pltpu.VMEM((targets, INC * RANK), BF16), pltpu.SemaphoreType.DMA((4,))],
        streamed=(0,),
        held=(2, 0, 1, 3, 4, 5),
        flops=10**11,
        name="far_up",
    )
    arrived = exchange(partial, surf_count)
    inner = swap_inner(inner, surf_count)
    near_part, lower, upper, expanded = call(
        prepare_body,
        [((INC, NP_DEV), F32), cube, cube, ((BLK, RANK, TILE), BF16)],
        (
            near_target, near_source, currents, inner, outer, gram_inverse, gram_lower, gram_upper,
            primal_expand, near_tiles,
        ),
        scratch=[
            pltpu.VMEM((BLK + 2, INC, TILE), BF16),
            pltpu.VMEM((BLK, INC, TILE), F32),
            pltpu.VMEM((near_count, INC, TILE), F32),
            pltpu.VMEM((2,) + currents.shape, BF16),
            pltpu.VMEM(near_tiles.shape, BF16),
            pltpu.SemaphoreType.DMA((near_count // NEAR_CHUNK,)),
        ],
        held=(5, 6, 7, 8, 2, 0, 1),
        far=(9,),
        small=(0, 1),
        flops=10**11,
        name="prepare",
    )
    start, after, inner_note, outer_note = call(
        solve_body,
        [((INC, NP_DEV), F32)] * 2 + [note] * 2,
        (arrived, near_part, expanded, lower, upper),
        scratch=[
            pltpu.VMEM((2,) + note[0], BF16),
            pltpu.VMEM((BLK * INC, INC * RANK), BF16),
        ],
        name="solve",
    )
    outer_note = swap_outer(outer_note, surf_count)
    high, hot, bounds, index_rows, weight = call(
        order_body,
        [
            ((BLK, TILE), I32), ((NP_DEV, TILE), BF16), ((surf_count, 2), I32),
            ((IDX_ROWS, NP_DEV), BF16), ((1, NP_DEV), F32),
        ],
        (
            dual_owner.reshape(1, NP_DEV), dual_index.reshape(1, NP_DEV),
            refine_weight.reshape(1, NP_DEV), start,
        ),
        scratch=[pltpu.VMEM((BLK, TILE), F32)],
        held=(0, 1, 2),
        flops=10**9,
        name="order",
    )
    (tails,) = call(
        tails_body,
        [((surf_count, TAIL, LANES), F32)],
        (index_rows, high, hot, bounds),
        scratch=[
            pltpu.VMEM((BLK * IDX_ROWS, NP_DEV), BF16),
            pltpu.VMEM((IDX_ROWS, NP_DEV + (pieces + 1) * LANES), F32),
        ],
        smem=(3,),
        flops=10**9,
        name="tails",
    )
    second, third, inner_note = call(
        middle_body,
        [((INC, NP_DEV), F32)] * 2 + [note],
        (start, after, lower, upper, inner_note),
        flops=10**9,
        name="middle",
    )
    inner_note = swap_inner(inner_note, surf_count)
    (send,) = call(
        finish_body,
        [((surf_count, INC * pieces + TAIL, LANES), BF16)],
        (
            start, after, second, third, inner_note, outer_note, lower, upper,
            weight, tails, high, hot, bounds,
        ),
        scratch=[
            pltpu.VMEM((2,) + note[0], BF16),
            pltpu.VMEM((BLK * INC, NP_DEV), BF16),
            pltpu.VMEM((INC, NP_DEV + (pieces + 1) * LANES), F32),
            pltpu.VMEM((surf_count, INC * pieces + TAIL, LANES), BF16),
            pltpu.SemaphoreType.DMA((surf_count,)),
        ],
        streamed=(0,),
        smem=(12,),
        name="finish",
    )
    shares = lax.all_to_all(send, "surf", split_axis=0, concat_axis=0, tiled=True)
    slots = surf_count * pieces * LANES
    couple, compress = call(
        couple_body,
        [((BLK * RANK, targets * RANK), BF16), (dual_compress.shape, BF16)],
        (dual_coupling,) + lists + (dual_compress,),
        scratch=[pltpu.VMEM((targets, RANK, BLK * RANK), F32), pltpu.VMEM((tiles, INC * RANK), F32)],
        held=(0, 1, 2, 3, 4),
        small=(1, 2, 3),
        flops=10**10,
        name="couple",
    )
    half = (surf_count // 2, INC, BLK * RANK)
    field, coef, give = call(
        gather_body,
        [((BLK, INC, TILE), BF16), ((INC, BLK * RANK), BF16), (half, BF16)],
        (shares, compress, couple),
        scratch=[
            pltpu.VMEM((surf_count * pieces, LANES), F32),
            pltpu.VMEM((BLK * INC, slots), BF16),
            pltpu.VMEM((slots, TILE), BF16),
        ],
        name="gather",
    )
    got = lax.ppermute(give, "surf", [(i, i ^ 1) for i in range(surf_count)])
    (own,) = call(own_body, [(half, F32)], (coef, couple), flops=10**9, name="own")
    (merged,) = call(merge_body, [(half, BF16)], (own, got), name="merge")
    arrived = lax.all_to_all(
        merged,
        "surf",
        split_axis=0,
        concat_axis=0,
        tiled=True,
        axis_index_groups=[list(range(core, surf_count, 2)) for core in range(2)],
    )
    near_dual, expand = call(
        self_body,
        [((INC, NP_DEV), F32), (dual_expand.shape, BF16)],
        (field, dual_self, dual_expand),
        held=(2, 1),
        name="self_part",
    )
    (response,) = call(
        answer_body,
        [((INC, NP_DEV), BF16)],
        (arrived, near_dual, expand),
        scratch=[pltpu.VMEM((BLK * INC, BLK * RANK), BF16)],
        name="answer",
    )
    return response


def solution(mesh):
    both = ("groups", "surf")
    row, flat = P(None, both), P(both)
    cube, flat2 = P(both, None, None), P(both, None)
    return jax.shard_map(
        shards,
        mesh=mesh,
        in_specs=(
            row, cube, flat, flat, cube, cube, flat2, flat, flat2, flat, cube, cube, cube, flat,
            flat2, flat, cube, cube, cube, flat2,
        ),
        out_specs=row,
        check_vma=False,
    )
```

```python
import jax
import jax.numpy as jnp
from jax import lax
from jax.experimental import pallas as pl
from jax.experimental.pallas import tpu as pltpu
from jax.sharding import PartitionSpec as P

TILE = 256
INC = 32
RANK = 32
BLK = 8
NP_DEV = 2048
LANES = 128
IDX_ROWS = 16
TAIL = 8
NEAR_CHUNK = 8
F32 = jnp.float32
BF16 = jnp.bfloat16
I32 = jnp.int32
NT = (((1,), (1,)), ((), ()))
VMEM_LIMIT = 36 * 1024 * 1024


def dot(a, b):
    return jnp.dot(a, b, preferred_element_type=F32)


def dot_nt(a, b):
    return lax.dot_general(a, b, NT, preferred_element_type=F32)


def iota(shape, dim):
    return lax.broadcasted_iota(I32, shape, dim)


def block(array, i):
    return array[:, i * TILE : (i + 1) * TILE]


def as_hot(mask):
    return mask.astype(F32).astype(BF16)


def call(body, outs, args, scratch=(), smem=(), held=(), far=(), small=(), streamed=(), flops=0, name=None):
    spaces = [
        pltpu.SMEM if k in smem else pltpu.HBM if k in held or k in far else pltpu.VMEM
        for k in range(len(args))
    ]
    size = sum(a.size * a.dtype.itemsize for a in args)
    outs = tuple(
        jax.ShapeDtypeStruct(s, d) for s, d in outs
    )
    buffers = [
        (pltpu.SMEM if k in small else pltpu.VMEM)(args[k].shape, args[k].dtype) for k in held
    ]
    waits = [pltpu.SemaphoreType.DMA(()) for _ in held]

    def wrapped(*refs):
        ins = list(refs[: len(args)])
        rest = refs[len(args) : len(refs) - 2 * len(held)]
        extra = refs[len(refs) - 2 * len(held) :]
        for n, k in enumerate(held):
            ins[k] = pltpu.make_async_copy(ins[k], extra[n], extra[len(held) + n])
            ins[k].start()
            ins[k] = (ins[k], extra[n])
        body(*ins, *rest)

    return pl.pallas_call(
        wrapped,
        out_shape=outs,
        in_specs=[pl.BlockSpec(memory_space=m) for m in spaces],
        out_specs=tuple(
            pl.BlockSpec(memory_space=pl.ANY if k in streamed else pltpu.VMEM)
            for k in range(len(outs))
        ),
        scratch_shapes=list(scratch) + buffers + waits,
        compiler_params=pltpu.CompilerParams(vmem_limit_bytes=VMEM_LIMIT),
        cost_estimate=pl.CostEstimate(flops=flops, bytes_accessed=size, transcendentals=0),
        name=name,
    )(*[pltpu.with_memory_space_constraint(a, m) if m is pltpu.HBM else a for a, m in zip(args, spaces)])


def ready(operand):
    operand[0].wait()
    return operand[1]


def fill_hot(hot, columns):
    height, count = columns.shape
    columns = columns.astype(BF16)
    lane = iota((height, TILE), 1).astype(F32).astype(BF16)
    one, zero = jnp.ones((height, TILE), BF16), jnp.zeros((height, TILE), BF16)
    for k in range(count):
        hot[k * height : (k + 1) * height, :] = jnp.where(lane == columns[:, k : k + 1], one, zero)


def coefficients(blocks, compress):
    width = BLK * RANK
    every = dot_nt(blocks, compress[...].reshape(width, TILE))
    owner = iota((INC, width), 1) // RANK
    coef = jnp.zeros((INC, width), F32)
    for s in range(BLK):
        coef = jnp.where(owner == s, every[s * INC : (s + 1) * INC], coef)
    return coef


def far_up_body(
    value, compress, coupling, source, owner, place,
    out_ref, blocks, turned, spread, pick, terms,
):
    coupling = ready(coupling)
    turned[...] = coupling[...].astype(F32).T
    value, compress = ready(value), ready(compress)
    for s in range(BLK):
        blocks[s * INC : (s + 1) * INC, :] = block(value, s)
    coef = coefficients(blocks[...], compress)
    width = BLK * RANK
    keep = (iota((RANK, width), 1) % RANK) == iota((RANK, width), 0)
    for i in range(INC):
        spread[i * RANK : (i + 1) * RANK, :] = jnp.where(keep, coef[i : i + 1, :], 0.0).astype(BF16)
    source = ready(source)
    tiles = source.shape[1]
    pick[...] = dot(spread[...], as_hot((iota((width, tiles), 0) // RANK) == source[...]))

    def step(pair, carry):
        rows = pl.multiple_of(pair * (2 * RANK), 2 * RANK)
        got = pick[pl.ds(rows, 2 * RANK), :]
        first = jnp.zeros((RANK, tiles), F32)
        second = jnp.zeros((RANK, tiles), F32)
        for r in range(RANK):
            factor = turned[r * RANK : (r + 1) * RANK, :]
            first += got[r : r + 1, :] * factor
            second += got[RANK + r : RANK + r + 1, :] * factor
        terms[pl.ds(rows, 2 * RANK), :] = jnp.concatenate([first, second], axis=0).astype(BF16)
        return carry

    lax.fori_loop(0, INC // 2, step, 0)
    targets = out_ref.shape[0]
    owner, place = ready(owner), ready(place)
    select = as_hot(iota((targets, tiles), 0) == owner[...] * BLK + place[...])
    out_ref[...] = dot_nt(select, terms[...]).astype(BF16)


def far_scratch(tiles):
    return [
        pltpu.VMEM((BLK * INC, TILE), BF16),
        pltpu.VMEM((RANK * RANK, tiles), F32),
        pltpu.VMEM((INC * RANK, BLK * RANK), BF16),
        pltpu.VMEM((INC * RANK, tiles), F32),
        pltpu.VMEM((INC * RANK, tiles), BF16),
    ]


def far_sums(arrived_ref, spread):
    rows = arrived_ref.shape[0]
    total = jnp.sum(arrived_ref[...].astype(F32).reshape(rows // BLK, BLK, INC * RANK), axis=0)
    width = INC * RANK
    keep = (iota((INC, width), 1) // RANK) == iota((INC, width), 0)
    for b in range(BLK):
        spread[b * INC : (b + 1) * INC, :] = jnp.where(keep, total[b : b + 1, :], 0.0).astype(BF16)
    fold = as_hot((iota((width, RANK), 0) % RANK) == iota((width, RANK), 1))
    return dot(spread[...], fold).astype(BF16)


def order_body(owner, index, weight, _, high_out, hot_out, bounds_out, rows_out, weight_out, ranks):
    owner, index = ready(owner), ready(index)
    owners = bounds_out.shape[0]
    pieces = -(-max(2, 2 * NP_DEV // owners) // LANES)
    before = as_hot(iota((TILE, TILE), 0) < iota((TILE, TILE), 1))
    number = iota((owners, TILE), 0)
    count = jnp.zeros((owners, 1), F32)
    begin = jnp.zeros((owners, 1), F32)
    hots, carries = [], []
    for c in range(BLK):
        names = block(owner, c)
        hot = (number == names).astype(F32)
        hots.append(hot)
        carries.append(count)
        count = count + jnp.sum(hot, axis=1, keepdims=True)
        begin = begin + jnp.sum((names < number).astype(F32), axis=1, keepdims=True)
    for c in range(BLK):
        rank = dot(hots[c].astype(BF16), before)
        ranks[c : c + 1, :] = jnp.sum(hots[c] * (rank + carries[c] + begin), axis=0, keepdims=True)
    spots = ranks[...].astype(I32)
    high_out[...] = spots // TILE
    fill_hot(hot_out, (spots % TILE).astype(F32).T)
    pair = iota((owners, 2), 1)
    bounds_out[...] = jnp.where(pair == 0, begin, count).astype(I32)
    row = iota((IDX_ROWS, NP_DEV), 0)
    index = index[...]
    digits = jnp.where(row % 2 == 0, index // TILE, index % TILE)
    rows_out[...] = jnp.where(row < 2 * pieces, digits, 0).astype(F32).astype(BF16)
    weight_out[...] = ready(weight)[...]


def prepare_body(
    target, origin, own, inner_ref, outer_ref, inverse, lower, upper, expand, tiles_ref,
    near_out, lower_out, upper_out, expand_out, cells, total, products, pair, tiles, arrivals,
):
    count = tiles_ref.shape[0]
    copies = []
    for c in range(count // NEAR_CHUNK):
        part = pl.ds(c * NEAR_CHUNK, NEAR_CHUNK)
        copy = pltpu.make_async_copy(tiles_ref.at[part], tiles.at[part], arrivals.at[c])
        copy.start()
        copies.append(copy)
    position = lax.axis_index("surf")
    odd = position % 2
    pair[0] = inner_ref[...]
    pair[1] = outer_ref[...]
    cells[0] = pair[1 - odd, :, NP_DEV - TILE :]
    cells[BLK + 1] = pair[odd, :, :TILE]
    inverse, lower, upper, expand = ready(inverse), ready(lower), ready(upper), ready(expand)
    for b in range(BLK):
        lower_out[b] = dot(lower[b], inverse[b]).astype(BF16)
        upper_out[b] = dot(upper[b], inverse[b]).astype(BF16)
        expand_out[b] = dot(expand[b], inverse[b]).astype(BF16)
    own, target, origin = ready(own), ready(target), ready(origin)
    for b in range(BLK):
        cells[b + 1] = block(own, b)
    total[...] = jnp.zeros_like(total)
    start = position * BLK - 1
    for c, copy in enumerate(copies):
        copy.wait()
        for k in range(c * NEAR_CHUNK, (c + 1) * NEAR_CHUNK):
            products[k] = dot(cells[origin[k] - start], tiles[k])
    for k in range(count):
        total[target[k]] += products[k]
    for b in range(BLK):
        near_out[:, b * TILE : (b + 1) * TILE] = dot(total[b].astype(BF16), inverse[b])


def solve_body(
    arrived_ref, near_ref, expand_ref, lower_ref, upper_ref,
    start_out, next_out, inner_out, outer_out, notes, spread,
):
    sums = far_sums(arrived_ref, spread)
    start, low = [], []
    for b in range(BLK):
        value = block(near_ref, b) + dot(sums[b * INC : (b + 1) * INC, :], expand_ref[b])
        start.append(value)
        low.append(value.astype(BF16))
        start_out[:, b * TILE : (b + 1) * TILE] = value
    after = []
    for b in range(BLK):
        value = start[b]
        if b > 0:
            value = value - dot(low[b - 1], lower_ref[b])
        if b < BLK - 1:
            value = value - dot(low[b + 1], upper_ref[b])
        after.append(value)
        next_out[:, b * TILE : (b + 1) * TILE] = value
    last = BLK - 1
    odd = lax.axis_index("surf") % 2
    for n, (edge, inside, away, back) in enumerate(
        ((last, last - 1, lower_ref, upper_ref), (0, 1, upper_ref, lower_ref))
    ):
        feedless = start[edge] - dot(after[inside].astype(BF16), away[edge])
        notes[n, 0:INC, :] = low[edge]
        notes[n, INC : 2 * INC, :] = after[edge].astype(BF16)
        notes[n, 2 * INC : 3 * INC, :] = feedless.astype(BF16)
        notes[n, 3 * INC :, :] = back[edge]
    inner_out[...] = notes[odd]
    outer_out[...] = notes[1 - odd]


def middle_body(
    start_ref, next_ref, lower_ref, upper_ref, note_ref, second_out, third_out, note_out
):
    note_out[...] = note_ref[...]
    last = BLK - 1
    now = [block(next_ref, b).astype(BF16) for b in range(BLK)]
    second = []
    for b in range(BLK):
        value = block(start_ref, b)
        if b > 1:
            value = value - dot(now[b - 1], lower_ref[b])
        if b < last - 1:
            value = value - dot(now[b + 1], upper_ref[b])
        second.append(value.astype(BF16))
        second_out[:, b * TILE : (b + 1) * TILE] = value
    for b in range(BLK):
        value = block(start_ref, b)
        if 2 < b < last:
            value = value - dot(second[b - 1], lower_ref[b])
        if 0 < b < last - 2:
            value = value - dot(second[b + 1], upper_ref[b])
        third_out[:, b * TILE : (b + 1) * TILE] = value


def finish_body(
    start_ref, next_ref, second_ref, third_ref, inner_note, outer_note, lower_ref, upper_ref,
    weight, tails_ref, high_ref, hot_ref, bounds_ref, send_ref,
    notes, spread, ordered, stage, sent,
):
    position = lax.axis_index("surf")
    odd = position % 2
    notes[0] = inner_note[...]
    notes[1] = outer_note[...]
    then = [block(third_ref, b) for b in range(BLK)]
    for left in (True, False):
        n = 1 - odd if left else odd
        exists = (position > 0) if left else (position < lax.axis_size("surf") - 1)
        exists = exists.astype(F32)
        edge, step = (0, 1) if left else (BLK - 1, -1)
        toward, away = (lower_ref, upper_ref) if left else (upper_ref, lower_ref)
        one, two = edge + step, edge + 2 * step
        first = block(start_ref, edge).astype(BF16)
        beyond = notes[n, 3 * INC :, :]
        beside = notes[n, INC : 2 * INC, :].astype(F32) - dot(first, beyond)
        beside = (beside * exists).astype(BF16)
        now = block(next_ref, edge) - dot(notes[n, 0:INC, :], toward[edge]) * exists
        now = now.astype(BF16)
        beside_next = notes[n, 2 * INC : 3 * INC, :].astype(F32) - dot(now, beyond)
        beside_next = (beside_next * exists).astype(BF16)
        second = (block(second_ref, edge) - dot(beside, toward[edge])).astype(BF16)
        second_one = (block(second_ref, one) - dot(now, toward[one])).astype(BF16)
        then[edge] = then[edge] - dot(beside_next, toward[edge]) - dot(second_one, away[edge])
        then[one] = then[one] - dot(second, toward[one])
        then[two] = then[two] - dot(second_one, toward[two])
    for b in range(BLK):
        solved = then[b].astype(BF16).astype(F32)
        shares = (solved * block(weight, b)).astype(BF16)
        by_high_digit(spread, shares, high_ref, b)
    put_in_order(ordered, spread, hot_ref)
    owners = send_ref.shape[0]
    pieces = (send_ref.shape[1] - TAIL) // INC
    for o in range(owners):
        piece = owner_window(ordered, bounds_ref[o, 0], pieces)
        parts = [piece[:, j * LANES : (j + 1) * LANES] for j in range(pieces)]
        stage[o] = jnp.concatenate(parts + [tails_ref[o]], axis=0).astype(BF16)
        pltpu.make_async_copy(stage.at[o], send_ref.at[o], sent.at[o]).start()
    for o in range(owners):
        pltpu.make_async_copy(stage.at[o], send_ref.at[o], sent.at[o]).wait()


def by_high_digit(spread, values, high_ref, b):
    rows = values.shape[0]
    high = high_ref[b : b + 1, :].astype(F32).astype(BF16)
    for h in range(BLK):
        spread[h * rows : (h + 1) * rows, b * TILE : (b + 1) * TILE] = jnp.where(
            high == h, values, jnp.zeros_like(values)
        )


def put_in_order(ordered, spread, hot_ref):
    rows = ordered.shape[0]
    sorted_rows = dot(spread[...], hot_ref[...])
    for h in range(BLK):
        ordered[:, h * TILE : (h + 1) * TILE] = sorted_rows[h * rows : (h + 1) * rows]
    ordered[:, NP_DEV:] = jnp.zeros((rows, ordered.shape[1] - NP_DEV), F32)


def owner_window(ordered, begin, pieces):
    wide = (pieces + 1) * LANES
    base = pl.multiple_of((begin // LANES) * LANES, LANES)
    return pltpu.roll(ordered[:, pl.ds(base, wide)], wide - (begin - base), 1)


def tails_body(index_rows, high_ref, hot_ref, bounds_ref, out_ref, spread, ordered):
    for b in range(BLK):
        by_high_digit(spread, block(index_rows, b), high_ref, b)
    put_in_order(ordered, spread, hot_ref)
    pieces = ordered.shape[1] // LANES - NP_DEV // LANES - 1
    row = iota((TAIL, LANES), 0)
    slot = iota((TAIL, LANES), 1) + (row // 2) * LANES
    for o in range(out_ref.shape[0]):
        piece = owner_window(ordered, bounds_ref[o, 0], pieces)
        tail = piece[:TAIL, :LANES]
        for j in range(1, pieces):
            tail = jnp.where(row // 2 == j, piece[:TAIL, j * LANES : (j + 1) * LANES], tail)
        out_ref[o] = jnp.where(slot >= bounds_ref[o, 1], -16.0, tail)


def gather_body(
    arrived_ref, compress, couple_ref, field_out, coef_out, give_out, index, spread, hot,
):
    owners, rows, _ = arrived_ref.shape
    pieces = (rows - TAIL) // INC
    for e in range(owners):
        tail = arrived_ref[e].astype(F32)[INC * pieces :]
        marks = tail.astype(BF16)
        for j in range(pieces):
            k = e * pieces + j
            part = arrived_ref[e, j * INC : (j + 1) * INC, :]
            high = marks[2 * j : 2 * j + 1]
            index[k : k + 1, :] = tail[2 * j + 1 : 2 * j + 2]
            for h in range(BLK):
                spread[h * INC : (h + 1) * INC, k * LANES : (k + 1) * LANES] = jnp.where(
                    high == h, part, jnp.zeros_like(part)
                )
    fill_hot(hot, index[...].T)
    field = dot(spread[...], hot[...]).astype(BF16)
    for b in range(BLK):
        field_out[b] = field[b * INC : (b + 1) * INC]
    coef = coefficients(field, compress).astype(BF16)
    coef_out[...] = coef
    other = 1 - lax.axis_index("surf") % 2
    for c in range(give_out.shape[0]):
        give_out[c] = dot(coef, owner_columns(couple_ref, c, other)).astype(BF16)


def owner_columns(couple_ref, chip, core):
    return couple_ref[:, pl.ds(pl.multiple_of((2 * chip + core) * TILE, TILE), TILE)]


def own_body(coef_ref, couple_ref, out_ref):
    core = lax.axis_index("surf") % 2
    for c in range(out_ref.shape[0]):
        out_ref[c] = dot(coef_ref[...], owner_columns(couple_ref, c, core))


def merge_body(own_ref, got_ref, out_ref):
    out_ref[...] = (own_ref[...] + got_ref[...].astype(F32)).astype(BF16)


def couple_body(coupling, source, owner, place, basis, out_ref, basis_out, total, lanes):
    tiles, width = lanes.shape[0], BLK * RANK
    flat = RANK * RANK
    total[...] = jnp.zeros_like(total)
    coupling = ready(coupling)
    lanes[...] = coupling[...].astype(F32)
    keep = (iota((RANK, flat), 1) % RANK) == iota((RANK, flat), 0)
    fold = as_hot((iota((flat, width), 0) // RANK) == (iota((flat, width), 1) % RANK))
    number = iota((RANK, width), 1) // RANK
    source, owner, place = ready(source), ready(owner), ready(place)
    group = 8

    def step(c, carry):
        begin = pl.multiple_of(c * group, group)
        rows = lanes[pl.ds(begin, group), :]
        tall = [jnp.where(keep, rows[k : k + 1], 0.0).astype(BF16) for k in range(group)]
        turned = dot(jnp.concatenate(tall, axis=0), fold)
        for k in range(group):
            f = begin + k
            tile = jnp.where(number == source[0, f], turned[k * RANK : (k + 1) * RANK], 0.0)
            total[owner[0, f] * BLK + place[0, f]] += tile
        return carry

    lax.fori_loop(0, tiles // group, step, 0)
    for o in range(out_ref.shape[1] // TILE):
        part = total[o * BLK : (o + 1) * BLK].reshape(TILE, width)
        out_ref[:, o * TILE : (o + 1) * TILE] = part.T.astype(BF16)
    basis_out[...] = ready(basis)[...]


def self_body(field_ref, tiles, basis, out_ref, basis_out):
    basis_out[...] = ready(basis)[...]
    tiles = ready(tiles)
    for b in range(BLK):
        out_ref[:, b * TILE : (b + 1) * TILE] = dot(field_ref[b], tiles[b])


def answer_body(arrived_ref, near_ref, expand, out_ref, spread):
    total = jnp.sum(arrived_ref[...].astype(F32), axis=0)
    number = iota(total.shape, 1) // RANK
    for b in range(BLK):
        spread[b * INC : (b + 1) * INC, :] = jnp.where(number == b, total, 0.0).astype(BF16)
    far = dot(spread[...], expand[...].reshape(BLK * RANK, TILE))
    for b in range(BLK):
        out_ref[:, b * TILE : (b + 1) * TILE] = (
            block(near_ref, b) + far[b * INC : (b + 1) * INC]
        ).astype(BF16)


def swap_inner(array, surf_count):
    return lax.ppermute(array, "surf", [(i, i ^ 1) for i in range(surf_count)])


def swap_outer(array, surf_count):
    pairs = [(0, 0), (surf_count - 1, surf_count - 1)]
    for i in range(1, surf_count - 1, 2):
        pairs += [(i, i + 1), (i + 1, i)]
    return lax.ppermute(array, "surf", pairs)


def exchange(array, surf_count):
    shape = array.shape
    array = array.reshape((surf_count, shape[0] // surf_count) + shape[1:])
    array = lax.all_to_all(array, "surf", split_axis=0, concat_axis=0, tiled=True)
    return array.reshape(shape)


def shards(
    currents, near_tiles, near_target, near_source, primal_compress, primal_expand, primal_coupling,
    far_source, far_owner, far_block, gram_inverse, gram_lower, gram_upper, refine_weight,
    dual_owner, dual_index, dual_self, dual_compress, dual_expand, dual_coupling,
):
    surf_count = lax.axis_size("surf")
    tiles = far_source.shape[0]
    near_count = near_tiles.shape[0]
    targets = surf_count * BLK
    capacity = max(2, 2 * NP_DEV // surf_count)
    pieces = -(-capacity // LANES)
    lists = (far_source.reshape(1, tiles), far_owner.reshape(1, tiles), far_block.reshape(1, tiles))
    cube = ((BLK, TILE, TILE), BF16)

    note = ((3 * INC + TILE, TILE), BF16)
    inner, outer = swap_inner(currents, surf_count), swap_outer(currents, surf_count)
    (partial,) = call(
        far_up_body,
        [((targets, INC * RANK), BF16)],
        (currents, primal_compress, primal_coupling) + lists,
        scratch=far_scratch(tiles),
        held=(2, 0, 1, 3, 4, 5),
        flops=10**11,
        name="far_up",
    )
    arrived = exchange(partial, surf_count)
    near_part, lower, upper, expanded = call(
        prepare_body,
        [((INC, NP_DEV), F32), cube, cube, ((BLK, RANK, TILE), BF16)],
        (
            near_target, near_source, currents, inner, outer, gram_inverse, gram_lower, gram_upper,
            primal_expand, near_tiles,
        ),
        scratch=[
            pltpu.VMEM((BLK + 2, INC, TILE), BF16),
            pltpu.VMEM((BLK, INC, TILE), F32),
            pltpu.VMEM((near_count, INC, TILE), F32),
            pltpu.VMEM((2,) + currents.shape, BF16),
            pltpu.VMEM(near_tiles.shape, BF16),
            pltpu.SemaphoreType.DMA((near_count // NEAR_CHUNK,)),
        ],
        held=(5, 6, 7, 8, 2, 0, 1),
        far=(9,),
        small=(0, 1),
        flops=10**11,
        name="prepare",
    )
    start, after, inner_note, outer_note = call(
        solve_body,
        [((INC, NP_DEV), F32)] * 2 + [note] * 2,
        (arrived, near_part, expanded, lower, upper),
        scratch=[
            pltpu.VMEM((2,) + note[0], BF16),
            pltpu.VMEM((BLK * INC, INC * RANK), BF16),
        ],
        name="solve",
    )
    outer_note = swap_outer(outer_note, surf_count)
    high, hot, bounds, index_rows, weight = call(
        order_body,
        [
            ((BLK, TILE), I32), ((NP_DEV, TILE), BF16), ((surf_count, 2), I32),
            ((IDX_ROWS, NP_DEV), BF16), ((1, NP_DEV), F32),
        ],
        (
            dual_owner.reshape(1, NP_DEV), dual_index.reshape(1, NP_DEV),
            refine_weight.reshape(1, NP_DEV), start,
        ),
        scratch=[pltpu.VMEM((BLK, TILE), F32)],
        held=(0, 1, 2),
        flops=10**9,
        name="order",
    )
    (tails,) = call(
        tails_body,
        [((surf_count, TAIL, LANES), F32)],
        (index_rows, high, hot, bounds),
        scratch=[
            pltpu.VMEM((BLK * IDX_ROWS, NP_DEV), BF16),
            pltpu.VMEM((IDX_ROWS, NP_DEV + (pieces + 1) * LANES), F32),
        ],
        smem=(3,),
        flops=10**9,
        name="tails",
    )
    second, third, inner_note = call(
        middle_body,
        [((INC, NP_DEV), F32)] * 2 + [note],
        (start, after, lower, upper, inner_note),
        flops=10**9,
        name="middle",
    )
    inner_note = swap_inner(inner_note, surf_count)
    (send,) = call(
        finish_body,
        [((surf_count, INC * pieces + TAIL, LANES), BF16)],
        (
            start, after, second, third, inner_note, outer_note, lower, upper,
            weight, tails, high, hot, bounds,
        ),
        scratch=[
            pltpu.VMEM((2,) + note[0], BF16),
            pltpu.VMEM((BLK * INC, NP_DEV), BF16),
            pltpu.VMEM((INC, NP_DEV + (pieces + 1) * LANES), F32),
            pltpu.VMEM((surf_count, INC * pieces + TAIL, LANES), BF16),
            pltpu.SemaphoreType.DMA((surf_count,)),
        ],
        streamed=(0,),
        smem=(12,),
        name="finish",
    )
    shares = lax.all_to_all(send, "surf", split_axis=0, concat_axis=0, tiled=True)
    slots = surf_count * pieces * LANES
    couple, compress = call(
        couple_body,
        [((BLK * RANK, targets * RANK), BF16), (dual_compress.shape, BF16)],
        (dual_coupling,) + lists + (dual_compress,),
        scratch=[pltpu.VMEM((targets, RANK, BLK * RANK), F32), pltpu.VMEM((tiles, INC * RANK), F32)],
        held=(0, 1, 2, 3, 4),
        small=(1, 2, 3),
        flops=10**10,
        name="couple",
    )
    half = (surf_count // 2, INC, BLK * RANK)
    field, coef, give = call(
        gather_body,
        [((BLK, INC, TILE), BF16), ((INC, BLK * RANK), BF16), (half, BF16)],
        (shares, compress, couple),
        scratch=[
            pltpu.VMEM((surf_count * pieces, LANES), F32),
            pltpu.VMEM((BLK * INC, slots), BF16),
            pltpu.VMEM((slots, TILE), BF16),
        ],
        name="gather",
    )
    got = lax.ppermute(give, "surf", [(i, i ^ 1) for i in range(surf_count)])
    (own,) = call(own_body, [(half, F32)], (coef, couple), flops=10**9, name="own")
    (merged,) = call(merge_body, [(half, BF16)], (own, got), name="merge")
    arrived = lax.all_to_all(
        merged,
        "surf",
        split_axis=0,
        concat_axis=0,
        tiled=True,
        axis_index_groups=[list(range(core, surf_count, 2)) for core in range(2)],
    )
    near_dual, expand = call(
        self_body,
        [((INC, NP_DEV), F32), (dual_expand.shape, BF16)],
        (field, dual_self, dual_expand),
        held=(2, 1),
        name="self_part",
    )
    (response,) = call(
        answer_body,
        [((INC, NP_DEV), BF16)],
        (arrived, near_dual, expand),
        scratch=[pltpu.VMEM((BLK * INC, BLK * RANK), BF16)],
        name="answer",
    )
    return response


def solution(mesh):
    both = ("groups", "surf")
    row, flat = P(None, both), P(both)
    cube, flat2 = P(both, None, None), P(both, None)
    return jax.shard_map(
        shards,
        mesh=mesh,
        in_specs=(
            row, cube, flat, flat, cube, cube, flat2, flat, flat2, flat, cube, cube, cube, flat,
            flat2, flat, cube, cube, cube, flat2,
        ),
        out_specs=row,
        check_vma=False,
    )
```

```python
import jax
import jax.numpy as jnp
from jax import lax
from jax.experimental import pallas as pl
from jax.experimental.pallas import tpu as pltpu
from jax.sharding import PartitionSpec as P

TILE = 256
INC = 32
RANK = 32
BLK = 8
NP_DEV = 2048
LANES = 128
IDX_ROWS = 16
TAIL = 8
NEAR_CHUNK = 8
F32 = jnp.float32
BF16 = jnp.bfloat16
I32 = jnp.int32
NT = (((1,), (1,)), ((), ()))
VMEM_LIMIT = 36 * 1024 * 1024


def dot(a, b):
    return jnp.dot(a, b, preferred_element_type=F32)


def dot_nt(a, b):
    return lax.dot_general(a, b, NT, preferred_element_type=F32)


def iota(shape, dim):
    return lax.broadcasted_iota(I32, shape, dim)


def block(array, i):
    return array[:, i * TILE : (i + 1) * TILE]


def as_hot(mask):
    return mask.astype(F32).astype(BF16)


def call(body, outs, args, scratch=(), smem=(), held=(), far=(), loose=(), small=(), streamed=(), flops=0, name=None):
    spaces = [
        pltpu.SMEM
        if k in smem
        else pl.ANY
        if k in loose
        else pltpu.HBM
        if k in held or k in far
        else pltpu.VMEM
        for k in range(len(args))
    ]
    size = sum(a.size * a.dtype.itemsize for a in args)
    outs = tuple(
        jax.ShapeDtypeStruct(s, d) for s, d in outs
    )
    buffers = [
        (pltpu.SMEM if k in small else pltpu.VMEM)(args[k].shape, args[k].dtype) for k in held
    ]
    waits = [pltpu.SemaphoreType.DMA(()) for _ in held]

    def wrapped(*refs):
        ins = list(refs[: len(args)])
        rest = refs[len(args) : len(refs) - 2 * len(held)]
        extra = refs[len(refs) - 2 * len(held) :]
        for n, k in enumerate(held):
            ins[k] = pltpu.make_async_copy(ins[k], extra[n], extra[len(held) + n])
            ins[k].start()
            ins[k] = (ins[k], extra[n])
        body(*ins, *rest)

    return pl.pallas_call(
        wrapped,
        out_shape=outs,
        in_specs=[pl.BlockSpec(memory_space=m) for m in spaces],
        out_specs=tuple(
            pl.BlockSpec(memory_space=pl.ANY if k in streamed else pltpu.VMEM)
            for k in range(len(outs))
        ),
        scratch_shapes=list(scratch) + buffers + waits,
        compiler_params=pltpu.CompilerParams(vmem_limit_bytes=VMEM_LIMIT),
        cost_estimate=pl.CostEstimate(flops=flops, bytes_accessed=size, transcendentals=0),
        name=name,
    )(*[pltpu.with_memory_space_constraint(a, m) if m is pltpu.HBM else a for a, m in zip(args, spaces)])


def ready(operand):
    operand[0].wait()
    return operand[1]


def fill_hot(hot, columns):
    height, count = columns.shape
    columns = columns.astype(BF16)
    lane = iota((height, TILE), 1).astype(F32).astype(BF16)
    one, zero = jnp.ones((height, TILE), BF16), jnp.zeros((height, TILE), BF16)
    for k in range(count):
        hot[k * height : (k + 1) * height, :] = jnp.where(lane == columns[:, k : k + 1], one, zero)


def coefficients(blocks, compress):
    width = BLK * RANK
    every = dot_nt(blocks, compress[...].reshape(width, TILE))
    owner = iota((INC, width), 1) // RANK
    coef = jnp.zeros((INC, width), F32)
    for s in range(BLK):
        coef = jnp.where(owner == s, every[s * INC : (s + 1) * INC], coef)
    return coef


def far_up_body(
    value, compress, coupling, source, owner, place,
    out_ref, blocks, turned, spread, pick, terms,
):
    coupling = ready(coupling)
    turned[...] = coupling[...].astype(F32).T
    value, compress = ready(value), ready(compress)
    for s in range(BLK):
        blocks[s * INC : (s + 1) * INC, :] = block(value, s)
    coef = coefficients(blocks[...], compress)
    width = BLK * RANK
    keep = (iota((RANK, width), 1) % RANK) == iota((RANK, width), 0)
    for i in range(INC):
        spread[i * RANK : (i + 1) * RANK, :] = jnp.where(keep, coef[i : i + 1, :], 0.0).astype(BF16)
    source = ready(source)
    tiles = source.shape[1]
    pick[...] = dot(spread[...], as_hot((iota((width, tiles), 0) // RANK) == source[...]))

    def step(pair, carry):
        rows = pl.multiple_of(pair * (2 * RANK), 2 * RANK)
        got = pick[pl.ds(rows, 2 * RANK), :]
        first = jnp.zeros((RANK, tiles), F32)
        second = jnp.zeros((RANK, tiles), F32)
        for r in range(RANK):
            factor = turned[r * RANK : (r + 1) * RANK, :]
            first += got[r : r + 1, :] * factor
            second += got[RANK + r : RANK + r + 1, :] * factor
        terms[pl.ds(rows, 2 * RANK), :] = jnp.concatenate([first, second], axis=0).astype(BF16)
        return carry

    lax.fori_loop(0, INC // 2, step, 0)
    targets = out_ref.shape[0]
    owner, place = ready(owner), ready(place)
    select = as_hot(iota((targets, tiles), 0) == owner[...] * BLK + place[...])
    out_ref[...] = dot_nt(select, terms[...]).astype(BF16)


def far_scratch(tiles):
    return [
        pltpu.VMEM((BLK * INC, TILE), BF16),
        pltpu.VMEM((RANK * RANK, tiles), F32),
        pltpu.VMEM((INC * RANK, BLK * RANK), BF16),
        pltpu.VMEM((INC * RANK, tiles), F32),
        pltpu.VMEM((INC * RANK, tiles), BF16),
    ]


def far_sums(arrived_ref, spread):
    rows = arrived_ref.shape[0]
    total = jnp.sum(arrived_ref[...].astype(F32).reshape(rows // BLK, BLK, INC * RANK), axis=0)
    width = INC * RANK
    keep = (iota((INC, width), 1) // RANK) == iota((INC, width), 0)
    for b in range(BLK):
        spread[b * INC : (b + 1) * INC, :] = jnp.where(keep, total[b : b + 1, :], 0.0).astype(BF16)
    fold = as_hot((iota((width, RANK), 0) % RANK) == iota((width, RANK), 1))
    return dot(spread[...], fold).astype(BF16)


def order_body(owner, index, weight, _, high_out, hot_out, bounds_out, rows_out, weight_out, ranks):
    owner, index = ready(owner), ready(index)
    owners = bounds_out.shape[0]
    pieces = -(-max(2, 2 * NP_DEV // owners) // LANES)
    before = as_hot(iota((TILE, TILE), 0) < iota((TILE, TILE), 1))
    number = iota((owners, TILE), 0)
    count = jnp.zeros((owners, 1), F32)
    begin = jnp.zeros((owners, 1), F32)
    hots, carries = [], []
    for c in range(BLK):
        names = block(owner, c)
        hot = (number == names).astype(F32)
        hots.append(hot)
        carries.append(count)
        count = count + jnp.sum(hot, axis=1, keepdims=True)
        begin = begin + jnp.sum((names < number).astype(F32), axis=1, keepdims=True)
    for c in range(BLK):
        rank = dot(hots[c].astype(BF16), before)
        ranks[c : c + 1, :] = jnp.sum(hots[c] * (rank + carries[c] + begin), axis=0, keepdims=True)
    spots = ranks[...].astype(I32)
    high_out[...] = spots // TILE
    fill_hot(hot_out, (spots % TILE).astype(F32).T)
    pair = iota((owners, 2), 1)
    bounds_out[...] = jnp.where(pair == 0, begin, count).astype(I32)
    row = iota((IDX_ROWS, NP_DEV), 0)
    index = index[...]
    digits = jnp.where(row % 2 == 0, index // TILE, index % TILE)
    rows_out[...] = jnp.where(row < 2 * pieces, digits, 0).astype(F32).astype(BF16)
    weight_out[...] = ready(weight)[...]


def prepare_body(
    target, origin, own, inner_ref, outer_ref, inverse, lower, upper, expand, tiles_ref,
    near_out, lower_out, upper_out, expand_out, cells, total, products, pair, tiles, arrivals,
):
    count = tiles_ref.shape[0]
    copies = []
    for c in range(count // NEAR_CHUNK):
        part = pl.ds(c * NEAR_CHUNK, NEAR_CHUNK)
        copy = pltpu.make_async_copy(tiles_ref.at[part], tiles.at[part], arrivals.at[c])
        copy.start()
        copies.append(copy)
    position = lax.axis_index("surf")
    odd = position % 2
    pair[0] = inner_ref[...]
    pair[1] = outer_ref[...]
    cells[0] = pair[1 - odd, :, NP_DEV - TILE :]
    cells[BLK + 1] = pair[odd, :, :TILE]
    inverse, lower, upper, expand = ready(inverse), ready(lower), ready(upper), ready(expand)
    for b in range(BLK):
        lower_out[b] = dot(lower[b], inverse[b]).astype(BF16)
        upper_out[b] = dot(upper[b], inverse[b]).astype(BF16)
        expand_out[b] = dot(expand[b], inverse[b]).astype(BF16)
    own, target, origin = ready(own), ready(target), ready(origin)
    for b in range(BLK):
        cells[b + 1] = block(own, b)
    total[...] = jnp.zeros_like(total)
    start = position * BLK - 1
    for c, copy in enumerate(copies):
        copy.wait()
        for k in range(c * NEAR_CHUNK, (c + 1) * NEAR_CHUNK):
            products[k] = dot(cells[origin[k] - start], tiles[k])
    for k in range(count):
        total[target[k]] += products[k]
    for b in range(BLK):
        near_out[:, b * TILE : (b + 1) * TILE] = dot(total[b].astype(BF16), inverse[b])


def solve_body(
    arrived_ref, near_ref, expand_ref, lower_ref, upper_ref,
    start_out, next_out, inner_out, outer_out, notes, spread,
):
    sums = far_sums(arrived_ref, spread)
    start, low = [], []
    for b in range(BLK):
        value = block(near_ref, b) + dot(sums[b * INC : (b + 1) * INC, :], expand_ref[b])
        start.append(value)
        low.append(value.astype(BF16))
        start_out[:, b * TILE : (b + 1) * TILE] = value
    after = []
    for b in range(BLK):
        value = start[b]
        if b > 0:
            value = value - dot(low[b - 1], lower_ref[b])
        if b < BLK - 1:
            value = value - dot(low[b + 1], upper_ref[b])
        after.append(value)
        next_out[:, b * TILE : (b + 1) * TILE] = value
    last = BLK - 1
    odd = lax.axis_index("surf") % 2
    for n, (edge, inside, away, back) in enumerate(
        ((last, last - 1, lower_ref, upper_ref), (0, 1, upper_ref, lower_ref))
    ):
        feedless = start[edge] - dot(after[inside].astype(BF16), away[edge])
        notes[n, 0:INC, :] = low[edge]
        notes[n, INC : 2 * INC, :] = after[edge].astype(BF16)
        notes[n, 2 * INC : 3 * INC, :] = feedless.astype(BF16)
        notes[n, 3 * INC :, :] = back[edge]
    inner_out[...] = notes[odd]
    outer_out[...] = notes[1 - odd]


def middle_body(
    start_ref, next_ref, lower_ref, upper_ref, note_ref, second_out, third_out, note_out
):
    note_out[...] = note_ref[...]
    last = BLK - 1
    now = [block(next_ref, b).astype(BF16) for b in range(BLK)]
    second = []
    for b in range(BLK):
        value = block(start_ref, b)
        if b > 1:
            value = value - dot(now[b - 1], lower_ref[b])
        if b < last - 1:
            value = value - dot(now[b + 1], upper_ref[b])
        second.append(value.astype(BF16))
        second_out[:, b * TILE : (b + 1) * TILE] = value
    for b in range(BLK):
        value = block(start_ref, b)
        if 2 < b < last:
            value = value - dot(second[b - 1], lower_ref[b])
        if 0 < b < last - 2:
            value = value - dot(second[b + 1], upper_ref[b])
        third_out[:, b * TILE : (b + 1) * TILE] = value


def finish_body(
    start_ref, next_ref, second_ref, third_ref, inner_note, outer_note, lower_ref, upper_ref,
    weight, tails_ref, high_ref, hot_ref, bounds, send_ref,
    notes, spread, ordered, stage, sent,
):
    position = lax.axis_index("surf")
    odd = position % 2
    notes[0] = inner_note[...]
    notes[1] = outer_note[...]
    then = [block(third_ref, b) for b in range(BLK)]
    for left in (True, False):
        n = 1 - odd if left else odd
        exists = (position > 0) if left else (position < lax.axis_size("surf") - 1)
        exists = exists.astype(F32)
        edge, step = (0, 1) if left else (BLK - 1, -1)
        toward, away = (lower_ref, upper_ref) if left else (upper_ref, lower_ref)
        one, two = edge + step, edge + 2 * step
        first = block(start_ref, edge).astype(BF16)
        beyond = notes[n, 3 * INC :, :]
        beside = notes[n, INC : 2 * INC, :].astype(F32) - dot(first, beyond)
        beside = (beside * exists).astype(BF16)
        now = block(next_ref, edge) - dot(notes[n, 0:INC, :], toward[edge]) * exists
        now = now.astype(BF16)
        beside_next = notes[n, 2 * INC : 3 * INC, :].astype(F32) - dot(now, beyond)
        beside_next = (beside_next * exists).astype(BF16)
        second = (block(second_ref, edge) - dot(beside, toward[edge])).astype(BF16)
        second_one = (block(second_ref, one) - dot(now, toward[one])).astype(BF16)
        then[edge] = then[edge] - dot(beside_next, toward[edge]) - dot(second_one, away[edge])
        then[one] = then[one] - dot(second, toward[one])
        then[two] = then[two] - dot(second_one, toward[two])
    for b in range(BLK):
        solved = then[b].astype(BF16).astype(F32)
        shares = (solved * block(weight, b)).astype(BF16)
        by_high_digit(spread, shares, high_ref, b)
    put_in_order(ordered, spread, hot_ref)
    owners = send_ref.shape[0]
    pieces = (send_ref.shape[1] - TAIL) // INC
    bounds_ref = ready(bounds)
    for o in range(owners):
        piece = owner_window(ordered, bounds_ref[o, 0], pieces)
        parts = [piece[:, j * LANES : (j + 1) * LANES] for j in range(pieces)]
        stage[o] = jnp.concatenate(parts + [tails_ref[o]], axis=0).astype(BF16)
        pltpu.make_async_copy(stage.at[o], send_ref.at[o], sent.at[o]).start()
    for o in range(owners):
        pltpu.make_async_copy(stage.at[o], send_ref.at[o], sent.at[o]).wait()


def by_high_digit(spread, values, high_ref, b):
    rows = values.shape[0]
    high = high_ref[b : b + 1, :].astype(F32).astype(BF16)
    for h in range(BLK):
        spread[h * rows : (h + 1) * rows, b * TILE : (b + 1) * TILE] = jnp.where(
            high == h, values, jnp.zeros_like(values)
        )


def put_in_order(ordered, spread, hot_ref):
    rows = ordered.shape[0]
    sorted_rows = dot(spread[...], hot_ref[...])
    for h in range(BLK):
        ordered[:, h * TILE : (h + 1) * TILE] = sorted_rows[h * rows : (h + 1) * rows]
    ordered[:, NP_DEV:] = jnp.zeros((rows, ordered.shape[1] - NP_DEV), F32)


def owner_window(ordered, begin, pieces):
    wide = (pieces + 1) * LANES
    base = pl.multiple_of((begin // LANES) * LANES, LANES)
    return pltpu.roll(ordered[:, pl.ds(base, wide)], wide - (begin - base), 1)


def tails_body(index_rows, high_ref, hot_ref, bounds_ref, out_ref, spread, ordered):
    for b in range(BLK):
        by_high_digit(spread, block(index_rows, b), high_ref, b)
    put_in_order(ordered, spread, hot_ref)
    pieces = ordered.shape[1] // LANES - NP_DEV // LANES - 1
    row = iota((TAIL, LANES), 0)
    slot = iota((TAIL, LANES), 1) + (row // 2) * LANES
    for o in range(out_ref.shape[0]):
        piece = owner_window(ordered, bounds_ref[o, 0], pieces)
        tail = piece[:TAIL, :LANES]
        for j in range(1, pieces):
            tail = jnp.where(row // 2 == j, piece[:TAIL, j * LANES : (j + 1) * LANES], tail)
        out_ref[o] = jnp.where(slot >= bounds_ref[o, 1], -16.0, tail)


def gather_body(
    arrived_ref, compress, couple_ref, field_out, coef_out, give_out, index, spread, hot,
):
    owners, rows, _ = arrived_ref.shape
    pieces = (rows - TAIL) // INC
    for e in range(owners):
        tail = arrived_ref[e].astype(F32)[INC * pieces :]
        marks = tail.astype(BF16)
        for j in range(pieces):
            k = e * pieces + j
            part = arrived_ref[e, j * INC : (j + 1) * INC, :]
            high = marks[2 * j : 2 * j + 1]
            index[k : k + 1, :] = tail[2 * j + 1 : 2 * j + 2]
            for h in range(BLK):
                spread[h * INC : (h + 1) * INC, k * LANES : (k + 1) * LANES] = jnp.where(
                    high == h, part, jnp.zeros_like(part)
                )
    fill_hot(hot, index[...].T)
    field = dot(spread[...], hot[...]).astype(BF16)
    for b in range(BLK):
        field_out[b] = field[b * INC : (b + 1) * INC]
    coef = coefficients(field, compress).astype(BF16)
    coef_out[...] = coef
    other = 1 - lax.axis_index("surf") % 2
    for c in range(give_out.shape[0]):
        give_out[c] = dot(coef, owner_columns(couple_ref, c, other)).astype(BF16)


def owner_columns(couple_ref, chip, core):
    return couple_ref[:, pl.ds(pl.multiple_of((2 * chip + core) * TILE, TILE), TILE)]


def own_body(coef_ref, couple_ref, out_ref):
    core = lax.axis_index("surf") % 2
    for c in range(out_ref.shape[0]):
        out_ref[c] = dot(coef_ref[...], owner_columns(couple_ref, c, core))


def merge_body(own_ref, got_ref, out_ref):
    out_ref[...] = (own_ref[...] + got_ref[...].astype(F32)).astype(BF16)


def couple_body(coupling, source, owner, place, basis, out_ref, basis_out, total, lanes):
    tiles, width = lanes.shape[0], BLK * RANK
    flat = RANK * RANK
    total[...] = jnp.zeros_like(total)
    coupling = ready(coupling)
    lanes[...] = coupling[...].astype(F32)
    keep = (iota((RANK, flat), 1) % RANK) == iota((RANK, flat), 0)
    fold = as_hot((iota((flat, width), 0) // RANK) == (iota((flat, width), 1) % RANK))
    number = iota((RANK, width), 1) // RANK
    source, owner, place = ready(source), ready(owner), ready(place)
    group = 8

    def step(c, carry):
        begin = pl.multiple_of(c * group, group)
        rows = lanes[pl.ds(begin, group), :]
        tall = [jnp.where(keep, rows[k : k + 1], 0.0).astype(BF16) for k in range(group)]
        turned = dot(jnp.concatenate(tall, axis=0), fold)
        for k in range(group):
            f = begin + k
            tile = jnp.where(number == source[0, f], turned[k * RANK : (k + 1) * RANK], 0.0)
            total[owner[0, f] * BLK + place[0, f]] += tile
        return carry

    lax.fori_loop(0, tiles // group, step, 0)
    for o in range(out_ref.shape[1] // TILE):
        part = total[o * BLK : (o + 1) * BLK].reshape(TILE, width)
        out_ref[:, o * TILE : (o + 1) * TILE] = part.T.astype(BF16)
    basis_out[...] = ready(basis)[...]


def self_body(field_ref, tiles, basis, out_ref, basis_out):
    basis_out[...] = ready(basis)[...]
    tiles = ready(tiles)
    for b in range(BLK):
        out_ref[:, b * TILE : (b + 1) * TILE] = dot(field_ref[b], tiles[b])


def answer_body(arrived_ref, near_ref, expand, out_ref, spread):
    total = jnp.sum(arrived_ref[...].astype(F32), axis=0)
    number = iota(total.shape, 1) // RANK
    for b in range(BLK):
        spread[b * INC : (b + 1) * INC, :] = jnp.where(number == b, total, 0.0).astype(BF16)
    far = dot(spread[...], expand[...].reshape(BLK * RANK, TILE))
    for b in range(BLK):
        out_ref[:, b * TILE : (b + 1) * TILE] = (
            block(near_ref, b) + far[b * INC : (b + 1) * INC]
        ).astype(BF16)


def swap_inner(array, surf_count):
    return lax.ppermute(array, "surf", [(i, i ^ 1) for i in range(surf_count)])


def swap_outer(array, surf_count):
    pairs = [(0, 0), (surf_count - 1, surf_count - 1)]
    for i in range(1, surf_count - 1, 2):
        pairs += [(i, i + 1), (i + 1, i)]
    return lax.ppermute(array, "surf", pairs)


def exchange(array, surf_count):
    shape = array.shape
    array = array.reshape((surf_count, shape[0] // surf_count) + shape[1:])
    array = lax.all_to_all(array, "surf", split_axis=0, concat_axis=0, tiled=True)
    return array.reshape(shape)


def shards(
    currents, near_tiles, near_target, near_source, primal_compress, primal_expand, primal_coupling,
    far_source, far_owner, far_block, gram_inverse, gram_lower, gram_upper, refine_weight,
    dual_owner, dual_index, dual_self, dual_compress, dual_expand, dual_coupling,
):
    surf_count = lax.axis_size("surf")
    tiles = far_source.shape[0]
    near_count = near_tiles.shape[0]
    targets = surf_count * BLK
    capacity = max(2, 2 * NP_DEV // surf_count)
    pieces = -(-capacity // LANES)
    lists = (far_source.reshape(1, tiles), far_owner.reshape(1, tiles), far_block.reshape(1, tiles))
    cube = ((BLK, TILE, TILE), BF16)

    note = ((3 * INC + TILE, TILE), BF16)
    inner, outer = swap_inner(currents, surf_count), swap_outer(currents, surf_count)
    (partial,) = call(
        far_up_body,
        [((targets, INC * RANK), BF16)],
        (currents, primal_compress, primal_coupling) + lists,
        scratch=far_scratch(tiles),
        held=(2, 0, 1, 3, 4, 5),
        flops=10**11,
        name="far_up",
    )
    arrived = exchange(partial, surf_count)
    near_part, lower, upper, expanded = call(
        prepare_body,
        [((INC, NP_DEV), F32), cube, cube, ((BLK, RANK, TILE), BF16)],
        (
            near_target, near_source, currents, inner, outer, gram_inverse, gram_lower, gram_upper,
            primal_expand, near_tiles,
        ),
        scratch=[
            pltpu.VMEM((BLK + 2, INC, TILE), BF16),
            pltpu.VMEM((BLK, INC, TILE), F32),
            pltpu.VMEM((near_count, INC, TILE), F32),
            pltpu.VMEM((2,) + currents.shape, BF16),
            pltpu.VMEM(near_tiles.shape, BF16),
            pltpu.SemaphoreType.DMA((near_count // NEAR_CHUNK,)),
        ],
        held=(5, 6, 7, 8, 2, 0, 1),
        far=(9,),
        small=(0, 1),
        flops=10**11,
        name="prepare",
    )
    start, after, inner_note, outer_note = call(
        solve_body,
        [((INC, NP_DEV), F32)] * 2 + [note] * 2,
        (arrived, near_part, expanded, lower, upper),
        scratch=[
            pltpu.VMEM((2,) + note[0], BF16),
            pltpu.VMEM((BLK * INC, INC * RANK), BF16),
        ],
        name="solve",
    )
    outer_note = swap_outer(outer_note, surf_count)
    high, hot, bounds, index_rows, weight = call(
        order_body,
        [
            ((BLK, TILE), I32), ((NP_DEV, TILE), BF16), ((surf_count, 2), I32),
            ((IDX_ROWS, NP_DEV), BF16), ((1, NP_DEV), F32),
        ],
        (
            dual_owner.reshape(1, NP_DEV), dual_index.reshape(1, NP_DEV),
            refine_weight.reshape(1, NP_DEV), start,
        ),
        scratch=[pltpu.VMEM((BLK, TILE), F32)],
        held=(0, 1, 2),
        flops=10**9,
        name="order",
    )
    (tails,) = call(
        tails_body,
        [((surf_count, TAIL, LANES), F32)],
        (index_rows, high, hot, bounds),
        scratch=[
            pltpu.VMEM((BLK * IDX_ROWS, NP_DEV), BF16),
            pltpu.VMEM((IDX_ROWS, NP_DEV + (pieces + 1) * LANES), F32),
        ],
        smem=(3,),
        flops=10**9,
        name="tails",
    )
    second, third, inner_note = call(
        middle_body,
        [((INC, NP_DEV), F32)] * 2 + [note],
        (start, after, lower, upper, inner_note),
        flops=10**9,
        name="middle",
    )
    inner_note = swap_inner(inner_note, surf_count)
    (send,) = call(
        finish_body,
        [((surf_count, INC * pieces + TAIL, LANES), BF16)],
        (
            start, after, second, third, inner_note, outer_note, lower, upper,
            weight, tails, high, hot, bounds,
        ),
        scratch=[
            pltpu.VMEM((2,) + note[0], BF16),
            pltpu.VMEM((BLK * INC, NP_DEV), BF16),
            pltpu.VMEM((INC, NP_DEV + (pieces + 1) * LANES), F32),
            pltpu.VMEM((surf_count, INC * pieces + TAIL, LANES), BF16),
            pltpu.SemaphoreType.DMA((surf_count,)),
        ],
        streamed=(0,),
        held=(12,),
        loose=(12,),
        small=(12,),
        name="finish",
    )
    shares = lax.all_to_all(send, "surf", split_axis=0, concat_axis=0, tiled=True)
    slots = surf_count * pieces * LANES
    couple, compress = call(
        couple_body,
        [((BLK * RANK, targets * RANK), BF16), (dual_compress.shape, BF16)],
        (dual_coupling,) + lists + (dual_compress,),
        scratch=[pltpu.VMEM((targets, RANK, BLK * RANK), F32), pltpu.VMEM((tiles, INC * RANK), F32)],
        held=(0, 1, 2, 3, 4),
        small=(1, 2, 3),
        flops=10**10,
        name="couple",
    )
    half = (surf_count // 2, INC, BLK * RANK)
    field, coef, give = call(
        gather_body,
        [((BLK, INC, TILE), BF16), ((INC, BLK * RANK), BF16), (half, BF16)],
        (shares, compress, couple),
        scratch=[
            pltpu.VMEM((surf_count * pieces, LANES), F32),
            pltpu.VMEM((BLK * INC, slots), BF16),
            pltpu.VMEM((slots, TILE), BF16),
        ],
        name="gather",
    )
    got = lax.ppermute(give, "surf", [(i, i ^ 1) for i in range(surf_count)])
    (own,) = call(own_body, [(half, F32)], (coef, couple), flops=10**9, name="own")
    (merged,) = call(merge_body, [(half, BF16)], (own, got), name="merge")
    arrived = lax.all_to_all(
        merged,
        "surf",
        split_axis=0,
        concat_axis=0,
        tiled=True,
        axis_index_groups=[list(range(core, surf_count, 2)) for core in range(2)],
    )
    near_dual, expand = call(
        self_body,
        [((INC, NP_DEV), F32), (dual_expand.shape, BF16)],
        (field, dual_self, dual_expand),
        held=(2, 1),
        name="self_part",
    )
    (response,) = call(
        answer_body,
        [((INC, NP_DEV), BF16)],
        (arrived, near_dual, expand),
        scratch=[pltpu.VMEM((BLK * INC, BLK * RANK), BF16)],
        name="answer",
    )
    return response


def solution(mesh):
    both = ("groups", "surf")
    row, flat = P(None, both), P(both)
    cube, flat2 = P(both, None, None), P(both, None)
    return jax.shard_map(
        shards,
        mesh=mesh,
        in_specs=(
            row, cube, flat, flat, cube, cube, flat2, flat, flat2, flat, cube, cube, cube, flat,
            flat2, flat, cube, cube, cube, flat2,
        ),
        out_specs=row,
        check_vma=False,
    )
```

```python
import jax
import jax.numpy as jnp
from jax import lax
from jax.experimental import pallas as pl
from jax.experimental.pallas import tpu as pltpu
from jax.sharding import PartitionSpec as P

TILE = 256
INC = 32
RANK = 32
BLK = 8
NP_DEV = 2048
LANES = 128
IDX_ROWS = 16
TAIL = 8
NEAR_CHUNK = 8
F32 = jnp.float32
BF16 = jnp.bfloat16
I32 = jnp.int32
NT = (((1,), (1,)), ((), ()))
VMEM_LIMIT = 36 * 1024 * 1024


def dot(a, b):
    return jnp.dot(a, b, preferred_element_type=F32)


def dot_nt(a, b):
    return lax.dot_general(a, b, NT, preferred_element_type=F32)


def iota(shape, dim):
    return lax.broadcasted_iota(I32, shape, dim)


def block(array, i):
    return array[:, i * TILE : (i + 1) * TILE]


def as_hot(mask):
    return mask.astype(F32).astype(BF16)


def call(body, outs, args, scratch=(), smem=(), held=(), far=(), loose=(), small=(), streamed=(), flops=0, name=None):
    spaces = [
        pltpu.SMEM
        if k in smem
        else pl.ANY
        if k in loose
        else pltpu.HBM
        if k in held or k in far
        else pltpu.VMEM
        for k in range(len(args))
    ]
    size = sum(a.size * a.dtype.itemsize for a in args)
    outs = tuple(
        jax.ShapeDtypeStruct(s, d) for s, d in outs
    )
    buffers = [
        (pltpu.SMEM if k in small else pltpu.VMEM)(args[k].shape, args[k].dtype) for k in held
    ]
    waits = [pltpu.SemaphoreType.DMA(()) for _ in held]

    def wrapped(*refs):
        ins = list(refs[: len(args)])
        rest = refs[len(args) : len(refs) - 2 * len(held)]
        extra = refs[len(refs) - 2 * len(held) :]
        for n, k in enumerate(held):
            ins[k] = pltpu.make_async_copy(ins[k], extra[n], extra[len(held) + n])
            ins[k].start()
            ins[k] = (ins[k], extra[n])
        body(*ins, *rest)

    return pl.pallas_call(
        wrapped,
        out_shape=outs,
        in_specs=[pl.BlockSpec(memory_space=m) for m in spaces],
        out_specs=tuple(
            pl.BlockSpec(memory_space=pl.ANY if k in streamed else pltpu.VMEM)
            for k in range(len(outs))
        ),
        scratch_shapes=list(scratch) + buffers + waits,
        compiler_params=pltpu.CompilerParams(vmem_limit_bytes=VMEM_LIMIT),
        cost_estimate=pl.CostEstimate(flops=flops, bytes_accessed=size, transcendentals=0),
        name=name,
    )(*[pltpu.with_memory_space_constraint(a, m) if m is pltpu.HBM else a for a, m in zip(args, spaces)])


def ready(operand):
    operand[0].wait()
    return operand[1]


def fill_hot(hot, columns):
    height, count = columns.shape
    columns = columns.astype(BF16)
    lane = iota((height, TILE), 1).astype(F32).astype(BF16)
    one, zero = jnp.ones((height, TILE), BF16), jnp.zeros((height, TILE), BF16)
    for k in range(count):
        hot[k * height : (k + 1) * height, :] = jnp.where(lane == columns[:, k : k + 1], one, zero)


def coefficients(blocks, compress):
    width = BLK * RANK
    every = dot_nt(blocks, compress[...].reshape(width, TILE))
    owner = iota((INC, width), 1) // RANK
    coef = jnp.zeros((INC, width), F32)
    for s in range(BLK):
        coef = jnp.where(owner == s, every[s * INC : (s + 1) * INC], coef)
    return coef


def far_up_body(
    value, compress, coupling, source, owner, place,
    out_ref, blocks, turned, spread, pick, terms,
):
    value, compress = ready(value), ready(compress)
    for s in range(BLK):
        blocks[s * INC : (s + 1) * INC, :] = block(value, s)
    coef = coefficients(blocks[...], compress)
    width = BLK * RANK
    keep = (iota((RANK, width), 1) % RANK) == iota((RANK, width), 0)
    for i in range(INC):
        spread[i * RANK : (i + 1) * RANK, :] = jnp.where(keep, coef[i : i + 1, :], 0.0).astype(BF16)
    source = ready(source)
    tiles = source.shape[1]
    pick[...] = dot(spread[...], as_hot((iota((width, tiles), 0) // RANK) == source[...]))

    coupling = ready(coupling)
    turned[...] = coupling[...].astype(F32).T

    def step(pair, carry):
        rows = pl.multiple_of(pair * (2 * RANK), 2 * RANK)
        got = pick[pl.ds(rows, 2 * RANK), :]
        first = jnp.zeros((RANK, tiles), F32)
        second = jnp.zeros((RANK, tiles), F32)
        for r in range(RANK):
            factor = turned[r * RANK : (r + 1) * RANK, :]
            first += got[r : r + 1, :] * factor
            second += got[RANK + r : RANK + r + 1, :] * factor
        terms[pl.ds(rows, 2 * RANK), :] = jnp.concatenate([first, second], axis=0).astype(BF16)
        return carry

    lax.fori_loop(0, INC // 2, step, 0)
    targets = out_ref.shape[0]
    owner, place = ready(owner), ready(place)
    select = as_hot(iota((targets, tiles), 0) == owner[...] * BLK + place[...])
    out_ref[...] = dot_nt(select, terms[...]).astype(BF16)


def far_scratch(tiles):
    return [
        pltpu.VMEM((BLK * INC, TILE), BF16),
        pltpu.VMEM((RANK * RANK, tiles), F32),
        pltpu.VMEM((INC * RANK, BLK * RANK), BF16),
        pltpu.VMEM((INC * RANK, tiles), F32),
        pltpu.VMEM((INC * RANK, tiles), BF16),
    ]


def far_sums(arrived_ref, spread):
    rows = arrived_ref.shape[0]
    total = jnp.sum(arrived_ref[...].astype(F32).reshape(rows // BLK, BLK, INC * RANK), axis=0)
    width = INC * RANK
    keep = (iota((INC, width), 1) // RANK) == iota((INC, width), 0)
    for b in range(BLK):
        spread[b * INC : (b + 1) * INC, :] = jnp.where(keep, total[b : b + 1, :], 0.0).astype(BF16)
    fold = as_hot((iota((width, RANK), 0) % RANK) == iota((width, RANK), 1))
    return dot(spread[...], fold).astype(BF16)


def order_body(owner, index, weight, _, high_out, hot_out, bounds_out, rows_out, weight_out, ranks):
    owner, index = ready(owner), ready(index)
    owners = bounds_out.shape[0]
    pieces = -(-max(2, 2 * NP_DEV // owners) // LANES)
    before = as_hot(iota((TILE, TILE), 0) < iota((TILE, TILE), 1))
    number = iota((owners, TILE), 0)
    count = jnp.zeros((owners, 1), F32)
    begin = jnp.zeros((owners, 1), F32)
    hots, carries = [], []
    for c in range(BLK):
        names = block(owner, c)
        hot = (number == names).astype(F32)
        hots.append(hot)
        carries.append(count)
        count = count + jnp.sum(hot, axis=1, keepdims=True)
        begin = begin + jnp.sum((names < number).astype(F32), axis=1, keepdims=True)
    for c in range(BLK):
        rank = dot(hots[c].astype(BF16), before)
        ranks[c : c + 1, :] = jnp.sum(hots[c] * (rank + carries[c] + begin), axis=0, keepdims=True)
    spots = ranks[...].astype(I32)
    high_out[...] = spots // TILE
    fill_hot(hot_out, (spots % TILE).astype(F32).T)
    pair = iota((owners, 2), 1)
    bounds_out[...] = jnp.where(pair == 0, begin, count).astype(I32)
    row = iota((IDX_ROWS, NP_DEV), 0)
    index = index[...]
    digits = jnp.where(row % 2 == 0, index // TILE, index % TILE)
    rows_out[...] = jnp.where(row < 2 * pieces, digits, 0).astype(F32).astype(BF16)
    weight_out[...] = ready(weight)[...]


def prepare_body(
    target, origin, own, inner_ref, outer_ref, inverse, lower, upper, expand, tiles_ref,
    near_out, lower_out, upper_out, expand_out, cells, total, products, pair, tiles, arrivals,
):
    count = tiles_ref.shape[0]
    copies = []
    for c in range(count // NEAR_CHUNK):
        part = pl.ds(c * NEAR_CHUNK, NEAR_CHUNK)
        copy = pltpu.make_async_copy(tiles_ref.at[part], tiles.at[part], arrivals.at[c])
        copy.start()
        copies.append(copy)
    position = lax.axis_index("surf")
    odd = position % 2
    pair[0] = inner_ref[...]
    pair[1] = outer_ref[...]
    cells[0] = pair[1 - odd, :, NP_DEV - TILE :]
    cells[BLK + 1] = pair[odd, :, :TILE]
    inverse, lower, upper, expand = ready(inverse), ready(lower), ready(upper), ready(expand)
    for b in range(BLK):
        lower_out[b] = dot(lower[b], inverse[b]).astype(BF16)
        upper_out[b] = dot(upper[b], inverse[b]).astype(BF16)
        expand_out[b] = dot(expand[b], inverse[b]).astype(BF16)
    own, target, origin = ready(own), ready(target), ready(origin)
    for b in range(BLK):
        cells[b + 1] = block(own, b)
    total[...] = jnp.zeros_like(total)
    start = position * BLK - 1
    for c, copy in enumerate(copies):
        copy.wait()
        for k in range(c * NEAR_CHUNK, (c + 1) * NEAR_CHUNK):
            products[k] = dot(cells[origin[k] - start], tiles[k])
    for k in range(count):
        total[target[k]] += products[k]
    for b in range(BLK):
        near_out[:, b * TILE : (b + 1) * TILE] = dot(total[b].astype(BF16), inverse[b])


def solve_body(
    arrived_ref, near_ref, expand_ref, lower_ref, upper_ref,
    start_out, next_out, inner_out, outer_out, notes, spread,
):
    sums = far_sums(arrived_ref, spread)
    start, low = [], []
    for b in range(BLK):
        value = block(near_ref, b) + dot(sums[b * INC : (b + 1) * INC, :], expand_ref[b])
        start.append(value)
        low.append(value.astype(BF16))
        start_out[:, b * TILE : (b + 1) * TILE] = value
    after = []
    for b in range(BLK):
        value = start[b]
        if b > 0:
            value = value - dot(low[b - 1], lower_ref[b])
        if b < BLK - 1:
            value = value - dot(low[b + 1], upper_ref[b])
        after.append(value)
        next_out[:, b * TILE : (b + 1) * TILE] = value
    last = BLK - 1
    odd = lax.axis_index("surf") % 2
    for n, (edge, inside, away, back) in enumerate(
        ((last, last - 1, lower_ref, upper_ref), (0, 1, upper_ref, lower_ref))
    ):
        feedless = start[edge] - dot(after[inside].astype(BF16), away[edge])
        notes[n, 0:INC, :] = low[edge]
        notes[n, INC : 2 * INC, :] = after[edge].astype(BF16)
        notes[n, 2 * INC : 3 * INC, :] = feedless.astype(BF16)
        notes[n, 3 * INC :, :] = back[edge]
    inner_out[...] = notes[odd]
    outer_out[...] = notes[1 - odd]


def middle_body(
    start_ref, next_ref, lower_ref, upper_ref, note_ref, second_out, third_out, note_out
):
    note_out[...] = note_ref[...]
    last = BLK - 1
    now = [block(next_ref, b).astype(BF16) for b in range(BLK)]
    second = []
    for b in range(BLK):
        value = block(start_ref, b)
        if b > 1:
            value = value - dot(now[b - 1], lower_ref[b])
        if b < last - 1:
            value = value - dot(now[b + 1], upper_ref[b])
        second.append(value.astype(BF16))
        second_out[:, b * TILE : (b + 1) * TILE] = value
    for b in range(BLK):
        value = block(start_ref, b)
        if 2 < b < last:
            value = value - dot(second[b - 1], lower_ref[b])
        if 0 < b < last - 2:
            value = value - dot(second[b + 1], upper_ref[b])
        third_out[:, b * TILE : (b + 1) * TILE] = value


def finish_body(
    start_ref, next_ref, second_ref, third_ref, inner_note, outer_note, lower_ref, upper_ref,
    weight, tails_ref, high_ref, hot_ref, bounds, send_ref,
    notes, spread, ordered, stage, sent,
):
    position = lax.axis_index("surf")
    odd = position % 2
    notes[0] = inner_note[...]
    notes[1] = outer_note[...]
    then = [block(third_ref, b) for b in range(BLK)]
    for left in (True, False):
        n = 1 - odd if left else odd
        exists = (position > 0) if left else (position < lax.axis_size("surf") - 1)
        exists = exists.astype(F32)
        edge, step = (0, 1) if left else (BLK - 1, -1)
        toward, away = (lower_ref, upper_ref) if left else (upper_ref, lower_ref)
        one, two = edge + step, edge + 2 * step
        first = block(start_ref, edge).astype(BF16)
        beyond = notes[n, 3 * INC :, :]
        beside = notes[n, INC : 2 * INC, :].astype(F32) - dot(first, beyond)
        beside = (beside * exists).astype(BF16)
        now = block(next_ref, edge) - dot(notes[n, 0:INC, :], toward[edge]) * exists
        now = now.astype(BF16)
        beside_next = notes[n, 2 * INC : 3 * INC, :].astype(F32) - dot(now, beyond)
        beside_next = (beside_next * exists).astype(BF16)
        second = (block(second_ref, edge) - dot(beside, toward[edge])).astype(BF16)
        second_one = (block(second_ref, one) - dot(now, toward[one])).astype(BF16)
        then[edge] = then[edge] - dot(beside_next, toward[edge]) - dot(second_one, away[edge])
        then[one] = then[one] - dot(second, toward[one])
        then[two] = then[two] - dot(second_one, toward[two])
    for b in range(BLK):
        solved = then[b].astype(BF16).astype(F32)
        shares = (solved * block(weight, b)).astype(BF16)
        by_high_digit(spread, shares, high_ref, b)
    put_in_order(ordered, spread, hot_ref)
    owners = send_ref.shape[0]
    pieces = (send_ref.shape[1] - TAIL) // INC
    bounds_ref = ready(bounds)
    for o in range(owners):
        piece = owner_window(ordered, bounds_ref[o, 0], pieces)
        parts = [piece[:, j * LANES : (j + 1) * LANES] for j in range(pieces)]
        stage[o] = jnp.concatenate(parts + [tails_ref[o]], axis=0).astype(BF16)
        pltpu.make_async_copy(stage.at[o], send_ref.at[o], sent.at[o]).start()
    for o in range(owners):
        pltpu.make_async_copy(stage.at[o], send_ref.at[o], sent.at[o]).wait()


def by_high_digit(spread, values, high_ref, b):
    rows = values.shape[0]
    high = high_ref[b : b + 1, :].astype(F32).astype(BF16)
    for h in range(BLK):
        spread[h * rows : (h + 1) * rows, b * TILE : (b + 1) * TILE] = jnp.where(
            high == h, values, jnp.zeros_like(values)
        )


def put_in_order(ordered, spread, hot_ref):
    rows = ordered.shape[0]
    sorted_rows = dot(spread[...], hot_ref[...])
    for h in range(BLK):
        ordered[:, h * TILE : (h + 1) * TILE] = sorted_rows[h * rows : (h + 1) * rows]
    ordered[:, NP_DEV:] = jnp.zeros((rows, ordered.shape[1] - NP_DEV), F32)


def owner_window(ordered, begin, pieces):
    wide = (pieces + 1) * LANES
    base = pl.multiple_of((begin // LANES) * LANES, LANES)
    return pltpu.roll(ordered[:, pl.ds(base, wide)], wide - (begin - base), 1)


def tails_body(index_rows, high_ref, hot_ref, bounds_ref, out_ref, spread, ordered):
    for b in range(BLK):
        by_high_digit(spread, block(index_rows, b), high_ref, b)
    put_in_order(ordered, spread, hot_ref)
    pieces = ordered.shape[1] // LANES - NP_DEV // LANES - 1
    row = iota((TAIL, LANES), 0)
    slot = iota((TAIL, LANES), 1) + (row // 2) * LANES
    for o in range(out_ref.shape[0]):
        piece = owner_window(ordered, bounds_ref[o, 0], pieces)
        tail = piece[:TAIL, :LANES]
        for j in range(1, pieces):
            tail = jnp.where(row // 2 == j, piece[:TAIL, j * LANES : (j + 1) * LANES], tail)
        out_ref[o] = jnp.where(slot >= bounds_ref[o, 1], -16.0, tail)


def gather_body(
    arrived_ref, compress, couple_ref, field_out, coef_out, give_out, index, spread, hot,
):
    owners, rows, _ = arrived_ref.shape
    pieces = (rows - TAIL) // INC
    for e in range(owners):
        tail = arrived_ref[e].astype(F32)[INC * pieces :]
        marks = tail.astype(BF16)
        for j in range(pieces):
            k = e * pieces + j
            part = arrived_ref[e, j * INC : (j + 1) * INC, :]
            high = marks[2 * j : 2 * j + 1]
            index[k : k + 1, :] = tail[2 * j + 1 : 2 * j + 2]
            for h in range(BLK):
                spread[h * INC : (h + 1) * INC, k * LANES : (k + 1) * LANES] = jnp.where(
                    high == h, part, jnp.zeros_like(part)
                )
    fill_hot(hot, index[...].T)
    field = dot(spread[...], hot[...]).astype(BF16)
    for b in range(BLK):
        field_out[b] = field[b * INC : (b + 1) * INC]
    coef = coefficients(field, compress).astype(BF16)
    coef_out[...] = coef
    other = 1 - lax.axis_index("surf") % 2
    for c in range(give_out.shape[0]):
        give_out[c] = dot(coef, owner_columns(couple_ref, c, other)).astype(BF16)


def owner_columns(couple_ref, chip, core):
    return couple_ref[:, pl.ds(pl.multiple_of((2 * chip + core) * TILE, TILE), TILE)]


def own_body(coef_ref, couple_ref, out_ref):
    core = lax.axis_index("surf") % 2
    for c in range(out_ref.shape[0]):
        out_ref[c] = dot(coef_ref[...], owner_columns(couple_ref, c, core))


def merge_body(own_ref, got_ref, out_ref):
    out_ref[...] = (own_ref[...] + got_ref[...].astype(F32)).astype(BF16)


def couple_body(coupling, source, owner, place, basis, out_ref, basis_out, total, lanes):
    tiles, width = lanes.shape[0], BLK * RANK
    flat = RANK * RANK
    total[...] = jnp.zeros_like(total)
    coupling = ready(coupling)
    lanes[...] = coupling[...].astype(F32)
    keep = (iota((RANK, flat), 1) % RANK) == iota((RANK, flat), 0)
    fold = as_hot((iota((flat, width), 0) // RANK) == (iota((flat, width), 1) % RANK))
    number = iota((RANK, width), 1) // RANK
    source, owner, place = ready(source), ready(owner), ready(place)
    group = 8

    def step(c, carry):
        begin = pl.multiple_of(c * group, group)
        rows = lanes[pl.ds(begin, group), :]
        tall = [jnp.where(keep, rows[k : k + 1], 0.0).astype(BF16) for k in range(group)]
        turned = dot(jnp.concatenate(tall, axis=0), fold)
        for k in range(group):
            f = begin + k
            tile = jnp.where(number == source[0, f], turned[k * RANK : (k + 1) * RANK], 0.0)
            total[owner[0, f] * BLK + place[0, f]] += tile
        return carry

    lax.fori_loop(0, tiles // group, step, 0)
    for o in range(out_ref.shape[1] // TILE):
        part = total[o * BLK : (o + 1) * BLK].reshape(TILE, width)
        out_ref[:, o * TILE : (o + 1) * TILE] = part.T.astype(BF16)
    basis_out[...] = ready(basis)[...]


def self_body(field_ref, tiles, basis, out_ref, basis_out):
    basis_out[...] = ready(basis)[...]
    tiles = ready(tiles)
    for b in range(BLK):
        out_ref[:, b * TILE : (b + 1) * TILE] = dot(field_ref[b], tiles[b])


def answer_body(arrived_ref, near_ref, expand, out_ref, spread):
    total = jnp.sum(arrived_ref[...].astype(F32), axis=0)
    number = iota(total.shape, 1) // RANK
    for b in range(BLK):
        spread[b * INC : (b + 1) * INC, :] = jnp.where(number == b, total, 0.0).astype(BF16)
    far = dot(spread[...], expand[...].reshape(BLK * RANK, TILE))
    for b in range(BLK):
        out_ref[:, b * TILE : (b + 1) * TILE] = (
            block(near_ref, b) + far[b * INC : (b + 1) * INC]
        ).astype(BF16)


def swap_inner(array, surf_count):
    return lax.ppermute(array, "surf", [(i, i ^ 1) for i in range(surf_count)])


def swap_outer(array, surf_count):
    pairs = [(0, 0), (surf_count - 1, surf_count - 1)]
    for i in range(1, surf_count - 1, 2):
        pairs += [(i, i + 1), (i + 1, i)]
    return lax.ppermute(array, "surf", pairs)


def exchange(array, surf_count):
    shape = array.shape
    array = array.reshape((surf_count, shape[0] // surf_count) + shape[1:])
    array = lax.all_to_all(array, "surf", split_axis=0, concat_axis=0, tiled=True)
    return array.reshape(shape)


def shards(
    currents, near_tiles, near_target, near_source, primal_compress, primal_expand, primal_coupling,
    far_source, far_owner, far_block, gram_inverse, gram_lower, gram_upper, refine_weight,
    dual_owner, dual_index, dual_self, dual_compress, dual_expand, dual_coupling,
):
    surf_count = lax.axis_size("surf")
    tiles = far_source.shape[0]
    near_count = near_tiles.shape[0]
    targets = surf_count * BLK
    capacity = max(2, 2 * NP_DEV // surf_count)
    pieces = -(-capacity // LANES)
    lists = (far_source.reshape(1, tiles), far_owner.reshape(1, tiles), far_block.reshape(1, tiles))
    cube = ((BLK, TILE, TILE), BF16)

    note = ((3 * INC + TILE, TILE), BF16)
    inner, outer = swap_inner(currents, surf_count), swap_outer(currents, surf_count)
    (partial,) = call(
        far_up_body,
        [((targets, INC * RANK), BF16)],
        (currents, primal_compress, primal_coupling) + lists,
        scratch=far_scratch(tiles),
        held=(0, 1, 3, 2, 4, 5),
        flops=10**11,
        name="far_up",
    )
    arrived = exchange(partial, surf_count)
    near_part, lower, upper, expanded = call(
        prepare_body,
        [((INC, NP_DEV), F32), cube, cube, ((BLK, RANK, TILE), BF16)],
        (
            near_target, near_source, currents, inner, outer, gram_inverse, gram_lower, gram_upper,
            primal_expand, near_tiles,
        ),
        scratch=[
            pltpu.VMEM((BLK + 2, INC, TILE), BF16),
            pltpu.VMEM((BLK, INC, TILE), F32),
            pltpu.VMEM((near_count, INC, TILE), F32),
            pltpu.VMEM((2,) + currents.shape, BF16),
            pltpu.VMEM(near_tiles.shape, BF16),
            pltpu.SemaphoreType.DMA((near_count // NEAR_CHUNK,)),
        ],
        held=(5, 6, 7, 8, 2, 0, 1),
        far=(9,),
        small=(0, 1),
        flops=10**11,
        name="prepare",
    )
    start, after, inner_note, outer_note = call(
        solve_body,
        [((INC, NP_DEV), F32)] * 2 + [note] * 2,
        (arrived, near_part, expanded, lower, upper),
        scratch=[
            pltpu.VMEM((2,) + note[0], BF16),
            pltpu.VMEM((BLK * INC, INC * RANK), BF16),
        ],
        name="solve",
    )
    outer_note = swap_outer(outer_note, surf_count)
    high, hot, bounds, index_rows, weight = call(
        order_body,
        [
            ((BLK, TILE), I32), ((NP_DEV, TILE), BF16), ((surf_count, 2), I32),
            ((IDX_ROWS, NP_DEV), BF16), ((1, NP_DEV), F32),
        ],
        (
            dual_owner.reshape(1, NP_DEV), dual_index.reshape(1, NP_DEV),
            refine_weight.reshape(1, NP_DEV), start,
        ),
        scratch=[pltpu.VMEM((BLK, TILE), F32)],
        held=(0, 1, 2),
        flops=10**9,
        name="order",
    )
    (tails,) = call(
        tails_body,
        [((surf_count, TAIL, LANES), F32)],
        (index_rows, high, hot, bounds),
        scratch=[
            pltpu.VMEM((BLK * IDX_ROWS, NP_DEV), BF16),
            pltpu.VMEM((IDX_ROWS, NP_DEV + (pieces + 1) * LANES), F32),
        ],
        smem=(3,),
        flops=10**9,
        name="tails",
    )
    second, third, inner_note = call(
        middle_body,
        [((INC, NP_DEV), F32)] * 2 + [note],
        (start, after, lower, upper, inner_note),
        flops=10**9,
        name="middle",
    )
    inner_note = swap_inner(inner_note, surf_count)
    (send,) = call(
        finish_body,
        [((surf_count, INC * pieces + TAIL, LANES), BF16)],
        (
            start, after, second, third, inner_note, outer_note, lower, upper,
            weight, tails, high, hot, bounds,
        ),
        scratch=[
            pltpu.VMEM((2,) + note[0], BF16),
            pltpu.VMEM((BLK * INC, NP_DEV), BF16),
            pltpu.VMEM((INC, NP_DEV + (pieces + 1) * LANES), F32),
            pltpu.VMEM((surf_count, INC * pieces + TAIL, LANES), BF16),
            pltpu.SemaphoreType.DMA((surf_count,)),
        ],
        streamed=(0,),
        held=(12,),
        loose=(12,),
        small=(12,),
        name="finish",
    )
    shares = lax.all_to_all(send, "surf", split_axis=0, concat_axis=0, tiled=True)
    slots = surf_count * pieces * LANES
    couple, compress = call(
        couple_body,
        [((BLK * RANK, targets * RANK), BF16), (dual_compress.shape, BF16)],
        (dual_coupling,) + lists + (dual_compress,),
        scratch=[pltpu.VMEM((targets, RANK, BLK * RANK), F32), pltpu.VMEM((tiles, INC * RANK), F32)],
        held=(0, 1, 2, 3, 4),
        small=(1, 2, 3),
        flops=10**10,
        name="couple",
    )
    half = (surf_count // 2, INC, BLK * RANK)
    field, coef, give = call(
        gather_body,
        [((BLK, INC, TILE), BF16), ((INC, BLK * RANK), BF16), (half, BF16)],
        (shares, compress, couple),
        scratch=[
            pltpu.VMEM((surf_count * pieces, LANES), F32),
            pltpu.VMEM((BLK * INC, slots), BF16),
            pltpu.VMEM((slots, TILE), BF16),
        ],
        name="gather",
    )
    got = lax.ppermute(give, "surf", [(i, i ^ 1) for i in range(surf_count)])
    (own,) = call(own_body, [(half, F32)], (coef, couple), flops=10**9, name="own")
    (merged,) = call(merge_body, [(half, BF16)], (own, got), name="merge")
    arrived = lax.all_to_all(
        merged,
        "surf",
        split_axis=0,
        concat_axis=0,
        tiled=True,
        axis_index_groups=[list(range(core, surf_count, 2)) for core in range(2)],
    )
    near_dual, expand = call(
        self_body,
        [((INC, NP_DEV), F32), (dual_expand.shape, BF16)],
        (field, dual_self, dual_expand),
        held=(2, 1),
        name="self_part",
    )
    (response,) = call(
        answer_body,
        [((INC, NP_DEV), BF16)],
        (arrived, near_dual, expand),
        scratch=[pltpu.VMEM((BLK * INC, BLK * RANK), BF16)],
        name="answer",
    )
    return response


def solution(mesh):
    both = ("groups", "surf")
    row, flat = P(None, both), P(both)
    cube, flat2 = P(both, None, None), P(both, None)
    return jax.shard_map(
        shards,
        mesh=mesh,
        in_specs=(
            row, cube, flat, flat, cube, cube, flat2, flat, flat2, flat, cube, cube, cube, flat,
            flat2, flat, cube, cube, cube, flat2,
        ),
        out_specs=row,
        check_vma=False,
    )
```
